32 devices in a mesh: row: 16 (over z, x, core), col: 2 (over y).
Axes of the slice: x: 2, y: 2, z: 4, core: 2. Of those that a mesh axis runs over, the one named last changes fastest.
Arguments:
- right_sides: float32 [8192, 1024], P('row', 'col'), may hold values from -6 to 6
- pencil_s: float32 [8192, 512], P('row'), as said below
- pencil_t: float32 [8192, 512], P('row'), as said below
- value_alpha: float32 [4096], replicated, may hold values from -3 to -0.5
- value_beta: float32 [4096], replicated, may hold values from 0.5 to 1
- selected: int32 [1024], P('col'), may hold values from 0 to 4095
- block_slot: int32 [32], replicated, may hold values from 0 to 31, as said below
- right_basis: float32 [65536, 2, 256], P('row', None, 'col'), may hold values from -0.25 to 0.25
- vectors: float32 [65536, 1024], P('row', 'col'), may hold values from -6 to 6
Outputs:
- updated_sides: float32 [8192, 1024], P('row', 'col')
- updated_vectors: float32 [65536, 1024], P('row', 'col')
The draws below stay inside these ranges and needn't reach their ends.
Inputs may be any that keep to these rules, and one draw needn't show every extreme that they name: A permutation: logical block b of 256 rows is stored at slot block_slot[b]. `pencil_s`: in the window, entries left of the diagonal are 0 and diagonal entries lie in [1, 2]. `pencil_t`: in the window, entries left of the diagonal are 0 and diagonal entries lie in [1, 2].
All inputs are finite; a program needn't handle non-finite values.
Results may differ from the reference program's by a relative error of at most 0.0003.
Values sent between devices are 32-bit elements; how exact they have to be, the bound alone decides.
No kernel may reach another device: no remote copies, remote signals or barrier semaphores. Data moves between devices by JAX's collectives and lax.ppermute only.
A program may use at most 128 MiB of HBM per device.

```python
import jax
import jax.numpy as jnp
from jax import lax

NEIG = 1024
BLK = 256
ORDER = 65536
POOL = 4096
LEAD = 8192
NBLK = 32
WIN = 512


def slot_order(key):
    return jax.random.permutation(jax.random.fold_in(key, 11), NBLK).astype(jnp.int32)


def draw_block_slot(key, part):
    return slot_order(key)


def pencil_factor(key, salt):
    base_key = jax.random.fold_in(key, salt)
    rough_key, diag_key = jax.random.split(base_key)
    width = 2 * BLK
    lead_rows = NBLK * BLK
    rough = jax.random.normal(rough_key, (lead_rows, width), jnp.float32)
    diagonal = jax.random.uniform(diag_key, (lead_rows, width), jnp.float32, 1.0, 2.0)
    row_index = jax.lax.broadcasted_iota(jnp.int32, (lead_rows, width), 0)
    col_index = jax.lax.broadcasted_iota(jnp.int32, (lead_rows, width), 1)
    window_row = row_index - (lead_rows - width)
    inside = jnp.where(col_index > window_row, rough * (0.6 / width ** 0.5), jnp.where(col_index == window_row, diagonal, 0.0))
    logical = jnp.where(window_row >= 0, inside, rough * (1.0 / width ** 0.5))
    stored = jnp.zeros((NBLK, BLK, width), jnp.float32).at[slot_order(key)].set(logical.reshape(NBLK, BLK, width))
    return stored.reshape(lead_rows, width)


def draw_pencil_s(key, part):
    return pencil_factor(key, 21)


def draw_pencil_t(key, part):
    return pencil_factor(key, 22)


def set_ends(result, stream_key, smallest, top_value):
    dims = result.shape
    place = [jax.random.randint(jax.random.fold_in(stream_key, axis), (), 0, dims[axis]) for axis in range(len(dims))]
    result = result.at[tuple(place)].set(smallest)
    longest = dims.index(max(dims))
    place[longest] = (place[longest] + 1) % dims[longest]
    return result.at[tuple(place)].set(top_value)


def steps_of(own_key, dims, shards, low, top_value):
    level, own = 1.0, jax.random.fold_in(own_key, 6)
    for position, blocks in shards:
        heights = jnp.exp(jax.random.uniform(jax.random.fold_in(own, position), (blocks,), jnp.float32, low / len(shards), top_value / len(shards)))
        level = level * jnp.repeat(heights, dims[position] // blocks).reshape([-1 if axis == position else 1 for axis in range(len(dims))])
    return level


def gaussian(own_key, extent, scale, reach, cuts=(), kind=jnp.bfloat16):
    array = scale * jax.random.normal(own_key, extent, jnp.float32)
    if cuts:
        array = array * steps_of(own_key, extent, cuts, -0.22, 0.18)
    return jnp.clip(array, -reach, reach).astype(kind)


def setup_inputs(seed: int = 0) -> dict:
    seeds = jax.random.split(jax.random.key(seed), 10)
    return {
        "right_sides": gaussian(seeds[0], (LEAD, NEIG), 1.0, 6.0, ((0, 16), (1, 2)), jnp.float32),
        "pencil_s": draw_pencil_s(jax.random.fold_in(seeds[9], 71), 0),
        "pencil_t": draw_pencil_t(jax.random.fold_in(seeds[9], 71), 0),
        "value_alpha": jnp.clip(jax.random.uniform(seeds[3], (POOL,), jnp.float32, -3.0, -0.5), -3.0, -0.5),
        "value_beta": jnp.clip(jax.random.uniform(seeds[4], (POOL,), jnp.float32, 0.5, 1.0), 0.5, 1.0),
        "selected": set_ends(jax.random.randint(seeds[5], (NEIG,), 0, POOL), jax.random.fold_in(seeds[5], 1), 0, POOL - 1).astype(jnp.int32),
        "block_slot": draw_block_slot(jax.random.fold_in(seeds[9], 71), 0),
        "right_basis": gaussian(seeds[7], (ORDER, 2, BLK), WIN ** -0.5, 0.25, ((0, 16), (2, 2)), jnp.float32),
        "vectors": gaussian(seeds[8], (ORDER, NEIG), 1.0, 6.0, ((0, 16), (1, 2)), jnp.float32),
    }


def reference(right_sides, pencil_s, pencil_t, value_alpha, value_beta, selected, block_slot, right_basis, vectors):
    exact_mode = lax.Precision.HIGHEST
    shift_alpha = value_alpha[selected]
    shift_beta = value_beta[selected]
    block_count = block_slot.shape[0]
    width = 2 * BLK
    lead_rows = block_count * BLK
    logical_s = pencil_s.reshape(block_count, BLK, width)[block_slot].reshape(lead_rows, width)
    logical_t = pencil_t.reshape(block_count, BLK, width)[block_slot].reshape(lead_rows, width)
    logical_r = right_sides.reshape(block_count, BLK, NEIG)[block_slot].reshape(lead_rows, NEIG)
    window_s = logical_s[lead_rows - width:]
    window_t = logical_t[lead_rows - width:]
    window_r = logical_r[lead_rows - width:]
    index_rows = jnp.arange(width, dtype=jnp.int32)

    def back_step(pending, column):
        s_column = lax.dynamic_index_in_dim(window_s, column, 1, keepdims=False)
        t_column = lax.dynamic_index_in_dim(window_t, column, 1, keepdims=False)
        pivot_value = shift_beta * s_column[column] - shift_alpha * t_column[column]
        solved = pending[column] / pivot_value
        s_masked = jnp.where(index_rows < column, s_column, 0.0)
        t_masked = jnp.where(index_rows < column, t_column, 0.0)
        pending = pending - (s_masked[:, None] * (shift_beta * solved)[None, :] - t_masked[:, None] * (shift_alpha * solved)[None, :])
        return pending, solved

    steps_down = jnp.arange(width - 1, -1, -1, dtype=jnp.int32)
    _, solved_rows = lax.scan(back_step, window_r, steps_down)
    window_x = solved_rows[::-1]
    update = jnp.dot(logical_s, window_x * shift_beta[None, :], precision=exact_mode, preferred_element_type=jnp.float32)
    update = update - jnp.dot(logical_t, window_x * shift_alpha[None, :], precision=exact_mode, preferred_element_type=jnp.float32)
    new_sides = (logical_r - update).at[lead_rows - width:].set(window_x)
    stored = jnp.zeros((block_count, BLK, NEIG), new_sides.dtype).at[block_slot].set(new_sides.reshape(block_count, BLK, NEIG))
    updated_sides = stored.reshape(lead_rows, NEIG)
    basis = right_basis.reshape(ORDER, width)
    updated_vectors = vectors + jnp.dot(basis, window_x, precision=exact_mode, preferred_element_type=jnp.float32)
    return (updated_sides, updated_vectors)
```

```python
import functools

import jax
import jax.numpy as jnp
from jax import lax
from jax.experimental import pallas as pl
from jax.experimental.pallas import tpu as pltpu
from jax.sharding import PartitionSpec as P

SUB = 32
GROUP = 8
VMEM_BYTES = 48 * 1024 * 1024
CHUNKS = 8


def exact_dot(left, right):
    return jnp.dot(left, right, precision=lax.Precision.HIGHEST, preferred_element_type=jnp.float32)


def split_two(value):
    high = value.astype(jnp.bfloat16)
    low = (value - high.astype(jnp.float32)).astype(jnp.bfloat16)
    return high, low


def near_dot(left, right_high, right_low):
    high, low = split_two(left)
    dot = functools.partial(jnp.dot, preferred_element_type=jnp.float32)
    return dot(high, right_high) + (dot(low, right_high) + dot(high, right_low))


def table_lookup(selected, table):
    positions = lax.broadcasted_iota(jnp.int32, (table.shape[0], selected.shape[0]), 0)
    return jnp.sum(jnp.where(positions == selected[None, :], table[:, None], 0.0), axis=0)


def back_substitute(s_ref, t_ref, alpha, beta, pending_ref, x_ref):
    size = x_ref.shape[0]
    rows = lax.broadcasted_iota(jnp.int32, (SUB, SUB), 0)
    cols = lax.broadcasted_iota(jnp.int32, (SUB, SUB), 1)
    groups = SUB // GROUP
    for first in range(size - SUB, -1, -SUB):
        s_small = s_ref[first : first + SUB, first : first + SUB]
        t_small = t_ref[first : first + SUB, first : first + SUB]
        s_diag = jnp.sum(jnp.where(rows == cols, s_small, 0.0), axis=1, keepdims=True)
        t_diag = jnp.sum(jnp.where(rows == cols, t_small, 0.0), axis=1, keepdims=True)
        inverse = 1.0 / (beta * s_diag - alpha * t_diag)
        s_strict = jnp.where(rows < cols, s_small, 0.0)
        t_strict = jnp.where(rows < cols, t_small, 0.0)
        pending = [
            pending_ref[first + g * GROUP : first + (g + 1) * GROUP, :] for g in range(groups)
        ]
        for column in range(SUB - 1, -1, -1):
            own, row = divmod(column, GROUP)
            solved = pending[own][row : row + 1, :] * inverse[column : column + 1, :]
            x_ref[first + column : first + column + 1, :] = solved
            scaled_beta = beta * solved
            scaled_alpha = alpha * solved
            for g in range(own + 1):
                span = slice(g * GROUP, (g + 1) * GROUP)
                pending[g] = pending[g] - (
                    s_strict[span, column : column + 1] * scaled_beta
                    - t_strict[span, column : column + 1] * scaled_alpha
                )
        if first:
            block = x_ref[first : first + SUB, :]
            pending_ref[:first, :] = pending_ref[:first, :] - (
                exact_dot(s_ref[:first, first : first + SUB], beta * block)
                - exact_dot(t_ref[:first, first : first + SUB], alpha * block)
            )


def lower_kernel(place, s_ref, t_ref, r_ref, alpha_ref, beta_ref, x_ref, pending_ref):
    pending_ref[...] = r_ref[...]
    back_substitute(s_ref, t_ref, alpha_ref[...], beta_ref[...], pending_ref, x_ref)


def upper_kernel(place, s_ref, t_ref, r_ref, alpha_ref, beta_ref, lower_ref, x_ref, pending_ref):
    block = x_ref.shape[0]
    alpha, beta = alpha_ref[...], beta_ref[...]
    lower = lower_ref[...]
    pending_ref[...] = r_ref[...] - (
        exact_dot(s_ref[:, block:], beta * lower) - exact_dot(t_ref[:, block:], alpha * lower)
    )
    back_substitute(s_ref, t_ref, alpha, beta, pending_ref, x_ref)


def solve_lower(place, pencil_s, pencil_t, sides, alpha, beta):
    block, eigs = pencil_s.shape[1] // 2, sides.shape[1]
    corner = pl.BlockSpec((block, block), lambda i, place: (place[0], 1))
    whole = pl.BlockSpec((block, eigs), lambda i, place: (place[0], 0))
    line = pl.BlockSpec((1, eigs), lambda i, place: (0, 0))
    return pl.pallas_call(
        lower_kernel,
        out_shape=jax.ShapeDtypeStruct((block, eigs), jnp.float32),
        grid_spec=pltpu.PrefetchScalarGridSpec(
            num_scalar_prefetch=1,
            grid=(1,),
            in_specs=[corner, corner, whole, line, line],
            out_specs=pl.BlockSpec((block, eigs), lambda i, place: (0, 0)),
            scratch_shapes=[pltpu.VMEM((block, eigs), jnp.float32)],
        ),
        compiler_params=pltpu.CompilerParams(vmem_limit_bytes=VMEM_BYTES),
        cost_estimate=pl.CostEstimate(flops=10**10, bytes_accessed=4 * 10**6, transcendentals=0),
        name="solve_lower",
    )(place, pencil_s, pencil_t, sides, alpha, beta)


def solve_upper(place, pencil_s, pencil_t, sides, alpha, beta, lower):
    block, eigs = pencil_s.shape[1] // 2, sides.shape[1]
    band = pl.BlockSpec((block, 2 * block), lambda i, place: (place[0], 0))
    whole = pl.BlockSpec((block, eigs), lambda i, place: (place[0], 0))
    line = pl.BlockSpec((1, eigs), lambda i, place: (0, 0))
    fixed = pl.BlockSpec((block, eigs), lambda i, place: (0, 0))
    return pl.pallas_call(
        upper_kernel,
        out_shape=jax.ShapeDtypeStruct((block, eigs), jnp.float32),
        grid_spec=pltpu.PrefetchScalarGridSpec(
            num_scalar_prefetch=1,
            grid=(1,),
            in_specs=[band, band, whole, line, line, fixed],
            out_specs=fixed,
            scratch_shapes=[pltpu.VMEM((block, eigs), jnp.float32)],
        ),
        compiler_params=pltpu.CompilerParams(vmem_limit_bytes=VMEM_BYTES),
        cost_estimate=pl.CostEstimate(flops=10**10, bytes_accessed=4 * 10**6, transcendentals=0),
        name="solve_upper",
    )(place, pencil_s, pencil_t, sides, alpha, beta, lower)


def sides_kernel(
    place, r_ref, s_ref, t_ref, alpha_ref, beta_ref, upper_ref, lower_ref, out_ref, high_ref, low_ref
):
    block = upper_ref.shape[0]
    alpha, beta = alpha_ref[...], beta_ref[...]
    upper, lower = upper_ref[...], lower_ref[...]
    for slot in range(out_ref.shape[0] // block):
        span = slice(slot * block, (slot + 1) * block)
        update = exact_dot(s_ref[span, :block], beta * upper) - exact_dot(
            t_ref[span, :block], alpha * upper
        )
        update = update + (
            exact_dot(s_ref[span, block:], beta * lower)
            - exact_dot(t_ref[span, block:], alpha * lower)
        )
        fresh = r_ref[span, :] - update
        fresh = jnp.where(place[0] == slot, upper, fresh)
        out_ref[span, :] = jnp.where(place[1] == slot, lower, fresh)
    parts = place.shape[0] - 2
    width = block // parts
    for part in range(parts):
        rows = pl.ds(pl.multiple_of(place[2 + part] * width, width), width)
        for half, source in enumerate((upper_ref, lower_ref)):
            target = (2 * part + half) * width
            high, low = split_two(source[rows, :])
            high_ref[target : target + width, :] = high
            low_ref[target : target + width, :] = low


def update_sides(place, sides, pencil_s, pencil_t, alpha, beta, upper, lower):
    block, eigs = upper.shape
    vmem = pl.BlockSpec(memory_space=pltpu.VMEM)
    return pl.pallas_call(
        sides_kernel,
        out_shape=(
            jax.ShapeDtypeStruct(sides.shape, jnp.float32),
            jax.ShapeDtypeStruct((2 * block, eigs), jnp.bfloat16),
            jax.ShapeDtypeStruct((2 * block, eigs), jnp.bfloat16),
        ),
        in_specs=[pl.BlockSpec(memory_space=pltpu.SMEM)] + [vmem] * 7,
        out_specs=(vmem, vmem, vmem),
        compiler_params=pltpu.CompilerParams(vmem_limit_bytes=VMEM_BYTES),
        cost_estimate=pl.CostEstimate(
            flops=24 * sides.shape[0] * block * eigs, bytes_accessed=6 * 10**6, transcendentals=0
        ),
        name="update_sides",
    )(place, sides, pencil_s, pencil_t, alpha, beta, upper, lower)


def vectors_kernel(parts, paired, refs):
    vectors_ref, high_ref, low_ref = refs[:3]
    part_refs = refs[3 : 3 + parts]
    out_ref = refs[-1]
    tile = out_ref.shape[0]
    pieces = []
    for ref in part_refs:
        if paired:
            pieces.append(ref[pl.ds(0, tile, 2), :])
            pieces.append(ref[pl.ds(1, tile, 2), :])
        else:
            pieces.append(ref[...])
    basis = jnp.concatenate(pieces, axis=1)
    out_ref[...] = vectors_ref[...] + near_dot(basis, high_ref[...], low_ref[...])


def add_chunk(index, count, vectors, high, low, own, received, paired, previous):
    rows, eigs = vectors.shape
    span = rows // count
    tile = min(256, span)
    steps = span // tile
    base = index * steps
    per = 2 if paired else 1
    width = own.shape[1]
    fixed = pl.BlockSpec(high.shape, lambda i: (0, 0))
    at_rows = pl.BlockSpec((tile, eigs), lambda i: (base + i, 0))
    in_specs = [
        at_rows,
        fixed,
        fixed,
        pl.BlockSpec((per * tile, width), lambda i: (base + i, 0)),
    ]
    in_specs += [pl.BlockSpec((per * tile, width), lambda i: (i, 0)) for _ in received]
    operands = [vectors, high, low, own, *received]
    aliases = {}
    if previous is not None:
        aliases = {len(operands): 0}
        operands.append(previous)
        in_specs.append(pl.BlockSpec(memory_space=pl.ANY))

    def body(*refs):
        vectors_kernel(1 + len(received), paired, refs)

    return pl.pallas_call(
        body,
        out_shape=jax.ShapeDtypeStruct((rows, eigs), jnp.float32),
        grid=(steps,),
        in_specs=in_specs,
        out_specs=at_rows,
        input_output_aliases=aliases,
        compiler_params=pltpu.CompilerParams(vmem_limit_bytes=VMEM_BYTES),
        cost_estimate=pl.CostEstimate(
            flops=6 * span * high.shape[0] * eigs,
            bytes_accessed=12 * span * eigs,
            transcendentals=0,
        ),
        name="add_chunk",
    )(*operands)


def spread(block, owner, axis, size):
    me = lax.axis_index(axis)
    if size & (size - 1) or size < 2:
        return lax.psum(jnp.where(me == owner, block, jnp.zeros_like(block)), axis)

    def exchange(value, bit):
        return lax.ppermute(value, axis, [(i, i ^ bit) for i in range(size)])

    half = block.shape[0] // 2
    core = me % 2
    kept = lax.dynamic_slice_in_dim(block, core * half, half, 0)
    given = lax.dynamic_slice_in_dim(block, (1 - core) * half, half, 0)
    kept = jnp.where(me == owner, kept, exchange(given, 1))
    bit = 2
    while bit < size:
        kept = jnp.where(me // bit == owner // bit, kept, exchange(kept, bit))
        bit *= 2
    other = exchange(kept, 1)
    first = jnp.where(core == 0, kept, other)
    second = jnp.where(core == 0, other, kept)
    return jnp.concatenate([first, second], 0)


def on_device(
    row_size,
    col_size,
    right_sides,
    pencil_s,
    pencil_t,
    value_alpha,
    value_beta,
    selected,
    block_slot,
    right_basis,
    vectors,
):
    block = pencil_s.shape[1] // 2
    slot_count = right_sides.shape[0] // block
    block_count = block_slot.shape[0]
    rows, _, width = right_basis.shape
    me_row = lax.axis_index("row")
    me_col = lax.axis_index("col")

    paired = width % 128 == 0
    own = right_basis.reshape((2 * rows, width) if paired else (rows, 2 * width))
    chunk_rows = own.shape[0] // CHUNKS
    received = []
    for index in range(CHUNKS):
        piece = own[index * chunk_rows : (index + 1) * chunk_rows]
        received.append(
            [
                lax.ppermute(piece, "col", [(i, (i + step) % col_size) for i in range(col_size)])
                for step in range(1, col_size)
            ]
        )

    alpha = table_lookup(selected, value_alpha)[None, :]
    beta = table_lookup(selected, value_beta)[None, :]
    slot_upper = block_slot[block_count - 2]
    slot_lower = block_slot[block_count - 1]

    lower = solve_lower(
        (slot_lower % slot_count)[None], pencil_s, pencil_t, right_sides, alpha, beta
    )
    lower = spread(lower, slot_lower // slot_count, "row", row_size)
    upper = solve_upper(
        (slot_upper % slot_count)[None], pencil_s, pencil_t, right_sides, alpha, beta, lower
    )
    upper = spread(upper, slot_upper // slot_count, "row", row_size)

    place = jnp.stack(
        [slot_upper - me_row * slot_count, slot_lower - me_row * slot_count]
        + [(me_col - step) % col_size for step in range(col_size)]
    ).astype(jnp.int32)
    updated_sides, high, low = update_sides(
        place, right_sides, pencil_s, pencil_t, alpha, beta, upper, lower
    )
    updated_vectors = None
    for index in range(CHUNKS):
        updated_vectors = add_chunk(
            index, CHUNKS, vectors, high, low, own, received[index], paired, updated_vectors
        )
    return (updated_sides, updated_vectors)


def solution(mesh):
    body = functools.partial(on_device, mesh.shape["row"], mesh.shape["col"])
    return jax.shard_map(
        body,
        mesh=mesh,
        in_specs=(
            P("row", "col"),
            P("row", None),
            P("row", None),
            P(),
            P(),
            P("col"),
            P(),
            P("row", None, "col"),
            P("row", "col"),
        ),
        out_specs=(P("row", "col"), P("row", "col")),
        check_vma=False,
    )
```

```python
import functools

import jax
import jax.numpy as jnp
from jax import lax
from jax.experimental import pallas as pl
from jax.experimental.pallas import tpu as pltpu
from jax.sharding import PartitionSpec as P

SUB = 32
GROUP = 8
VMEM_BYTES = 48 * 1024 * 1024
SHARES = (12, 2, 1, 1)
TILE = 512
PIECES = 2


def exact_dot(left, right):
    return jnp.dot(left, right, precision=lax.Precision.HIGHEST, preferred_element_type=jnp.float32)


def split_two(value):
    high = value.astype(jnp.bfloat16)
    low = (value - high.astype(jnp.float32)).astype(jnp.bfloat16)
    return high, low


def near_dot(left, right_high, right_low):
    high, low = split_two(left)
    dot = functools.partial(jnp.dot, preferred_element_type=jnp.float32)
    return dot(high, right_high) + (dot(low, right_high) + dot(high, right_low))


def table_lookup(selected, table):
    table_rows, lanes = table.shape
    lane = lax.broadcasted_iota(jnp.int32, (lanes, selected.shape[1]), 0)
    in_lane = jnp.where(lane == selected % lanes, 1.0, 0.0)
    candidates = exact_dot(table, in_lane)
    row = lax.broadcasted_iota(jnp.int32, candidates.shape, 0)
    return jnp.sum(jnp.where(row == selected // lanes, candidates, 0.0), axis=0, keepdims=True)


def back_substitute(s_ref, t_ref, alpha, beta, pending_ref, x_ref):
    size = x_ref.shape[0]
    rows = lax.broadcasted_iota(jnp.int32, (SUB, SUB), 0)
    cols = lax.broadcasted_iota(jnp.int32, (SUB, SUB), 1)
    groups = SUB // GROUP
    for first in range(size - SUB, -1, -SUB):
        s_small = s_ref[first : first + SUB, first : first + SUB]
        t_small = t_ref[first : first + SUB, first : first + SUB]
        s_diag = jnp.sum(jnp.where(rows == cols, s_small, 0.0), axis=1, keepdims=True)
        t_diag = jnp.sum(jnp.where(rows == cols, t_small, 0.0), axis=1, keepdims=True)
        inverse = 1.0 / (beta * s_diag - alpha * t_diag)
        s_strict = jnp.where(rows < cols, s_small, 0.0)
        t_strict = jnp.where(rows < cols, t_small, 0.0)
        pending = [
            pending_ref[first + g * GROUP : first + (g + 1) * GROUP, :] for g in range(groups)
        ]
        for column in range(SUB - 1, -1, -1):
            own, row = divmod(column, GROUP)
            right = pending[own][row : row + 1, :]
            reciprocal = inverse[column : column + 1, :]
            x_ref[first + column : first + column + 1, :] = right * reciprocal
            scaled_beta = beta * reciprocal
            scaled_alpha = alpha * reciprocal
            for g in range(own + 1):
                span = slice(g * GROUP, (g + 1) * GROUP)
                factor = (
                    s_strict[span, column : column + 1] * scaled_beta
                    - t_strict[span, column : column + 1] * scaled_alpha
                )
                pending[g] = pending[g] - factor * right
        if first:
            block = x_ref[first : first + SUB, :]
            pending_ref[:first, :] = pending_ref[:first, :] - (
                exact_dot(s_ref[:first, first : first + SUB], beta * block)
                - exact_dot(t_ref[:first, first : first + SUB], alpha * block)
            )


def put_together(core, piece_refs, whole_ref):
    half = whole_ref.shape[0] // 2
    count = len(piece_refs) // 2
    height = half // count
    for index, ref in enumerate(piece_refs):
        side = core if index < count else 1 - core
        start = side * half + (index % count) * height
        whole_ref[pl.ds(pl.multiple_of(start, height), height), :] = ref[...]


def lower_kernel(
    slots, s_ref, t_ref, r_ref, values_a, values_b, selected, x_ref, alpha_ref, beta_ref, pending_ref
):
    alpha = table_lookup(selected[...], values_a[...])
    beta = table_lookup(selected[...], values_b[...])
    alpha_ref[...] = alpha
    beta_ref[...] = beta
    pending_ref[...] = r_ref[...]
    back_substitute(s_ref, t_ref, alpha, beta, pending_ref, x_ref)


def upper_kernel(slots, core, s_ref, t_ref, r_ref, alpha_ref, beta_ref, *refs):
    piece_refs, (x_ref, pending_ref, lower_ref) = refs[:-3], refs[-3:]
    block = x_ref.shape[0]
    alpha, beta = alpha_ref[...], beta_ref[...]
    put_together(core[0], piece_refs, lower_ref)
    lower = lower_ref[...]
    pending_ref[...] = r_ref[...] - (
        exact_dot(s_ref[:, block:], beta * lower) - exact_dot(t_ref[:, block:], alpha * lower)
    )
    back_substitute(s_ref, t_ref, alpha, beta, pending_ref, x_ref)


def solve_lower(slots, pencil_s, pencil_t, sides, value_alpha, value_beta, selected):
    block, eigs = pencil_s.shape[1] // 2, sides.shape[1]
    count, last = sides.shape[0] // block, slots.shape[0] - 1
    lanes = 128 if value_alpha.shape[0] % 128 == 0 else value_alpha.shape[0]
    table_shape = (value_alpha.shape[0] // lanes, lanes)
    corner = pl.BlockSpec((block, block), lambda i, slots: (lax.rem(slots[last], count), 1))
    whole = pl.BlockSpec((block, eigs), lambda i, slots: (lax.rem(slots[last], count), 0))
    line = pl.BlockSpec((1, eigs), lambda i, slots: (0, 0))
    table = pl.BlockSpec(table_shape, lambda i, slots: (0, 0))
    return pl.pallas_call(
        lower_kernel,
        out_shape=(
            jax.ShapeDtypeStruct((block, eigs), jnp.float32),
            jax.ShapeDtypeStruct((1, eigs), jnp.float32),
            jax.ShapeDtypeStruct((1, eigs), jnp.float32),
        ),
        grid_spec=pltpu.PrefetchScalarGridSpec(
            num_scalar_prefetch=1,
            grid=(1,),
            in_specs=[corner, corner, whole, table, table, line],
            out_specs=(pl.BlockSpec((block, eigs), lambda i, slots: (0, 0)), line, line),
            scratch_shapes=[pltpu.VMEM((block, eigs), jnp.float32)],
        ),
        compiler_params=pltpu.CompilerParams(vmem_limit_bytes=VMEM_BYTES),
        cost_estimate=pl.CostEstimate(flops=10**6, bytes_accessed=10**6, transcendentals=0),
        name="solve_lower",
    )(
        slots,
        pencil_s,
        pencil_t,
        sides,
        value_alpha.reshape(table_shape),
        value_beta.reshape(table_shape),
        selected[None, :],
    )


def solve_upper(slots, core, pencil_s, pencil_t, sides, alpha, beta, pieces):
    block, eigs = pencil_s.shape[1] // 2, sides.shape[1]
    count, index = sides.shape[0] // block, slots.shape[0] - 2
    band = pl.BlockSpec((block, 2 * block), lambda i, slots, core: (lax.rem(slots[index], count), 0))
    whole = pl.BlockSpec((block, eigs), lambda i, slots, core: (lax.rem(slots[index], count), 0))
    line = pl.BlockSpec((1, eigs), lambda i, slots, core: (0, 0))
    fixed = [pl.BlockSpec(piece.shape, lambda i, slots, core: (0, 0)) for piece in pieces]
    return pl.pallas_call(
        upper_kernel,
        out_shape=jax.ShapeDtypeStruct((block, eigs), jnp.float32),
        grid_spec=pltpu.PrefetchScalarGridSpec(
            num_scalar_prefetch=2,
            grid=(1,),
            in_specs=[band, band, whole, line, line, *fixed],
            out_specs=pl.BlockSpec((block, eigs), lambda i, slots, core: (0, 0)),
            scratch_shapes=[pltpu.VMEM((block, eigs), jnp.float32)] * 2,
        ),
        compiler_params=pltpu.CompilerParams(vmem_limit_bytes=VMEM_BYTES),
        cost_estimate=pl.CostEstimate(flops=10**6, bytes_accessed=10**6, transcendentals=0),
        name="solve_upper",
    )(slots, core, pencil_s, pencil_t, sides, alpha, beta, *pieces)


def sides_kernel(pieces, place, r_ref, s_ref, t_ref, alpha_ref, beta_ref, *refs):
    upper_pieces, lower_pieces = refs[:pieces], refs[pieces : 2 * pieces]
    out_ref, high_ref, low_ref, upper_ref, lower_ref = refs[2 * pieces :]
    block = upper_ref.shape[0]
    put_together(place[2], upper_pieces, upper_ref)
    put_together(place[2], lower_pieces, lower_ref)
    alpha, beta = alpha_ref[...], beta_ref[...]
    upper, lower = upper_ref[...], lower_ref[...]
    for slot in range(out_ref.shape[0] // block):
        span = slice(slot * block, (slot + 1) * block)
        update = exact_dot(s_ref[span, :block], beta * upper) - exact_dot(
            t_ref[span, :block], alpha * upper
        )
        update = update + (
            exact_dot(s_ref[span, block:], beta * lower)
            - exact_dot(t_ref[span, block:], alpha * lower)
        )
        fresh = r_ref[span, :] - update
        fresh = jnp.where(place[0] == slot, upper, fresh)
        out_ref[span, :] = jnp.where(place[1] == slot, lower, fresh)
    parts = place.shape[0] - 3
    width = block // parts
    for part in range(parts):
        rows = pl.ds(pl.multiple_of(place[3 + part] * width, width), width)
        for half, source in enumerate((upper_ref, lower_ref)):
            target = (2 * part + half) * width
            high, low = split_two(source[rows, :])
            high_ref[target : target + width, :] = high
            low_ref[target : target + width, :] = low


def update_sides(place, sides, pencil_s, pencil_t, alpha, beta, upper, lower):
    block, eigs = pencil_s.shape[1] // 2, sides.shape[1]
    vmem = pl.BlockSpec(memory_space=pltpu.VMEM)
    return pl.pallas_call(
        functools.partial(sides_kernel, len(upper)),
        out_shape=(
            jax.ShapeDtypeStruct(sides.shape, jnp.float32),
            jax.ShapeDtypeStruct((2 * block, eigs), jnp.bfloat16),
            jax.ShapeDtypeStruct((2 * block, eigs), jnp.bfloat16),
        ),
        in_specs=[pl.BlockSpec(memory_space=pltpu.SMEM)] + [vmem] * (5 + 2 * len(upper)),
        out_specs=(vmem, vmem, vmem),
        scratch_shapes=[pltpu.VMEM((block, eigs), jnp.float32)] * 2,
        compiler_params=pltpu.CompilerParams(vmem_limit_bytes=VMEM_BYTES),
        cost_estimate=pl.CostEstimate(
            flops=24 * sides.shape[0] * block * eigs, bytes_accessed=6 * 10**6, transcendentals=0
        ),
        name="update_sides",
    )(place, sides, pencil_s, pencil_t, alpha, beta, *upper, *lower)


def vectors_kernel(parts, paired, refs):
    vectors_ref, high_ref, low_ref = refs[:3]
    part_refs = refs[3 : 3 + parts]
    out_ref = refs[-1]
    tile = out_ref.shape[0]
    pieces = []
    for ref in part_refs:
        if paired:
            pieces.append(ref[pl.ds(0, tile, 2), :])
            pieces.append(ref[pl.ds(1, tile, 2), :])
        else:
            pieces.append(ref[...])
    basis = jnp.concatenate(pieces, axis=1)
    out_ref[...] = vectors_ref[...] + near_dot(basis, high_ref[...], low_ref[...])


def add_chunk(start, span, vectors, high, low, own, received, paired, previous):
    rows, eigs = vectors.shape
    tile = min(TILE, span)
    steps = span // tile
    base = start // tile
    per = 2 if paired else 1
    width = own.shape[1]
    fixed = pl.BlockSpec(high.shape, lambda i: (0, 0))
    at_rows = pl.BlockSpec((tile, eigs), lambda i: (base + i, 0))
    in_specs = [
        at_rows,
        fixed,
        fixed,
        pl.BlockSpec((per * tile, width), lambda i: (base + i, 0)),
    ]
    in_specs += [pl.BlockSpec((per * tile, width), lambda i: (i, 0)) for _ in received]
    operands = [vectors, high, low, own, *received]
    aliases = {}
    if previous is not None:
        aliases = {len(operands): 0}
        operands.append(previous)
        in_specs.append(pl.BlockSpec(memory_space=pl.ANY))

    def body(*refs):
        vectors_kernel(1 + len(received), paired, refs)

    return pl.pallas_call(
        body,
        out_shape=jax.ShapeDtypeStruct((rows, eigs), jnp.float32),
        grid=(steps,),
        in_specs=in_specs,
        out_specs=at_rows,
        input_output_aliases=aliases,
        compiler_params=pltpu.CompilerParams(vmem_limit_bytes=VMEM_BYTES),
        cost_estimate=pl.CostEstimate(
            flops=6 * span * high.shape[0] * eigs,
            bytes_accessed=12 * span * eigs,
            transcendentals=0,
        ),
        name="add_chunk",
    )(*operands)


def spread(block, owner, axis, size):
    me = lax.axis_index(axis)
    half = block.shape[0] // 2
    core = me % 2
    if size & (size - 1) or size < 2:
        block = lax.psum(jnp.where(me == owner, block, jnp.zeros_like(block)), axis)
        return [lax.dynamic_slice_in_dim(block, side * half, half, 0) for side in (core, 1 - core)]

    def exchange(value, bit):
        return lax.ppermute(value, axis, [(i, i ^ bit) for i in range(size)])

    height = half // PIECES
    bits = [1 << k for k in range(1, size.bit_length() - 1)]
    pieces = []
    for index in range(PIECES):
        kept = lax.dynamic_slice_in_dim(block, core * half + index * height, height, 0)
        given = lax.dynamic_slice_in_dim(block, (1 - core) * half + index * height, height, 0)
        pieces.append(jnp.where(me == owner, kept, exchange(given, 1)))
    apart = [(me ^ owner) & ~1] * PIECES
    for step in range(len(bits)):
        for index in range(PIECES):
            bit = bits[(step + index) % len(bits)]
            arrived = exchange(pieces[index], bit)
            pieces[index] = jnp.where(apart[index] == 0, pieces[index], arrived)
            apart[index] = apart[index] & ~bit
    return pieces + [exchange(piece, 1) for piece in pieces]


def on_device(
    row_size,
    col_size,
    right_sides,
    pencil_s,
    pencil_t,
    value_alpha,
    value_beta,
    selected,
    block_slot,
    right_basis,
    vectors,
):
    block = pencil_s.shape[1] // 2
    slot_count = right_sides.shape[0] // block
    block_count = block_slot.shape[0]
    rows, _, width = right_basis.shape
    me_row = lax.axis_index("row")
    me_col = lax.axis_index("col")
    slot_upper = block_slot[block_count - 2]
    slot_lower = block_slot[block_count - 1]

    paired = width % 128 == 0
    own = right_basis.reshape((2 * rows, width) if paired else (rows, 2 * width))
    per = own.shape[0] // rows
    chunks = []
    start = 0
    for parts in SHARES:
        span = rows * parts // sum(SHARES)
        piece = own[per * start : per * (start + span)]
        received = [
            lax.ppermute(piece, "col", [(i, (i + step) % col_size) for i in range(col_size)])
            for step in range(1, col_size)
        ]
        chunks.append((start, span, received))
        start += span

    place = jnp.stack(
        [slot_upper - me_row * slot_count, slot_lower - me_row * slot_count, me_row % 2]
        + [(me_col - step) % col_size for step in range(col_size)]
    ).astype(jnp.int32)
    lower, alpha, beta = solve_lower(
        block_slot, pencil_s, pencil_t, right_sides, value_alpha, value_beta, selected
    )
    lower = spread(lower, slot_lower // slot_count, "row", row_size)
    upper = solve_upper(
        block_slot, place[2:3], pencil_s, pencil_t, right_sides, alpha, beta, lower
    )
    upper = spread(upper, slot_upper // slot_count, "row", row_size)
    updated_sides, high, low = update_sides(
        place, right_sides, pencil_s, pencil_t, alpha, beta, upper, lower
    )
    updated_vectors = None
    for start, span, received in chunks:
        updated_vectors = add_chunk(
            start, span, vectors, high, low, own, received, paired, updated_vectors
        )
    return (updated_sides, updated_vectors)


def solution(mesh):
    body = functools.partial(on_device, mesh.shape["row"], mesh.shape["col"])
    return jax.shard_map(
        body,
        mesh=mesh,
        in_specs=(
            P("row", "col"),
            P("row", None),
            P("row", None),
            P(),
            P(),
            P("col"),
            P(),
            P("row", None, "col"),
            P("row", "col"),
        ),
        out_specs=(P("row", "col"), P("row", "col")),
        check_vma=False,
    )
```

```python
import functools
import math

import jax
import jax.numpy as jnp
from jax import lax
from jax.experimental import pallas as pl
from jax.experimental.pallas import tpu as pltpu
from jax.sharding import PartitionSpec as P

SUB = 32
GROUP = 8
VMEM_BYTES = 48 * 1024 * 1024
FULL_VMEM_BYTES = 60 * 1024 * 1024
SHARES = (6, 12, 12, 1, 1)
TILE = 512


def exact_dot(left, right):
    return jnp.dot(left, right, precision=lax.Precision.HIGHEST, preferred_element_type=jnp.float32)


def split_two(value):
    high = value.astype(jnp.bfloat16)
    low = (value - high.astype(jnp.float32)).astype(jnp.bfloat16)
    return high, low


def split_three(value):
    high = value.astype(jnp.bfloat16)
    rest = value - high.astype(jnp.float32)
    middle = rest.astype(jnp.bfloat16)
    low = (rest - middle.astype(jnp.float32)).astype(jnp.bfloat16)
    return high, middle, low


def stacked_dot(left, right):
    high, middle, low = split_three(left)
    top, mid, end = split_three(right)
    return jnp.dot(
        jnp.concatenate([high, middle, high, middle, high, low], axis=1),
        jnp.concatenate([top, top, mid, mid, end, top], axis=0),
        preferred_element_type=jnp.float32,
    )


def near_dot(left, right_high, right_low):
    high, low = split_two(left)
    dot = functools.partial(jnp.dot, preferred_element_type=jnp.float32)
    return dot(high, right_high) + (dot(low, right_high) + dot(high, right_low))


def table_lookup(selected, table):
    table_rows, lanes = table.shape
    lane = lax.broadcasted_iota(jnp.int32, (lanes, selected.shape[1]), 0)
    in_lane = jnp.where(lane == selected % lanes, 1.0, 0.0)
    candidates = exact_dot(table, in_lane)
    row = lax.broadcasted_iota(jnp.int32, candidates.shape, 0)
    return jnp.sum(jnp.where(row == selected // lanes, candidates, 0.0), axis=0, keepdims=True)


def back_substitute(s_ref, t_ref, alpha, beta, pending_ref, x_ref):
    size = x_ref.shape[0]
    rows = lax.broadcasted_iota(jnp.int32, (SUB, SUB), 0)
    cols = lax.broadcasted_iota(jnp.int32, (SUB, SUB), 1)
    groups = SUB // GROUP
    for first in range(size - SUB, -1, -SUB):
        s_small = s_ref[first : first + SUB, first : first + SUB]
        t_small = t_ref[first : first + SUB, first : first + SUB]
        s_diag = jnp.sum(jnp.where(rows == cols, s_small, 0.0), axis=1, keepdims=True)
        t_diag = jnp.sum(jnp.where(rows == cols, t_small, 0.0), axis=1, keepdims=True)
        inverse = 1.0 / (beta * s_diag - alpha * t_diag)
        s_strict = jnp.where(rows < cols, s_small, 0.0)
        t_strict = jnp.where(rows < cols, t_small, 0.0)
        pending = [
            pending_ref[first + g * GROUP : first + (g + 1) * GROUP, :] for g in range(groups)
        ]
        for column in range(SUB - 1, -1, -1):
            own, row = divmod(column, GROUP)
            right = pending[own][row : row + 1, :]
            reciprocal = inverse[column : column + 1, :]
            x_ref[first + column : first + column + 1, :] = right * reciprocal
            scaled_beta = beta * reciprocal
            scaled_alpha = alpha * reciprocal
            for g in range(own + 1):
                span = slice(g * GROUP, (g + 1) * GROUP)
                factor = (
                    s_strict[span, column : column + 1] * scaled_beta
                    - t_strict[span, column : column + 1] * scaled_alpha
                )
                pending[g] = pending[g] - factor * right
        if first:
            block = x_ref[first : first + SUB, :]
            columns = slice(first, first + SUB)
            pending_ref[:first, :] = pending_ref[:first, :] - stacked_dot(
                jnp.concatenate([s_ref[:first, columns], t_ref[:first, columns]], axis=1),
                jnp.concatenate([beta * block, -alpha * block], axis=0),
            )


def put_together(core, side, piece_refs, whole_ref):
    quarter = whole_ref.shape[0] // 4
    places = [(core, side), (core, 1 - side), (1 - core, side), (1 - core, 1 - side)]
    for ref, (half, part) in zip(piece_refs, places):
        start = (2 * half + part) * quarter
        whole_ref[pl.ds(pl.multiple_of(start, quarter), quarter), :] = ref[...]


def lower_kernel(bounds, slots, s_ref, t_ref, r_ref, values_a, values_b, selected, own_ref, *refs):
    x_ref, alpha_ref, beta_ref, *chunk_refs, pending_ref, done = refs
    copies = [
        pltpu.make_async_copy(own_ref.at[pl.ds(start, span)], ref, done.at[index])
        for index, ((start, span), ref) in enumerate(zip(bounds, chunk_refs))
    ]
    for copy in copies:
        copy.start()
    alpha = table_lookup(selected[...], values_a[...])
    beta = table_lookup(selected[...], values_b[...])
    alpha_ref[...] = alpha
    beta_ref[...] = beta
    pending_ref[...] = r_ref[...]
    back_substitute(s_ref, t_ref, alpha, beta, pending_ref, x_ref)
    for copy in copies:
        copy.wait()


def upper_kernel(slots, lane, s_ref, t_ref, r_ref, alpha_ref, beta_ref, *refs):
    piece_refs, (x_ref, pending_ref, lower_ref) = refs[:4], refs[-3:]
    block = x_ref.shape[0]
    alpha, beta = alpha_ref[...], beta_ref[...]
    put_together(lane[0], lane[1], piece_refs, lower_ref)
    lower = lower_ref[...]
    pending_ref[...] = r_ref[...] - (
        exact_dot(s_ref[:, block:], beta * lower) - exact_dot(t_ref[:, block:], alpha * lower)
    )
    back_substitute(s_ref, t_ref, alpha, beta, pending_ref, x_ref)


def solve_lower(slots, pencil_s, pencil_t, sides, value_alpha, value_beta, selected, own, bounds):
    block, eigs = pencil_s.shape[1] // 2, sides.shape[1]
    count, last = sides.shape[0] // block, slots.shape[0] - 1
    lanes = 128 if value_alpha.shape[0] % 128 == 0 else value_alpha.shape[0]
    table_shape = (value_alpha.shape[0] // lanes, lanes)
    corner = pl.BlockSpec((block, block), lambda i, slots: (lax.rem(slots[last], count), 1))
    whole = pl.BlockSpec((block, eigs), lambda i, slots: (lax.rem(slots[last], count), 0))
    line = pl.BlockSpec((1, eigs), lambda i, slots: (0, 0))
    table = pl.BlockSpec(table_shape, lambda i, slots: (0, 0))
    anywhere = pl.BlockSpec(memory_space=pl.ANY)
    return pl.pallas_call(
        functools.partial(lower_kernel, bounds),
        out_shape=(
            jax.ShapeDtypeStruct((block, eigs), jnp.float32),
            jax.ShapeDtypeStruct((1, eigs), jnp.float32),
            jax.ShapeDtypeStruct((1, eigs), jnp.float32),
            *[jax.ShapeDtypeStruct((span, own.shape[1]), jnp.float32) for _, span in bounds],
        ),
        grid_spec=pltpu.PrefetchScalarGridSpec(
            num_scalar_prefetch=1,
            grid=(1,),
            in_specs=[corner, corner, whole, table, table, line, anywhere],
            out_specs=(
                pl.BlockSpec((block, eigs), lambda i, slots: (0, 0)),
                line,
                line,
                *[anywhere] * len(bounds),
            ),
            scratch_shapes=[
                pltpu.VMEM((block, eigs), jnp.float32),
                pltpu.SemaphoreType.DMA((len(bounds),)),
            ],
        ),
        compiler_params=pltpu.CompilerParams(vmem_limit_bytes=FULL_VMEM_BYTES),
        cost_estimate=pl.CostEstimate(flops=10**6, bytes_accessed=10**6, transcendentals=0),
        name="solve_lower",
    )(
        slots,
        pencil_s,
        pencil_t,
        sides,
        value_alpha.reshape(table_shape),
        value_beta.reshape(table_shape),
        selected[None, :],
        own,
    )


def solve_upper(slots, lane, pencil_s, pencil_t, sides, alpha, beta, pieces):
    block, eigs = pencil_s.shape[1] // 2, sides.shape[1]
    count, index = sides.shape[0] // block, slots.shape[0] - 2
    band = pl.BlockSpec((block, 2 * block), lambda i, slots, lane: (lax.rem(slots[index], count), 0))
    whole = pl.BlockSpec((block, eigs), lambda i, slots, lane: (lax.rem(slots[index], count), 0))
    line = pl.BlockSpec((1, eigs), lambda i, slots, lane: (0, 0))
    fixed = [pl.BlockSpec(piece.shape, lambda i, slots, lane: (0, 0)) for piece in pieces]
    return pl.pallas_call(
        upper_kernel,
        out_shape=jax.ShapeDtypeStruct((block, eigs), jnp.float32),
        grid_spec=pltpu.PrefetchScalarGridSpec(
            num_scalar_prefetch=2,
            grid=(1,),
            in_specs=[band, band, whole, line, line, *fixed],
            out_specs=pl.BlockSpec((block, eigs), lambda i, slots, lane: (0, 0)),
            scratch_shapes=[pltpu.VMEM((block, eigs), jnp.float32)] * 2,
        ),
        compiler_params=pltpu.CompilerParams(vmem_limit_bytes=VMEM_BYTES),
        cost_estimate=pl.CostEstimate(flops=10**6, bytes_accessed=10**6, transcendentals=0),
        name="solve_upper",
    )(slots, lane, pencil_s, pencil_t, sides, alpha, beta, *pieces)


def sides_kernel(pieces, place, r_ref, s_ref, t_ref, alpha_ref, beta_ref, *refs):
    upper_pieces, lower_pieces = refs[:pieces], refs[pieces : 2 * pieces]
    out_ref, high_ref, low_ref, upper_ref, lower_ref = refs[2 * pieces :]
    block = upper_ref.shape[0]
    put_together(place[2], place[3], upper_pieces, upper_ref)
    put_together(place[2], place[3], lower_pieces, lower_ref)
    alpha, beta = alpha_ref[...], beta_ref[...]
    upper, lower = upper_ref[...], lower_ref[...]
    for slot in range(out_ref.shape[0] // block):
        span = slice(slot * block, (slot + 1) * block)
        update = exact_dot(s_ref[span, :block], beta * upper) - exact_dot(
            t_ref[span, :block], alpha * upper
        )
        update = update + (
            exact_dot(s_ref[span, block:], beta * lower)
            - exact_dot(t_ref[span, block:], alpha * lower)
        )
        fresh = r_ref[span, :] - update
        fresh = jnp.where(place[0] == slot, upper, fresh)
        out_ref[span, :] = jnp.where(place[1] == slot, lower, fresh)
    parts = place.shape[0] - 4
    width = block // parts
    for part in range(parts):
        rows = pl.ds(pl.multiple_of(place[4 + part] * width, width), width)
        for half, source in enumerate((upper_ref, lower_ref)):
            target = (2 * part + half) * width
            high, low = split_two(source[rows, :])
            high_ref[target : target + width, :] = high
            low_ref[target : target + width, :] = low


def update_sides(place, sides, pencil_s, pencil_t, alpha, beta, upper, lower):
    block, eigs = pencil_s.shape[1] // 2, sides.shape[1]
    vmem = pl.BlockSpec(memory_space=pltpu.VMEM)
    return pl.pallas_call(
        functools.partial(sides_kernel, len(upper)),
        out_shape=(
            jax.ShapeDtypeStruct(sides.shape, jnp.float32),
            jax.ShapeDtypeStruct((2 * block, eigs), jnp.bfloat16),
            jax.ShapeDtypeStruct((2 * block, eigs), jnp.bfloat16),
        ),
        in_specs=[pl.BlockSpec(memory_space=pltpu.SMEM)] + [vmem] * (5 + 2 * len(upper)),
        out_specs=(vmem, vmem, vmem),
        scratch_shapes=[pltpu.VMEM((block, eigs), jnp.float32)] * 2,
        compiler_params=pltpu.CompilerParams(vmem_limit_bytes=VMEM_BYTES),
        cost_estimate=pl.CostEstimate(
            flops=24 * sides.shape[0] * block * eigs, bytes_accessed=6 * 10**6, transcendentals=0
        ),
        name="update_sides",
    )(place, sides, pencil_s, pencil_t, alpha, beta, *upper, *lower)


def vectors_kernel(parts, paired, refs):
    vectors_ref, high_ref, low_ref = refs[:3]
    part_refs = refs[3 : 3 + parts]
    out_ref = refs[-1]
    tile = out_ref.shape[0]
    pieces = []
    for ref in part_refs:
        if paired:
            pieces.append(ref[pl.ds(0, tile, 2), :])
            pieces.append(ref[pl.ds(1, tile, 2), :])
        else:
            pieces.append(ref[...])
    basis = jnp.concatenate(pieces, axis=1)
    out_ref[...] = vectors_ref[...] + near_dot(basis, high_ref[...], low_ref[...])


def add_chunk(start, span, vectors, high, low, own, received, paired, previous):
    rows, eigs = vectors.shape
    tile = math.gcd(start, span)
    while tile > TILE:
        tile //= 2
    steps = span // tile
    base = start // tile
    per = 2 if paired else 1
    width = own.shape[1]
    fixed = pl.BlockSpec(high.shape, lambda i: (0, 0))
    at_rows = pl.BlockSpec((tile, eigs), lambda i: (base + i, 0))
    in_specs = [
        at_rows,
        fixed,
        fixed,
        pl.BlockSpec((per * tile, width), lambda i: (base + i, 0)),
    ]
    in_specs += [pl.BlockSpec((per * tile, width), lambda i: (i, 0)) for _ in received]
    operands = [vectors, high, low, own, *received]
    aliases = {}
    if previous is not None:
        aliases = {len(operands): 0}
        operands.append(previous)
        in_specs.append(pl.BlockSpec(memory_space=pl.ANY))

    def body(*refs):
        vectors_kernel(1 + len(received), paired, refs)

    return pl.pallas_call(
        body,
        out_shape=jax.ShapeDtypeStruct((rows, eigs), jnp.float32),
        grid=(steps,),
        in_specs=in_specs,
        out_specs=at_rows,
        input_output_aliases=aliases,
        compiler_params=pltpu.CompilerParams(vmem_limit_bytes=VMEM_BYTES),
        cost_estimate=pl.CostEstimate(
            flops=6 * span * high.shape[0] * eigs,
            bytes_accessed=12 * span * eigs,
            transcendentals=0,
        ),
        name="add_chunk",
    )(*operands)


def choose(flag, kept, arrived, ties):
    def body(flag_ref, kept_ref, arrived_ref, *refs):
        refs[-1][...] = jnp.where(flag_ref[0] != 0, kept_ref[...], arrived_ref[...])

    vmem = pl.BlockSpec(memory_space=pltpu.VMEM)
    return pl.pallas_call(
        body,
        out_shape=jax.ShapeDtypeStruct(kept.shape, kept.dtype),
        in_specs=[pl.BlockSpec(memory_space=pltpu.SMEM), vmem, vmem]
        + [pl.BlockSpec(memory_space=pl.ANY)] * len(ties),
        out_specs=vmem,
        compiler_params=pltpu.CompilerParams(vmem_limit_bytes=VMEM_BYTES),
        cost_estimate=pl.CostEstimate(flops=10**5, bytes_accessed=10**5, transcendentals=0),
        name="choose",
    )(flag.astype(jnp.int32)[None], kept, arrived, *ties)


def spread(block, owner, axis, size, ties):
    me = lax.axis_index(axis)
    half, quarter = block.shape[0] // 2, block.shape[0] // 4
    core, side = me & 1, (me >> 1) & 1
    if size & (size - 1) or size < 4:
        block = lax.psum(jnp.where(me == owner, block, jnp.zeros_like(block)), axis)
        places = [(core, side), (core, 1 - side), (1 - core, side), (1 - core, 1 - side)]
        return [
            lax.dynamic_slice_in_dim(block, (2 * first + second) * quarter, quarter, 0)
            for first, second in places
        ]

    def exchange(value, bit):
        return lax.ppermute(value, axis, [(i, i ^ bit) for i in range(size)])

    apart = me ^ owner
    kept = lax.dynamic_slice_in_dim(block, core * half, half, 0)
    given = lax.dynamic_slice_in_dim(block, (1 - core) * half, half, 0)
    kept = jnp.where(apart == 0, kept, exchange(given, 1))
    given = lax.dynamic_slice_in_dim(kept, (1 - side) * quarter, quarter, 0)
    kept = lax.dynamic_slice_in_dim(kept, side * quarter, quarter, 0)
    kept = choose(apart & ~1 == 0, kept, exchange(given, 2), ties)
    bit = 4
    while bit < size:
        kept = jnp.where(apart & ~(bit - 1) == 0, kept, exchange(kept, bit))
        bit *= 2
    beside = exchange(kept, 2)
    return [kept, beside, exchange(kept, 1), exchange(beside, 1)]


def on_device(
    row_size,
    col_size,
    right_sides,
    pencil_s,
    pencil_t,
    value_alpha,
    value_beta,
    selected,
    block_slot,
    right_basis,
    vectors,
):
    block = pencil_s.shape[1] // 2
    slot_count = right_sides.shape[0] // block
    block_count = block_slot.shape[0]
    rows, _, width = right_basis.shape
    me_row = lax.axis_index("row")
    me_col = lax.axis_index("col")
    slot_upper = block_slot[block_count - 2]
    slot_lower = block_slot[block_count - 1]

    paired = width % 128 == 0
    own = right_basis.reshape((2 * rows, width) if paired else (rows, 2 * width))
    per = own.shape[0] // rows
    bounds, start = [], 0
    for parts in SHARES:
        span = rows * parts // sum(SHARES)
        bounds.append((start, span))
        start += span
    local = [(per * start, per * span) for start, span in bounds]

    def fetch(piece):
        return [
            lax.ppermute(piece, "col", [(i, (i + step) % col_size) for i in range(col_size)])
            for step in range(1, col_size)
        ]

    seed = fetch(own[: local[0][1]])
    place = jnp.stack(
        [slot_upper - me_row * slot_count, slot_lower - me_row * slot_count]
        + [me_row & 1, (me_row >> 1) & 1]
        + [(me_col - step) % col_size for step in range(col_size)]
    ).astype(jnp.int32)
    lower, alpha, beta, *pieces = solve_lower(
        *[block_slot, pencil_s, pencil_t, right_sides, value_alpha, value_beta, selected],
        *[own, local[1:]],
    )
    received = [seed] + [fetch(piece) for piece in pieces]
    lower = spread(lower, slot_lower // slot_count, "row", row_size, received[0])
    upper = solve_upper(
        block_slot, place[2:4], pencil_s, pencil_t, right_sides, alpha, beta, lower
    )
    upper = spread(upper, slot_upper // slot_count, "row", row_size, received[1])
    updated_sides, high, low = update_sides(
        place, right_sides, pencil_s, pencil_t, alpha, beta, upper, lower
    )
    updated_vectors = None
    for (start, span), arrived in zip(bounds, received):
        updated_vectors = add_chunk(
            start, span, vectors, high, low, own, arrived, paired, updated_vectors
        )
    return (updated_sides, updated_vectors)


def solution(mesh):
    body = functools.partial(on_device, mesh.shape["row"], mesh.shape["col"])
    return jax.shard_map(
        body,
        mesh=mesh,
        in_specs=(
            P("row", "col"),
            P("row", None),
            P("row", None),
            P(),
            P(),
            P("col"),
            P(),
            P("row", None, "col"),
            P("row", "col"),
        ),
        out_specs=(P("row", "col"), P("row", "col")),
        check_vma=False,
    )
```

```python
import functools
import math

import jax
import jax.numpy as jnp
from jax import lax
from jax.experimental import pallas as pl
from jax.experimental.pallas import tpu as pltpu
from jax.sharding import PartitionSpec as P

SUB = 32
GROUP = 8
VMEM_BYTES = 48 * 1024 * 1024
FULL_VMEM_BYTES = 59 * 1024 * 1024
SMALL_VMEM_BYTES = 12 * 1024 * 1024
SHARES = (7, 12, 11, 1, 1)
SIDES_BEFORE = 2
TILE = 512


def exact_dot(left, right):
    return jnp.dot(left, right, precision=lax.Precision.HIGHEST, preferred_element_type=jnp.float32)


def split_two(value):
    high = value.astype(jnp.bfloat16)
    low = (value - high.astype(jnp.float32)).astype(jnp.bfloat16)
    return high, low


def split_three(value):
    high = value.astype(jnp.bfloat16)
    rest = value - high.astype(jnp.float32)
    middle = rest.astype(jnp.bfloat16)
    low = (rest - middle.astype(jnp.float32)).astype(jnp.bfloat16)
    return high, middle, low


def stacked_dot(left, right):
    high, middle, low = split_three(left)
    top, mid, end = split_three(right)
    return jnp.dot(
        jnp.concatenate([high, middle, high, middle, high, low], axis=1),
        jnp.concatenate([top, top, mid, mid, end, top], axis=0),
        preferred_element_type=jnp.float32,
    )


def table_lookup(selected, table):
    table_rows, lanes = table.shape
    lane = lax.broadcasted_iota(jnp.int32, (lanes, selected.shape[1]), 0)
    in_lane = jnp.where(lane == selected % lanes, 1.0, 0.0)
    candidates = exact_dot(table, in_lane)
    row = lax.broadcasted_iota(jnp.int32, candidates.shape, 0)
    return jnp.sum(jnp.where(row == selected // lanes, candidates, 0.0), axis=0, keepdims=True)


def back_substitute(s_ref, t_ref, alpha, beta, pending_ref, x_ref, midway=None):
    size = x_ref.shape[0]
    rows = lax.broadcasted_iota(jnp.int32, (SUB, SUB), 0)
    cols = lax.broadcasted_iota(jnp.int32, (SUB, SUB), 1)
    groups = SUB // GROUP
    for first in range(size - SUB, -1, -SUB):
        if midway is not None and first == size // 2 - SUB:
            midway()
        s_small = s_ref[first : first + SUB, first : first + SUB]
        t_small = t_ref[first : first + SUB, first : first + SUB]
        s_diag = jnp.sum(jnp.where(rows == cols, s_small, 0.0), axis=1, keepdims=True)
        t_diag = jnp.sum(jnp.where(rows == cols, t_small, 0.0), axis=1, keepdims=True)
        inverse = 1.0 / (beta * s_diag - alpha * t_diag)
        s_strict = jnp.where(rows < cols, s_small, 0.0)
        t_strict = jnp.where(rows < cols, t_small, 0.0)
        pending = [
            pending_ref[first + g * GROUP : first + (g + 1) * GROUP, :] for g in range(groups)
        ]
        for column in range(SUB - 1, -1, -1):
            own, row = divmod(column, GROUP)
            right = pending[own][row : row + 1, :]
            reciprocal = inverse[column : column + 1, :]
            x_ref[first + column : first + column + 1, :] = right * reciprocal
            scaled_beta = beta * reciprocal
            scaled_alpha = alpha * reciprocal
            for g in range(own + 1):
                span = slice(g * GROUP, (g + 1) * GROUP)
                factor = (
                    s_strict[span, column : column + 1] * scaled_beta
                    - t_strict[span, column : column + 1] * scaled_alpha
                )
                pending[g] = pending[g] - factor * right
        if first:
            block = x_ref[first : first + SUB, :]
            columns = slice(first, first + SUB)
            pending_ref[:first, :] = pending_ref[:first, :] - stacked_dot(
                jnp.concatenate([s_ref[:first, columns], t_ref[:first, columns]], axis=1),
                jnp.concatenate([beta * block, -alpha * block], axis=0),
            )


def put_together(core, side, piece_refs, whole_ref):
    quarter = whole_ref.shape[0] // 4
    places = [(core, side), (core, 1 - side), (1 - core, side), (1 - core, 1 - side)]
    for ref, (half, part) in zip(piece_refs, places):
        start = (2 * half + part) * quarter
        whole_ref[pl.ds(pl.multiple_of(start, quarter), quarter), :] = ref[...]


def lower_kernel(bounds, slots, s_ref, t_ref, r_ref, values_a, values_b, selected, own_ref, *refs):
    x_ref, alpha_ref, beta_ref = refs[:3]
    chunk_refs, held_refs = refs[3 : 3 + len(bounds)], refs[3 + len(bounds) : -2]
    pending_ref, done = refs[-2:]
    inward, outward = [], []
    for index, (start, span) in enumerate(bounds):
        held, chunk = held_refs[index], chunk_refs[index]
        inward.append(pltpu.make_async_copy(own_ref.at[pl.ds(start, span)], held, done.at[0, index]))
        outward.append(pltpu.make_async_copy(held, chunk, done.at[1, index]))
    for copy in inward:
        copy.start()
    alpha = table_lookup(selected[...], values_a[...])
    beta = table_lookup(selected[...], values_b[...])
    alpha_ref[...] = alpha
    beta_ref[...] = beta
    pending_ref[...] = r_ref[...]

    def hand_on():
        for arrive, leave in zip(inward, outward):
            arrive.wait()
            leave.start()

    back_substitute(s_ref, t_ref, alpha, beta, pending_ref, x_ref, hand_on)
    for copy in outward:
        copy.wait()


def upper_kernel(slots, lane, s_ref, t_ref, r_ref, alpha_ref, beta_ref, *refs):
    piece_refs, (x_ref, lower_ref, pending_ref) = refs[:4], refs[-3:]
    block = x_ref.shape[0]
    alpha, beta = alpha_ref[...], beta_ref[...]
    put_together(lane[0], lane[1], piece_refs, lower_ref)
    lower = lower_ref[...]
    pending_ref[...] = r_ref[...] - (
        exact_dot(s_ref[:, block:], beta * lower) - exact_dot(t_ref[:, block:], alpha * lower)
    )
    back_substitute(s_ref, t_ref, alpha, beta, pending_ref, x_ref)


def solve_lower(slots, pencil_s, pencil_t, sides, value_alpha, value_beta, selected, own, bounds):
    block, eigs = pencil_s.shape[1] // 2, sides.shape[1]
    count, last = sides.shape[0] // block, slots.shape[0] - 1
    lanes = 128 if value_alpha.shape[0] % 128 == 0 else value_alpha.shape[0]
    table_shape = (value_alpha.shape[0] // lanes, lanes)
    corner = pl.BlockSpec((block, block), lambda i, slots: (lax.rem(slots[last], count), 1))
    whole = pl.BlockSpec((block, eigs), lambda i, slots: (lax.rem(slots[last], count), 0))
    line = pl.BlockSpec((1, eigs), lambda i, slots: (0, 0))
    table = pl.BlockSpec(table_shape, lambda i, slots: (0, 0))
    anywhere = pl.BlockSpec(memory_space=pl.ANY)
    return pl.pallas_call(
        functools.partial(lower_kernel, bounds),
        out_shape=(
            jax.ShapeDtypeStruct((block, eigs), jnp.float32),
            jax.ShapeDtypeStruct((1, eigs), jnp.float32),
            jax.ShapeDtypeStruct((1, eigs), jnp.float32),
            *[jax.ShapeDtypeStruct((span, own.shape[1]), jnp.float32) for _, span in bounds],
        ),
        grid_spec=pltpu.PrefetchScalarGridSpec(
            num_scalar_prefetch=1,
            grid=(1,),
            in_specs=[corner, corner, whole, table, table, line, anywhere],
            out_specs=(
                pl.BlockSpec((block, eigs), lambda i, slots: (0, 0)),
                line,
                line,
                *[anywhere] * len(bounds),
            ),
            scratch_shapes=[
                *[pltpu.VMEM((span, own.shape[1]), jnp.float32) for _, span in bounds],
                pltpu.VMEM((block, eigs), jnp.float32),
                pltpu.SemaphoreType.DMA((2, len(bounds))),
            ],
        ),
        compiler_params=pltpu.CompilerParams(vmem_limit_bytes=FULL_VMEM_BYTES),
        cost_estimate=pl.CostEstimate(flops=10**6, bytes_accessed=10**6, transcendentals=0),
        name="solve_lower",
    )(
        slots,
        pencil_s,
        pencil_t,
        sides,
        value_alpha.reshape(table_shape),
        value_beta.reshape(table_shape),
        selected[None, :],
        own,
    )


def solve_upper(slots, lane, pencil_s, pencil_t, sides, alpha, beta, pieces):
    block, eigs = pencil_s.shape[1] // 2, sides.shape[1]
    count, index = sides.shape[0] // block, slots.shape[0] - 2
    band = pl.BlockSpec((block, 2 * block), lambda i, slots, lane: (lax.rem(slots[index], count), 0))
    whole = pl.BlockSpec((block, eigs), lambda i, slots, lane: (lax.rem(slots[index], count), 0))
    line = pl.BlockSpec((1, eigs), lambda i, slots, lane: (0, 0))
    fixed = [pl.BlockSpec(piece.shape, lambda i, slots, lane: (0, 0)) for piece in pieces]
    return pl.pallas_call(
        upper_kernel,
        out_shape=(jax.ShapeDtypeStruct((block, eigs), jnp.float32),) * 2,
        grid_spec=pltpu.PrefetchScalarGridSpec(
            num_scalar_prefetch=2,
            grid=(1,),
            in_specs=[band, band, whole, line, line, *fixed],
            out_specs=(pl.BlockSpec((block, eigs), lambda i, slots, lane: (0, 0)),) * 2,
            scratch_shapes=[pltpu.VMEM((block, eigs), jnp.float32)],
        ),
        compiler_params=pltpu.CompilerParams(vmem_limit_bytes=FULL_VMEM_BYTES),
        cost_estimate=pl.CostEstimate(flops=10**6, bytes_accessed=10**6, transcendentals=0),
        name="solve_upper",
    )(slots, lane, pencil_s, pencil_t, sides, alpha, beta, *pieces)


def order_kernel(lane, *refs):
    piece_refs, (lower_ref, upper_ref, terms_ref) = refs[:4], refs[4:]
    put_together(lane[0], lane[1], piece_refs, upper_ref)
    block = upper_ref.shape[0]
    parts = lane.shape[0] - 2
    width = block // parts
    for part in range(parts):
        rows = pl.ds(pl.multiple_of(lane[2 + part] * width, width), width)
        for half, source in enumerate((upper_ref, lower_ref)):
            target = (2 * part + half) * width
            high, low = split_two(source[rows, :])
            for term, value in enumerate((high, high, low)):
                first = 2 * block * term + target
                terms_ref[first : first + width, :] = value


def order_rows(lane, pieces, lower):
    block, eigs = lower.shape
    vmem = pl.BlockSpec(memory_space=pltpu.VMEM)
    return pl.pallas_call(
        order_kernel,
        out_shape=(
            jax.ShapeDtypeStruct((block, eigs), jnp.float32),
            jax.ShapeDtypeStruct((6 * block, eigs), jnp.bfloat16),
        ),
        in_specs=[pl.BlockSpec(memory_space=pltpu.SMEM)] + [vmem] * (len(pieces) + 1),
        out_specs=(vmem, vmem),
        compiler_params=pltpu.CompilerParams(vmem_limit_bytes=SMALL_VMEM_BYTES),
        cost_estimate=pl.CostEstimate(flops=10**6, bytes_accessed=10**6, transcendentals=0),
        name="order_rows",
    )(lane, *pieces, lower)


def sides_kernel(slots, me, r_ref, s_ref, t_ref, alpha_ref, beta_ref, upper_ref, lower_ref, out_ref):
    block = upper_ref.shape[0]
    count = out_ref.shape[0] // block
    base = me[0] * count
    alpha, beta = alpha_ref[...], beta_ref[...]
    upper, lower = upper_ref[...], lower_ref[...]
    for slot in range(count):
        span = slice(slot * block, (slot + 1) * block)
        update = exact_dot(s_ref[span, :block], beta * upper) - exact_dot(
            t_ref[span, :block], alpha * upper
        )
        update = update + (
            exact_dot(s_ref[span, block:], beta * lower)
            - exact_dot(t_ref[span, block:], alpha * lower)
        )
        fresh = r_ref[span, :] - update
        fresh = jnp.where(slots[slots.shape[0] - 2] == base + slot, upper, fresh)
        out_ref[span, :] = jnp.where(slots[slots.shape[0] - 1] == base + slot, lower, fresh)


def update_sides(slots, me, sides, pencil_s, pencil_t, alpha, beta, upper, lower):
    smem, vmem = pl.BlockSpec(memory_space=pltpu.SMEM), pl.BlockSpec(memory_space=pltpu.VMEM)
    return pl.pallas_call(
        sides_kernel,
        out_shape=jax.ShapeDtypeStruct(sides.shape, jnp.float32),
        in_specs=[smem] * 2 + [vmem] * 7,
        out_specs=vmem,
        compiler_params=pltpu.CompilerParams(vmem_limit_bytes=VMEM_BYTES),
        cost_estimate=pl.CostEstimate(
            flops=24 * sides.size * upper.shape[0], bytes_accessed=6 * 10**6, transcendentals=0
        ),
        name="update_sides",
    )(slots, me, sides, pencil_s, pencil_t, alpha, beta, upper, lower)


def vectors_kernel(parts, paired, refs):
    vectors_ref, terms_ref = refs[:2]
    part_refs = refs[2 : 2 + parts]
    out_ref = refs[-1]
    tile = out_ref.shape[0]
    pieces = []
    for ref in part_refs:
        if paired:
            pieces.append(ref[pl.ds(0, tile, 2), :])
            pieces.append(ref[pl.ds(1, tile, 2), :])
        else:
            pieces.append(ref[...])
    basis = jnp.concatenate(pieces, axis=1)
    high, low = split_two(basis)
    product = jnp.dot(
        jnp.concatenate([high, low, high], axis=1),
        terms_ref[...],
        preferred_element_type=jnp.float32,
    )
    out_ref[...] = vectors_ref[...] + product


def add_chunk(start, span, vectors, terms, own, received, paired, previous, ties):
    rows, eigs = vectors.shape
    tile = span
    while tile > TILE:
        tile //= 2
    steps = span // tile
    unit = math.gcd(start, tile)

    def row_of(i):
        return (start // unit + i * (tile // unit)) * unit

    per = 2 if paired else 1
    width = own.shape[1]
    fixed = pl.BlockSpec(terms.shape, lambda i: (0, 0))
    at_rows = pl.BlockSpec((pl.Element(tile), pl.Element(eigs)), lambda i: (row_of(i), 0))
    in_specs = [
        at_rows,
        fixed,
        pl.BlockSpec(
            (pl.Element(per * tile), pl.Element(width)), lambda i: (per * row_of(i), 0)
        ),
    ]
    in_specs += [pl.BlockSpec((per * tile, width), lambda i: (i, 0)) for _ in received]
    operands = [vectors, terms, own, *received]
    aliases = {}
    if previous is not None:
        aliases = {len(operands): 0}
        operands.append(previous)
        in_specs.append(pl.BlockSpec(memory_space=pl.ANY))

    operands += ties
    in_specs += [pl.BlockSpec(memory_space=pl.ANY)] * len(ties)

    def body(*refs):
        vectors_kernel(1 + len(received), paired, refs)

    return pl.pallas_call(
        body,
        out_shape=jax.ShapeDtypeStruct((rows, eigs), jnp.float32),
        grid=(steps,),
        in_specs=in_specs,
        out_specs=at_rows,
        input_output_aliases=aliases,
        compiler_params=pltpu.CompilerParams(vmem_limit_bytes=VMEM_BYTES),
        cost_estimate=pl.CostEstimate(
            flops=2 * span * terms.size,
            bytes_accessed=12 * span * eigs,
            transcendentals=0,
        ),
        name="add_chunk",
    )(*operands)


def choose(flag, kept, arrived, ties):
    def body(flag_ref, kept_ref, arrived_ref, *refs):
        refs[-1][...] = jnp.where(flag_ref[0] != 0, kept_ref[...], arrived_ref[...])

    vmem = pl.BlockSpec(memory_space=pltpu.VMEM)
    return pl.pallas_call(
        body,
        out_shape=jax.ShapeDtypeStruct(kept.shape, kept.dtype),
        in_specs=[pl.BlockSpec(memory_space=pltpu.SMEM), vmem, vmem]
        + [pl.BlockSpec(memory_space=pl.ANY)] * len(ties),
        out_specs=vmem,
        compiler_params=pltpu.CompilerParams(vmem_limit_bytes=SMALL_VMEM_BYTES),
        cost_estimate=pl.CostEstimate(flops=10**5, bytes_accessed=10**5, transcendentals=0),
        name="choose",
    )(flag.astype(jnp.int32)[None], kept, arrived, *ties)


def spread(block, me, owner, axis, size, ties):
    half, quarter = block.shape[0] // 2, block.shape[0] // 4
    core, side = me & 1, (me >> 1) & 1
    if size & (size - 1) or size < 4:
        block = lax.psum(jnp.where(me == owner, block, jnp.zeros_like(block)), axis)
        places = [(core, side), (core, 1 - side), (1 - core, side), (1 - core, 1 - side)]
        return [
            lax.dynamic_slice_in_dim(block, (2 * first + second) * quarter, quarter, 0)
            for first, second in places
        ]

    def exchange(value, bit):
        return lax.ppermute(value, axis, [(i, i ^ bit) for i in range(size)])

    def halves(value, bit):
        middle = value.shape[0] // 2
        first, second = value[:middle], value[middle:]
        return jnp.where(bit == 0, first, second), jnp.where(bit == 0, second, first)

    apart = me ^ owner
    kept, given = halves(block, core)
    kept = jnp.where(apart == 0, kept, exchange(given, 1))
    kept, given = halves(kept, side)
    kept = choose(apart < 2, kept, exchange(given, 2), ties)
    bit = 4
    while bit < size:
        kept = jnp.where(apart < bit, kept, exchange(kept, bit))
        bit *= 2
    beside = exchange(kept, 2)
    return [kept, beside, exchange(kept, 1), exchange(beside, 1)]


def on_device(
    row_size,
    col_size,
    right_sides,
    pencil_s,
    pencil_t,
    value_alpha,
    value_beta,
    selected,
    block_slot,
    right_basis,
    vectors,
):
    block = pencil_s.shape[1] // 2
    slot_count = right_sides.shape[0] // block
    block_count = block_slot.shape[0]
    rows, _, width = right_basis.shape
    me_row = lax.axis_index("row")
    me_col = lax.axis_index("col")
    slot_upper = block_slot[block_count - 2]
    slot_lower = block_slot[block_count - 1]

    paired = width % 128 == 0
    own = right_basis.reshape((2 * rows, width) if paired else (rows, 2 * width))
    per = own.shape[0] // rows
    bounds, start = [], 0
    for parts in SHARES:
        span = rows * parts // sum(SHARES)
        bounds.append((start, span))
        start += span
    local = [(per * start, per * span) for start, span in bounds]

    def fetch(piece):
        return [
            lax.ppermute(piece, "col", [(i, (i + step) % col_size) for i in range(col_size)])
            for step in range(1, col_size)
        ]

    seed = fetch(own[: local[0][1]])
    lane = jnp.stack(
        [me_row & 1, (me_row >> 1) & 1]
        + [lax.rem(me_col + (col_size - step), col_size) for step in range(col_size)]
    )
    lower, alpha, beta, *pieces = solve_lower(
        *[block_slot, pencil_s, pencil_t, right_sides, value_alpha, value_beta, selected],
        *[own, local[1:]],
    )
    received = [seed] + [fetch(piece) for piece in pieces]
    lower = spread(lower, me_row, lax.div(slot_lower, slot_count), "row", row_size, received[0])
    upper, lower = solve_upper(
        block_slot, lane, pencil_s, pencil_t, right_sides, alpha, beta, lower
    )
    upper = spread(upper, me_row, lax.div(slot_upper, slot_count), "row", row_size, received[1])
    upper, terms = order_rows(lane, upper, lower)
    updated_sides = update_sides(
        block_slot, me_row[None], right_sides, pencil_s, pencil_t, alpha, beta, upper, lower
    )
    updated_vectors = None
    for index, ((start, span), arrived) in enumerate(zip(bounds, received)):
        ties = [updated_sides] if index == SIDES_BEFORE else []
        updated_vectors = add_chunk(
            start, span, vectors, terms, own, arrived, paired, updated_vectors, ties
        )
    return (updated_sides, updated_vectors)


def solution(mesh):
    body = functools.partial(on_device, mesh.shape["row"], mesh.shape["col"])
    return jax.shard_map(
        body,
        mesh=mesh,
        in_specs=(
            P("row", "col"),
            P("row", None),
            P("row", None),
            P(),
            P(),
            P("col"),
            P(),
            P("row", None, "col"),
            P("row", "col"),
        ),
        out_specs=(P("row", "col"), P("row", "col")),
        check_vma=False,
    )
```

```python
import functools
import math

import jax
import jax.numpy as jnp
from jax import lax
from jax.experimental import pallas as pl
from jax.experimental.pallas import tpu as pltpu
from jax.sharding import PartitionSpec as P

SUB = 32
GROUP = 8
VMEM_BYTES = 32 * 1024 * 1024
MOST_VMEM_BYTES = 58 * 1024 * 1024
SMALL_VMEM_BYTES = 12 * 1024 * 1024
SHARES = (10, 18, 4)
SIDES_BEFORE = 2
TILE = 512
LIGHT = pl.CostEstimate(flops=1000, bytes_accessed=1000, transcendentals=0)


def exact_dot(left, right):
    return jnp.dot(left, right, precision=lax.Precision.HIGHEST, preferred_element_type=jnp.float32)


def split_two(value):
    high = value.astype(jnp.bfloat16)
    low = (value - high.astype(jnp.float32)).astype(jnp.bfloat16)
    return high, low


def split_three(value):
    high = value.astype(jnp.bfloat16)
    rest = value - high.astype(jnp.float32)
    middle = rest.astype(jnp.bfloat16)
    low = (rest - middle.astype(jnp.float32)).astype(jnp.bfloat16)
    return high, middle, low


def stacked_dot(left, right):
    high, middle, low = split_three(left)
    top, mid, end = split_three(right)
    return jnp.dot(
        jnp.concatenate([high, middle, high, middle, high, low], axis=1),
        jnp.concatenate([top, top, mid, mid, end, top], axis=0),
        preferred_element_type=jnp.float32,
    )


def table_lookup(selected, table):
    table_rows, lanes = table.shape
    lane = lax.broadcasted_iota(jnp.int32, (lanes, selected.shape[1]), 0)
    in_lane = jnp.where(lane == selected % lanes, 1.0, 0.0)
    candidates = exact_dot(table, in_lane)
    row = lax.broadcasted_iota(jnp.int32, candidates.shape, 0)
    return jnp.sum(jnp.where(row == selected // lanes, candidates, 0.0), axis=0, keepdims=True)


def back_substitute(s_ref, t_ref, alpha, beta, pending_ref, x_ref, midway=None):
    size = x_ref.shape[0]
    rows = lax.broadcasted_iota(jnp.int32, (SUB, SUB), 0)
    cols = lax.broadcasted_iota(jnp.int32, (SUB, SUB), 1)
    groups = SUB // GROUP
    for first in range(size - SUB, -1, -SUB):
        if midway is not None and first == size // 2 - SUB:
            midway()
        s_small = s_ref[first : first + SUB, first : first + SUB]
        t_small = t_ref[first : first + SUB, first : first + SUB]
        s_diag = jnp.sum(jnp.where(rows == cols, s_small, 0.0), axis=1, keepdims=True)
        t_diag = jnp.sum(jnp.where(rows == cols, t_small, 0.0), axis=1, keepdims=True)
        inverse = 1.0 / (beta * s_diag - alpha * t_diag)
        s_strict = jnp.where(rows < cols, s_small, 0.0)
        t_strict = jnp.where(rows < cols, t_small, 0.0)
        pending = [
            pending_ref[first + g * GROUP : first + (g + 1) * GROUP, :] for g in range(groups)
        ]
        for column in range(SUB - 1, -1, -1):
            own, row = divmod(column, GROUP)
            right = pending[own][row : row + 1, :]
            reciprocal = inverse[column : column + 1, :]
            x_ref[first + column : first + column + 1, :] = right * reciprocal
            scaled_beta = beta * reciprocal
            scaled_alpha = alpha * reciprocal
            for g in range(own + 1):
                span = slice(g * GROUP, (g + 1) * GROUP)
                factor = (
                    s_strict[span, column : column + 1] * scaled_beta
                    - t_strict[span, column : column + 1] * scaled_alpha
                )
                pending[g] = pending[g] - factor * right
        if first:
            block = x_ref[first : first + SUB, :]
            columns = slice(first, first + SUB)
            pending_ref[:first, :] = pending_ref[:first, :] - stacked_dot(
                jnp.concatenate([s_ref[:first, columns], t_ref[:first, columns]], axis=1),
                jnp.concatenate([beta * block, -alpha * block], axis=0),
            )


def put_together(core, side, piece_refs, whole_ref):
    quarter = whole_ref.shape[0] // 4
    places = [(core, side), (core, 1 - side), (1 - core, side), (1 - core, 1 - side)]
    for ref, (half, part) in zip(piece_refs, places):
        start = (2 * half + part) * quarter
        whole_ref[pl.ds(pl.multiple_of(start, quarter), quarter), :] = ref[...]


def hand_out(core, x_ref, kept_ref, given_ref):
    half = kept_ref.shape[0]
    kept_ref[...] = x_ref[pl.ds(pl.multiple_of(core * half, half), half), :]
    given_ref[...] = x_ref[pl.ds(pl.multiple_of((1 - core) * half, half), half), :]


def lower_kernel(bounds, slots, lane, s_ref, t_ref, r_ref, values_a, values_b, selected, own_ref, *refs):
    kept_ref, given_ref, alpha_ref, beta_ref, s_band, t_band, r_band = refs[:7]
    chunk_refs, held_refs = refs[7 : 7 + len(bounds)], refs[7 + len(bounds) : 7 + 2 * len(bounds)]
    s_corner, t_corner, pending_ref, x_ref, table_a, table_b, chosen, done, moved = refs[7 + 2 * len(bounds) :]
    block = x_ref.shape[0]
    count, total = r_ref.shape[0] // block, slots.shape[0]

    def rows_of(slot):
        return pl.ds(pl.multiple_of(lax.rem(slots[slot], count) * block, block), block)

    low, high = rows_of(total - 1), rows_of(total - 2)
    first = [
        (values_a, table_a),
        (values_b, table_b),
        (selected, chosen),
        (s_ref.at[low, block:], s_corner),
        (t_ref.at[low, block:], t_corner),
        (r_ref.at[low], pending_ref),
        (s_ref.at[high], s_band),
        (t_ref.at[high], t_band),
        (r_ref.at[high], r_band),
    ]
    loads = [pltpu.make_async_copy(a, b, done.at[index]) for index, (a, b) in enumerate(first)]
    inward, outward = [], []
    for index, (start, span) in enumerate(bounds):
        held, chunk = held_refs[index], chunk_refs[index]
        inward.append(pltpu.make_async_copy(own_ref.at[pl.ds(start, span)], held, moved.at[0, index]))
        outward.append(pltpu.make_async_copy(held, chunk, moved.at[1, index]))
    for copy in loads + inward:
        copy.start()
    for copy in loads[:3]:
        copy.wait()
    alpha = table_lookup(chosen[...], table_a[...])
    beta = table_lookup(chosen[...], table_b[...])
    alpha_ref[...] = alpha
    beta_ref[...] = beta
    for copy in loads[3:6]:
        copy.wait()

    def hand_on():
        for arrive, leave in zip(inward, outward):
            arrive.wait()
            leave.start()

    back_substitute(s_corner, t_corner, alpha, beta, pending_ref, x_ref, hand_on)
    hand_out(lane[0], x_ref, kept_ref, given_ref)
    for copy in loads[6:] + outward:
        copy.wait()


def upper_kernel(lane, s_ref, t_ref, r_ref, alpha_ref, beta_ref, *refs):
    piece_refs, (kept_ref, given_ref, lower_ref, pending_ref, x_ref) = refs[:4], refs[4:]
    block = x_ref.shape[0]
    alpha, beta = alpha_ref[...], beta_ref[...]
    put_together(lane[0], lane[1], piece_refs, lower_ref)
    lower = lower_ref[...]
    pending_ref[...] = r_ref[...] - (
        exact_dot(s_ref[:, block:], beta * lower) - exact_dot(t_ref[:, block:], alpha * lower)
    )
    back_substitute(s_ref, t_ref, alpha, beta, pending_ref, x_ref)
    hand_out(lane[0], x_ref, kept_ref, given_ref)


def solve_lower(slots, lane, pencil_s, pencil_t, sides, value_alpha, value_beta, selected, own, bounds):
    block, eigs = pencil_s.shape[1] // 2, sides.shape[1]
    lanes = 128 if value_alpha.shape[0] % 128 == 0 else value_alpha.shape[0]
    table_shape = (value_alpha.shape[0] // lanes, lanes)
    smem, vmem = pl.BlockSpec(memory_space=pltpu.SMEM), pl.BlockSpec(memory_space=pltpu.VMEM)
    hbm, anywhere = pl.BlockSpec(memory_space=pltpu.HBM), pl.BlockSpec(memory_space=pl.ANY)

    def floats(*shape):
        return jax.ShapeDtypeStruct(shape, jnp.float32)

    chunks = [floats(span, own.shape[1]) for _, span in bounds]
    return pl.pallas_call(
        functools.partial(lower_kernel, bounds),
        out_shape=(
            *[floats(block // 2, eigs)] * 2,
            *[floats(1, eigs)] * 2,
            *[floats(block, 2 * block)] * 2,
            floats(block, eigs),
            *chunks,
        ),
        in_specs=[smem] * 2 + [hbm] * 7,
        out_specs=(*[vmem] * 7, *[anywhere] * len(bounds)),
        scratch_shapes=[
            *[pltpu.VMEM(chunk.shape, jnp.float32) for chunk in chunks],
            *[pltpu.VMEM((block, block), jnp.float32)] * 2,
            *[pltpu.VMEM((block, eigs), jnp.float32)] * 2,
            *[pltpu.VMEM(table_shape, jnp.float32)] * 2,
            pltpu.VMEM((1, eigs), jnp.int32),
            pltpu.SemaphoreType.DMA((9,)),
            pltpu.SemaphoreType.DMA((2, len(bounds))),
        ],
        compiler_params=pltpu.CompilerParams(vmem_limit_bytes=MOST_VMEM_BYTES),
        cost_estimate=LIGHT,
        name="solve_lower",
    )(
        slots,
        lane,
        pencil_s,
        pencil_t,
        sides,
        value_alpha.reshape(table_shape),
        value_beta.reshape(table_shape),
        selected[None, :],
        own,
    )


def solve_upper(lane, s_band, t_band, r_band, alpha, beta, pieces):
    block, eigs = r_band.shape
    smem, vmem = pl.BlockSpec(memory_space=pltpu.SMEM), pl.BlockSpec(memory_space=pltpu.VMEM)
    half = jax.ShapeDtypeStruct((block // 2, eigs), jnp.float32)
    return pl.pallas_call(
        upper_kernel,
        out_shape=(half, half, jax.ShapeDtypeStruct((block, eigs), jnp.float32)),
        in_specs=[smem] + [vmem] * (5 + len(pieces)),
        out_specs=(vmem,) * 3,
        scratch_shapes=[pltpu.VMEM((block, eigs), jnp.float32)] * 2,
        compiler_params=pltpu.CompilerParams(vmem_limit_bytes=SMALL_VMEM_BYTES),
        cost_estimate=LIGHT,
        name="solve_upper",
    )(lane, s_band, t_band, r_band, alpha, beta, *pieces)


def order_kernel(lane, *refs):
    piece_refs, (lower_ref, upper_ref, terms_ref) = refs[:4], refs[4:]
    put_together(lane[0], lane[1], piece_refs, upper_ref)
    block = upper_ref.shape[0]
    parts = lane.shape[0] - 2
    width = block // parts
    for part in range(parts):
        rows = pl.ds(pl.multiple_of(lane[2 + part] * width, width), width)
        for half, source in enumerate((upper_ref, lower_ref)):
            target = (2 * part + half) * width
            high, low = split_two(source[rows, :])
            for term, value in enumerate((high, high, low)):
                first = 2 * block * term + target
                terms_ref[first : first + width, :] = value


def order_rows(lane, pieces, lower):
    block, eigs = lower.shape
    vmem = pl.BlockSpec(memory_space=pltpu.VMEM)
    return pl.pallas_call(
        order_kernel,
        out_shape=(
            jax.ShapeDtypeStruct((block, eigs), jnp.float32),
            jax.ShapeDtypeStruct((6 * block, eigs), jnp.bfloat16),
        ),
        in_specs=[pl.BlockSpec(memory_space=pltpu.SMEM)] + [vmem] * (len(pieces) + 1),
        out_specs=(vmem, vmem),
        compiler_params=pltpu.CompilerParams(vmem_limit_bytes=SMALL_VMEM_BYTES),
        cost_estimate=LIGHT,
        name="order_rows",
    )(lane, *pieces, lower)


def near_dot(left, right_terms):
    high, low = split_two(left)
    return jnp.dot(
        jnp.concatenate([high, low, high], axis=1), right_terms, preferred_element_type=jnp.float32
    )


def three_terms(right):
    high, low = split_two(right)
    return jnp.concatenate([high, high, low], axis=0)


def sides_kernel(slots, me, r_ref, s_ref, t_ref, alpha_ref, beta_ref, upper_ref, lower_ref, out_ref):
    block = upper_ref.shape[0]
    count = out_ref.shape[0] // block
    base = me[0] * count
    alpha, beta = alpha_ref[...], beta_ref[...]
    upper, lower = upper_ref[...], lower_ref[...]
    x = jnp.concatenate([upper, lower], axis=0)
    update = near_dot(s_ref[...], three_terms(beta * x)) - near_dot(t_ref[...], three_terms(alpha * x))
    for slot in range(count):
        span = slice(slot * block, (slot + 1) * block)
        fresh = r_ref[span, :] - update[span, :]
        fresh = jnp.where(slots[slots.shape[0] - 2] == base + slot, upper, fresh)
        out_ref[span, :] = jnp.where(slots[slots.shape[0] - 1] == base + slot, lower, fresh)


def update_sides(slots, me, sides, pencil_s, pencil_t, alpha, beta, upper, lower):
    smem, vmem = pl.BlockSpec(memory_space=pltpu.SMEM), pl.BlockSpec(memory_space=pltpu.VMEM)
    return pl.pallas_call(
        sides_kernel,
        out_shape=jax.ShapeDtypeStruct(sides.shape, jnp.float32),
        in_specs=[smem] * 2 + [vmem] * 7,
        out_specs=vmem,
        compiler_params=pltpu.CompilerParams(vmem_limit_bytes=VMEM_BYTES),
        cost_estimate=LIGHT,
        name="update_sides",
    )(slots, me, sides, pencil_s, pencil_t, alpha, beta, upper, lower)


def vectors_kernel(parts, paired, refs):
    vectors_ref, terms_ref = refs[:2]
    part_refs = refs[2 : 2 + parts]
    out_ref = refs[-1]
    tile = out_ref.shape[0]
    pieces = []
    for ref in part_refs:
        if paired:
            pieces.append(ref[pl.ds(0, tile, 2), :])
            pieces.append(ref[pl.ds(1, tile, 2), :])
        else:
            pieces.append(ref[...])
    basis = jnp.concatenate(pieces, axis=1)
    out_ref[...] = vectors_ref[...] + near_dot(basis, terms_ref[...])


def add_chunk(start, span, vectors, terms, own, received, paired, previous, ties):
    rows, eigs = vectors.shape
    tile = span
    while tile > TILE:
        tile //= 2
    steps = span // tile
    unit = math.gcd(start, tile)

    def row_of(i):
        return (start // unit + i * (tile // unit)) * unit

    per = 2 if paired else 1
    width = own.shape[1]
    fixed = pl.BlockSpec(memory_space=pltpu.VMEM)
    at_rows = pl.BlockSpec((pl.Element(tile), pl.Element(eigs)), lambda i: (row_of(i), 0))
    in_specs = [
        at_rows,
        fixed,
        pl.BlockSpec(
            (pl.Element(per * tile), pl.Element(width)), lambda i: (per * row_of(i), 0)
        ),
    ]
    in_specs += [pl.BlockSpec((per * tile, width), lambda i: (i, 0)) for _ in received]
    operands = [vectors, terms, own, *received]
    aliases = {}
    if previous is not None:
        aliases = {len(operands): 0}
        operands.append(previous)
        in_specs.append(pl.BlockSpec(memory_space=pl.ANY))

    operands += ties
    in_specs += [pl.BlockSpec(memory_space=pl.ANY)] * len(ties)

    def body(*refs):
        vectors_kernel(1 + len(received), paired, refs)

    return pl.pallas_call(
        body,
        out_shape=jax.ShapeDtypeStruct((rows, eigs), jnp.float32),
        grid=(steps,),
        in_specs=in_specs,
        out_specs=at_rows,
        input_output_aliases=aliases,
        compiler_params=pltpu.CompilerParams(vmem_limit_bytes=VMEM_BYTES),
        cost_estimate=LIGHT,
        name="add_chunk",
    )(*operands)


def choose(flag, kept, arrived, ties):
    def body(flag_ref, kept_ref, arrived_ref, *refs):
        refs[-1][...] = jnp.where(flag_ref[0] != 0, kept_ref[...], arrived_ref[...])

    vmem = pl.BlockSpec(memory_space=pltpu.VMEM)
    return pl.pallas_call(
        body,
        out_shape=jax.ShapeDtypeStruct(kept.shape, kept.dtype),
        in_specs=[pl.BlockSpec(memory_space=pltpu.SMEM), vmem, vmem]
        + [pl.BlockSpec(memory_space=pl.ANY)] * len(ties),
        out_specs=vmem,
        compiler_params=pltpu.CompilerParams(vmem_limit_bytes=SMALL_VMEM_BYTES),
        cost_estimate=LIGHT,
        name="choose",
    )(flag.astype(jnp.int32)[None], kept, arrived, *ties)


def spread(kept, given, me, owner, axis, size, ties):
    core, side = me & 1, (me >> 1) & 1
    if size & (size - 1) or size < 4:
        parts = [jnp.where(core == 0, kept, given), jnp.where(core == 0, given, kept)]
        block = jnp.concatenate(parts, axis=0)
        block = lax.psum(jnp.where(me == owner, block, jnp.zeros_like(block)), axis)
        quarter = block.shape[0] // 4
        places = [(core, side), (core, 1 - side), (1 - core, side), (1 - core, 1 - side)]
        return [
            lax.dynamic_slice_in_dim(block, (2 * first + second) * quarter, quarter, 0)
            for first, second in places
        ]

    def exchange(value, bit):
        return lax.ppermute(value, axis, [(i, i ^ bit) for i in range(size)])

    apart = me ^ owner
    kept = jnp.where(apart == 0, kept, exchange(given, 1))
    middle = kept.shape[0] // 2
    first, second = kept[:middle], kept[middle:]
    kept, given = jnp.where(side == 0, first, second), jnp.where(side == 0, second, first)
    kept = jnp.where(apart < 2, kept, exchange(given, 2))
    bit = 4
    while bit < size:
        if bit == 4 and ties:
            kept = choose(apart < bit, kept, exchange(kept, bit), ties)
        else:
            kept = jnp.where(apart < bit, kept, exchange(kept, bit))
        bit *= 2
    beside = exchange(kept, 2)
    return [kept, beside, exchange(kept, 1), exchange(beside, 1)]


def on_device(
    row_size,
    col_size,
    right_sides,
    pencil_s,
    pencil_t,
    value_alpha,
    value_beta,
    selected,
    block_slot,
    right_basis,
    vectors,
):
    block = pencil_s.shape[1] // 2
    slot_count = right_sides.shape[0] // block
    block_count = block_slot.shape[0]
    rows, _, width = right_basis.shape
    me_row = lax.axis_index("row")
    me_col = lax.axis_index("col")
    slot_upper = block_slot[block_count - 2]
    slot_lower = block_slot[block_count - 1]

    paired = width % 128 == 0
    own = right_basis.reshape((2 * rows, width) if paired else (rows, 2 * width))
    per = own.shape[0] // rows
    bounds, start = [], 0
    for parts in SHARES:
        span = rows * parts // sum(SHARES)
        bounds.append((start, span))
        start += span
    local = [(per * start, per * span) for start, span in bounds]

    def fetch(piece):
        return [
            lax.ppermute(piece, "col", [(i, (i + step) % col_size) for i in range(col_size)])
            for step in range(1, col_size)
        ]

    seed = fetch(own[: local[0][1]])
    lane = jnp.stack(
        [me_row & 1, (me_row >> 1) & 1]
        + [lax.rem(me_col + (col_size - step), col_size) for step in range(col_size)]
    )
    kept, given, alpha, beta, s_band, t_band, r_band, *pieces = solve_lower(
        *[block_slot, lane, pencil_s, pencil_t, right_sides, value_alpha, value_beta, selected],
        *[own, local[1:]],
    )
    received = [seed] + [fetch(piece) for piece in pieces]
    owner_lower, owner_upper = lax.div(slot_lower, slot_count), lax.div(slot_upper, slot_count)
    lower = spread(kept, given, me_row, owner_lower, "row", row_size, seed)
    kept, given, lower = solve_upper(lane, s_band, t_band, r_band, alpha, beta, lower)
    upper = spread(kept, given, me_row, owner_upper, "row", row_size, [])
    upper, terms = order_rows(lane, upper, lower)
    updated_sides = update_sides(
        block_slot, me_row[None], right_sides, pencil_s, pencil_t, alpha, beta, upper, lower
    )
    updated_vectors = None
    for index, ((start, span), arrived) in enumerate(zip(bounds, received)):
        ties = [updated_sides] if index == SIDES_BEFORE else []
        updated_vectors = add_chunk(
            start, span, vectors, terms, own, arrived, paired, updated_vectors, ties
        )
    return (updated_sides, updated_vectors)


def solution(mesh):
    body = functools.partial(on_device, mesh.shape["row"], mesh.shape["col"])
    return jax.shard_map(
        body,
        mesh=mesh,
        in_specs=(
            P("row", "col"),
            P("row", None),
            P("row", None),
            P(),
            P(),
            P("col"),
            P(),
            P("row", None, "col"),
            P("row", "col"),
        ),
        out_specs=(P("row", "col"), P("row", "col")),
        check_vma=False,
    )
```

```python
import functools
import math

import jax
import jax.numpy as jnp
from jax import lax
from jax.experimental import pallas as pl
from jax.experimental.pallas import tpu as pltpu
from jax.sharding import PartitionSpec as P

SUB = 32
GROUP = 8
VMEM_BYTES = 48 * 1024 * 1024
FULL_VMEM_BYTES = 59 * 1024 * 1024
SMALL_VMEM_BYTES = 12 * 1024 * 1024
TILE = 512
LIGHT = pl.CostEstimate(flops=1000, bytes_accessed=1000, transcendentals=0)


def exact_dot(left, right):
    return jnp.dot(left, right, precision=lax.Precision.HIGHEST, preferred_element_type=jnp.float32)


def split_two(value):
    high = value.astype(jnp.bfloat16)
    low = (value - high.astype(jnp.float32)).astype(jnp.bfloat16)
    return high, low


def split_three(value):
    high = value.astype(jnp.bfloat16)
    rest = value - high.astype(jnp.float32)
    middle = rest.astype(jnp.bfloat16)
    low = (rest - middle.astype(jnp.float32)).astype(jnp.bfloat16)
    return high, middle, low


def stacked_dot(left, right):
    high, middle, low = split_three(left)
    top, mid, end = split_three(right)
    return jnp.dot(
        jnp.concatenate([high, middle, high, middle, high, low], axis=1),
        jnp.concatenate([top, top, mid, mid, end, top], axis=0),
        preferred_element_type=jnp.float32,
    )


def table_lookup(selected, table):
    table_rows, lanes = table.shape
    lane = lax.broadcasted_iota(jnp.int32, (lanes, selected.shape[1]), 0)
    in_lane = jnp.where(lane == selected % lanes, 1.0, 0.0)
    candidates = exact_dot(table, in_lane)
    row = lax.broadcasted_iota(jnp.int32, candidates.shape, 0)
    return jnp.sum(jnp.where(row == selected // lanes, candidates, 0.0), axis=0, keepdims=True)


def back_substitute(s_ref, t_ref, alpha, beta, pending_ref, x_ref):
    size = x_ref.shape[0]
    rows = lax.broadcasted_iota(jnp.int32, (SUB, SUB), 0)
    cols = lax.broadcasted_iota(jnp.int32, (SUB, SUB), 1)
    groups = SUB // GROUP
    for first in range(size - SUB, -1, -SUB):
        s_small = s_ref[first : first + SUB, first : first + SUB]
        t_small = t_ref[first : first + SUB, first : first + SUB]
        s_diag = jnp.sum(jnp.where(rows == cols, s_small, 0.0), axis=1, keepdims=True)
        t_diag = jnp.sum(jnp.where(rows == cols, t_small, 0.0), axis=1, keepdims=True)
        inverse = 1.0 / (beta * s_diag - alpha * t_diag)
        s_strict = jnp.where(rows < cols, s_small, 0.0)
        t_strict = jnp.where(rows < cols, t_small, 0.0)
        pending = [
            pending_ref[first + g * GROUP : first + (g + 1) * GROUP, :] for g in range(groups)
        ]
        for column in range(SUB - 1, -1, -1):
            own, row = divmod(column, GROUP)
            right = pending[own][row : row + 1, :]
            reciprocal = inverse[column : column + 1, :]
            x_ref[first + column : first + column + 1, :] = right * reciprocal
            scaled_beta = beta * reciprocal
            scaled_alpha = alpha * reciprocal
            for g in range(own + 1):
                span = slice(g * GROUP, (g + 1) * GROUP)
                factor = (
                    s_strict[span, column : column + 1] * scaled_beta
                    - t_strict[span, column : column + 1] * scaled_alpha
                )
                pending[g] = pending[g] - factor * right
        if first:
            block = x_ref[first : first + SUB, :]
            columns = slice(first, first + SUB)
            pending_ref[:first, :] = pending_ref[:first, :] - stacked_dot(
                jnp.concatenate([s_ref[:first, columns], t_ref[:first, columns]], axis=1),
                jnp.concatenate([beta * block, -alpha * block], axis=0),
            )


def put_together(core, side, piece_refs, whole_ref):
    quarter = whole_ref.shape[0] // 4
    places = [(core, side), (core, 1 - side), (1 - core, side), (1 - core, 1 - side)]
    for ref, (half, part) in zip(piece_refs, places):
        start = (2 * half + part) * quarter
        whole_ref[pl.ds(pl.multiple_of(start, quarter), quarter), :] = ref[...]


def lower_kernel(
    slots, s_ref, t_ref, r_ref, values_a, values_b, selected, x_ref, alpha_ref, beta_ref, pending_ref
):
    alpha = table_lookup(selected[...], values_a[...])
    beta = table_lookup(selected[...], values_b[...])
    alpha_ref[...] = alpha
    beta_ref[...] = beta
    pending_ref[...] = r_ref[...]
    back_substitute(s_ref, t_ref, alpha, beta, pending_ref, x_ref)


def upper_kernel(slots, lane, s_ref, t_ref, r_ref, alpha_ref, beta_ref, *refs):
    piece_refs, (x_ref, lower_ref, pending_ref) = refs[:4], refs[-3:]
    block = x_ref.shape[0]
    alpha, beta = alpha_ref[...], beta_ref[...]
    put_together(lane[0], lane[1], piece_refs, lower_ref)
    lower = lower_ref[...]
    pending_ref[...] = r_ref[...] - (
        exact_dot(s_ref[:, block:], beta * lower) - exact_dot(t_ref[:, block:], alpha * lower)
    )
    back_substitute(s_ref, t_ref, alpha, beta, pending_ref, x_ref)


def solve_lower(slots, pencil_s, pencil_t, sides, value_alpha, value_beta, selected):
    block, eigs = pencil_s.shape[1] // 2, sides.shape[1]
    count, last = sides.shape[0] // block, slots.shape[0] - 1
    lanes = 128 if value_alpha.shape[0] % 128 == 0 else value_alpha.shape[0]
    table_shape = (value_alpha.shape[0] // lanes, lanes)
    corner = pl.BlockSpec((block, block), lambda i, slots: (lax.rem(slots[last], count), 1))
    whole = pl.BlockSpec((block, eigs), lambda i, slots: (lax.rem(slots[last], count), 0))
    line = pl.BlockSpec((1, eigs), lambda i, slots: (0, 0))
    table = pl.BlockSpec(table_shape, lambda i, slots: (0, 0))
    return pl.pallas_call(
        lower_kernel,
        out_shape=(
            jax.ShapeDtypeStruct((block, eigs), jnp.float32),
            jax.ShapeDtypeStruct((1, eigs), jnp.float32),
            jax.ShapeDtypeStruct((1, eigs), jnp.float32),
        ),
        grid_spec=pltpu.PrefetchScalarGridSpec(
            num_scalar_prefetch=1,
            grid=(1,),
            in_specs=[corner, corner, whole, table, table, line],
            out_specs=(
                pl.BlockSpec((block, eigs), lambda i, slots: (0, 0)),
                line,
                line,
            ),
            scratch_shapes=[
                pltpu.VMEM((block, eigs), jnp.float32),
            ],
        ),
        compiler_params=pltpu.CompilerParams(vmem_limit_bytes=FULL_VMEM_BYTES),
        cost_estimate=LIGHT,
        name="solve_lower",
    )(
        slots,
        pencil_s,
        pencil_t,
        sides,
        value_alpha.reshape(table_shape),
        value_beta.reshape(table_shape),
        selected[None, :],
    )


def solve_upper(slots, lane, pencil_s, pencil_t, sides, alpha, beta, pieces):
    block, eigs = pencil_s.shape[1] // 2, sides.shape[1]
    count, index = sides.shape[0] // block, slots.shape[0] - 2
    band = pl.BlockSpec((block, 2 * block), lambda i, slots, lane: (lax.rem(slots[index], count), 0))
    whole = pl.BlockSpec((block, eigs), lambda i, slots, lane: (lax.rem(slots[index], count), 0))
    line = pl.BlockSpec((1, eigs), lambda i, slots, lane: (0, 0))
    fixed = [pl.BlockSpec(piece.shape, lambda i, slots, lane: (0, 0)) for piece in pieces]
    return pl.pallas_call(
        upper_kernel,
        out_shape=(jax.ShapeDtypeStruct((block, eigs), jnp.float32),) * 2,
        grid_spec=pltpu.PrefetchScalarGridSpec(
            num_scalar_prefetch=2,
            grid=(1,),
            in_specs=[band, band, whole, line, line, *fixed],
            out_specs=(pl.BlockSpec((block, eigs), lambda i, slots, lane: (0, 0)),) * 2,
            scratch_shapes=[pltpu.VMEM((block, eigs), jnp.float32)],
        ),
        compiler_params=pltpu.CompilerParams(vmem_limit_bytes=FULL_VMEM_BYTES),
        cost_estimate=LIGHT,
        name="solve_upper",
    )(slots, lane, pencil_s, pencil_t, sides, alpha, beta, *pieces)


def order_kernel(lane, *refs):
    piece_refs, (lower_ref, upper_ref, own_ref, others_ref) = refs[:4], refs[4:]
    put_together(lane[0], lane[1], piece_refs, upper_ref)
    block = upper_ref.shape[0]
    width = block // (lane.shape[0] - 2)
    for part in range(lane.shape[0] - 2):
        rows = pl.ds(pl.multiple_of(lane[2 + part] * width, width), width)
        terms_ref = others_ref if part else own_ref
        for half, source in enumerate((upper_ref, lower_ref)):
            target = (2 * max(part - 1, 0) + half) * width
            high, low = split_two(source[rows, :])
            for term, value in enumerate((high, high, low)):
                first = terms_ref.shape[0] // 3 * term + target
                terms_ref[first : first + width, :] = value


def order_rows(lane, pieces, lower):
    block, eigs = lower.shape
    width = block // (lane.shape[0] - 2)
    vmem = pl.BlockSpec(memory_space=pltpu.VMEM)
    return pl.pallas_call(
        order_kernel,
        out_shape=(
            jax.ShapeDtypeStruct((block, eigs), jnp.float32),
            jax.ShapeDtypeStruct((6 * width, eigs), jnp.bfloat16),
            jax.ShapeDtypeStruct((6 * (block - width), eigs), jnp.bfloat16),
        ),
        in_specs=[pl.BlockSpec(memory_space=pltpu.SMEM)] + [vmem] * (len(pieces) + 1),
        out_specs=(vmem, vmem, vmem),
        compiler_params=pltpu.CompilerParams(vmem_limit_bytes=SMALL_VMEM_BYTES),
        cost_estimate=LIGHT,
        name="order_rows",
    )(lane, *pieces, lower)


def near_dot(left, right_terms):
    high, low = split_two(left)
    return jnp.dot(
        jnp.concatenate([high, low, high], axis=1), right_terms, preferred_element_type=jnp.float32
    )


def three_terms(right):
    high, low = split_two(right)
    return jnp.concatenate([high, high, low], axis=0)


def sides_kernel(slots, me, r_ref, s_ref, t_ref, alpha_ref, beta_ref, upper_ref, lower_ref, out_ref):
    block = upper_ref.shape[0]
    count = out_ref.shape[0] // block
    base = me[0] * count
    alpha, beta = alpha_ref[...], beta_ref[...]
    upper, lower = upper_ref[...], lower_ref[...]
    x = jnp.concatenate([upper, lower], axis=0)
    update = near_dot(s_ref[...], three_terms(beta * x)) - near_dot(t_ref[...], three_terms(alpha * x))
    for slot in range(count):
        span = slice(slot * block, (slot + 1) * block)
        fresh = r_ref[span, :] - update[span, :]
        fresh = jnp.where(slots[slots.shape[0] - 2] == base + slot, upper, fresh)
        out_ref[span, :] = jnp.where(slots[slots.shape[0] - 1] == base + slot, lower, fresh)


def update_sides(slots, me, sides, pencil_s, pencil_t, alpha, beta, upper, lower):
    smem, vmem = pl.BlockSpec(memory_space=pltpu.SMEM), pl.BlockSpec(memory_space=pltpu.VMEM)
    return pl.pallas_call(
        sides_kernel,
        out_shape=jax.ShapeDtypeStruct(sides.shape, jnp.float32),
        in_specs=[smem] * 2 + [vmem] * 7,
        out_specs=vmem,
        compiler_params=pltpu.CompilerParams(vmem_limit_bytes=FULL_VMEM_BYTES),
        cost_estimate=LIGHT,
        name="update_sides",
    )(slots, me, sides, pencil_s, pencil_t, alpha, beta, upper, lower)


def add_kernel(paired, base_ref, terms_ref, *refs):
    part_refs, out_ref = refs[: len(refs) - 1], refs[-1]
    tile = out_ref.shape[0]
    pieces = []
    for ref in part_refs:
        if paired:
            pieces.append(ref[pl.ds(0, tile, 2), :])
            pieces.append(ref[pl.ds(1, tile, 2), :])
        else:
            pieces.append(ref[...])
    basis = jnp.concatenate(pieces, axis=1)
    out_ref[...] = base_ref[...] + near_dot(basis, terms_ref[...])


def add_product(base, terms, parts, paired, name):
    rows, eigs = base.shape
    tile = math.gcd(TILE, rows)
    per, width = parts[0].shape[0] // rows, parts[0].shape[1]
    at_rows = pl.BlockSpec((tile, eigs), lambda i: (i, 0))
    return pl.pallas_call(
        functools.partial(add_kernel, paired),
        out_shape=jax.ShapeDtypeStruct((rows, eigs), jnp.float32),
        grid=(rows // tile,),
        in_specs=[at_rows, pl.BlockSpec(memory_space=pltpu.VMEM)]
        + [pl.BlockSpec((per * tile, width), lambda i: (i, 0)) for _ in parts],
        out_specs=at_rows,
        compiler_params=pltpu.CompilerParams(vmem_limit_bytes=VMEM_BYTES),
        cost_estimate=LIGHT,
        name=name,
    )(base, terms, *parts)


def spread(block, me, owner, axis, size):
    half, quarter = block.shape[0] // 2, block.shape[0] // 4
    core, side = me & 1, (me >> 1) & 1
    if size & (size - 1) or size < 4:
        block = lax.psum(jnp.where(me == owner, block, jnp.zeros_like(block)), axis)
        places = [(core, side), (core, 1 - side), (1 - core, side), (1 - core, 1 - side)]
        return [
            lax.dynamic_slice_in_dim(block, (2 * first + second) * quarter, quarter, 0)
            for first, second in places
        ]

    def exchange(value, bit):
        return lax.ppermute(value, axis, [(i, i ^ bit) for i in range(size)])

    def halves(value, bit):
        middle = value.shape[0] // 2
        first, second = value[:middle], value[middle:]
        return jnp.where(bit == 0, first, second), jnp.where(bit == 0, second, first)

    apart = me ^ owner
    kept, given = halves(block, core)
    kept = jnp.where(apart == 0, kept, exchange(given, 1))
    kept, given = halves(kept, side)
    kept = jnp.where(apart < 2, kept, exchange(given, 2))
    bit = 4
    while bit < size:
        kept = jnp.where(apart < bit, kept, exchange(kept, bit))
        bit *= 2
    return [kept] + [exchange(kept, bits) for bits in (2, 1, 3)]


def on_device(
    row_size,
    col_size,
    right_sides,
    pencil_s,
    pencil_t,
    value_alpha,
    value_beta,
    selected,
    block_slot,
    right_basis,
    vectors,
):
    block = pencil_s.shape[1] // 2
    slot_count = right_sides.shape[0] // block
    block_count = block_slot.shape[0]
    rows, _, width = right_basis.shape
    me_row = lax.axis_index("row")
    me_col = lax.axis_index("col")
    slot_upper = block_slot[block_count - 2]
    slot_lower = block_slot[block_count - 1]

    paired = width % 128 == 0
    own = right_basis.reshape((2 * rows, width) if paired else (rows, 2 * width))
    received = [
        lax.ppermute(own, "col", [(i, (i + step) % col_size) for i in range(col_size)])
        for step in range(1, col_size)
    ]
    lane = jnp.stack(
        [me_row & 1, (me_row >> 1) & 1]
        + [lax.rem(me_col + (col_size - step), col_size) for step in range(col_size)]
    )
    lower, alpha, beta = solve_lower(
        block_slot, pencil_s, pencil_t, right_sides, value_alpha, value_beta, selected
    )
    lower = spread(lower, me_row, lax.div(slot_lower, slot_count), "row", row_size)
    upper, lower = solve_upper(
        block_slot, lane, pencil_s, pencil_t, right_sides, alpha, beta, lower
    )
    upper = spread(upper, me_row, lax.div(slot_upper, slot_count), "row", row_size)
    upper, own_terms, other_terms = order_rows(lane, upper, lower)
    updated_vectors = add_product(vectors, own_terms, [own], paired, "add_own")
    updated_sides = update_sides(
        block_slot, me_row[None], right_sides, pencil_s, pencil_t, alpha, beta, upper, lower
    )
    if received:
        updated_vectors = add_product(
            updated_vectors, other_terms, received, paired, "add_received"
        )
    return (updated_sides, updated_vectors)


def solution(mesh):
    body = functools.partial(on_device, mesh.shape["row"], mesh.shape["col"])
    return jax.shard_map(
        body,
        mesh=mesh,
        in_specs=(
            P("row", "col"),
            P("row", None),
            P("row", None),
            P(),
            P(),
            P("col"),
            P(),
            P("row", None, "col"),
            P("row", "col"),
        ),
        out_specs=(P("row", "col"), P("row", "col")),
        check_vma=False,
    )
```

```python
import functools
import math

import jax
import jax.numpy as jnp
from jax import lax
from jax.experimental import pallas as pl
from jax.experimental.pallas import tpu as pltpu
from jax.sharding import PartitionSpec as P

SUB = 32
GROUP = 8
VMEM_BYTES = 57 * 1024 * 1024
ADD_VMEM_BYTES = 48 * 1024 * 1024
FULL_VMEM_BYTES = 59 * 1024 * 1024
TILE = 512
LIGHT = pl.CostEstimate(flops=1000, bytes_accessed=1000, transcendentals=0)


def exact_dot(left, right):
    return jnp.dot(left, right, precision=lax.Precision.HIGHEST, preferred_element_type=jnp.float32)


def split_two(value):
    high = value.astype(jnp.bfloat16)
    low = (value - high.astype(jnp.float32)).astype(jnp.bfloat16)
    return high, low


def split_three(value):
    high = value.astype(jnp.bfloat16)
    rest = value - high.astype(jnp.float32)
    middle = rest.astype(jnp.bfloat16)
    low = (rest - middle.astype(jnp.float32)).astype(jnp.bfloat16)
    return high, middle, low


def stacked_dot(left, right):
    high, middle, low = split_three(left)
    top, mid, end = split_three(right)
    return jnp.dot(
        jnp.concatenate([high, middle, high, middle, high, low], axis=1),
        jnp.concatenate([top, top, mid, mid, end, top], axis=0),
        preferred_element_type=jnp.float32,
    )


def table_lookup(selected, table):
    table_rows, lanes = table.shape
    lane = lax.broadcasted_iota(jnp.int32, (lanes, selected.shape[1]), 0)
    in_lane = jnp.where(lane == selected % lanes, 1.0, 0.0)
    candidates = exact_dot(table, in_lane)
    row = lax.broadcasted_iota(jnp.int32, candidates.shape, 0)
    return jnp.sum(jnp.where(row == selected // lanes, candidates, 0.0), axis=0, keepdims=True)


def back_substitute(s_ref, t_ref, alpha, beta, pending_ref, x_ref):
    size = x_ref.shape[0]
    rows = lax.broadcasted_iota(jnp.int32, (SUB, SUB), 0)
    cols = lax.broadcasted_iota(jnp.int32, (SUB, SUB), 1)
    groups = SUB // GROUP
    for first in range(size - SUB, -1, -SUB):
        s_small = s_ref[first : first + SUB, first : first + SUB]
        t_small = t_ref[first : first + SUB, first : first + SUB]
        s_diag = jnp.sum(jnp.where(rows == cols, s_small, 0.0), axis=1, keepdims=True)
        t_diag = jnp.sum(jnp.where(rows == cols, t_small, 0.0), axis=1, keepdims=True)
        inverse = 1.0 / (beta * s_diag - alpha * t_diag)
        s_strict = jnp.where(rows < cols, s_small, 0.0)
        t_strict = jnp.where(rows < cols, t_small, 0.0)
        pending = [
            pending_ref[first + g * GROUP : first + (g + 1) * GROUP, :] for g in range(groups)
        ]
        for column in range(SUB - 1, -1, -1):
            own, row = divmod(column, GROUP)
            right = pending[own][row : row + 1, :]
            reciprocal = inverse[column : column + 1, :]
            x_ref[first + column : first + column + 1, :] = right * reciprocal
            scaled_beta = beta * reciprocal
            scaled_alpha = alpha * reciprocal
            for g in range(own + 1):
                span = slice(g * GROUP, (g + 1) * GROUP)
                factor = (
                    s_strict[span, column : column + 1] * scaled_beta
                    - t_strict[span, column : column + 1] * scaled_alpha
                )
                pending[g] = pending[g] - factor * right
        if first:
            block = x_ref[first : first + SUB, :]
            columns = slice(first, first + SUB)
            pending_ref[:first, :] = pending_ref[:first, :] - stacked_dot(
                jnp.concatenate([s_ref[:first, columns], t_ref[:first, columns]], axis=1),
                jnp.concatenate([beta * block, -alpha * block], axis=0),
            )


def put_together(core, side, piece_refs, whole_ref):
    quarter = whole_ref.shape[0] // 4
    places = [(core, side), (core, 1 - side), (1 - core, side), (1 - core, 1 - side)]
    for ref, (half, part) in zip(piece_refs, places):
        start = (2 * half + part) * quarter
        whole_ref[pl.ds(pl.multiple_of(start, quarter), quarter), :] = ref[...]


def hand_out(core, x_ref, kept_ref, given_ref):
    half = kept_ref.shape[0]
    kept_ref[...] = x_ref[pl.ds(pl.multiple_of(core * half, half), half), :]
    given_ref[...] = x_ref[pl.ds(pl.multiple_of((1 - core) * half, half), half), :]


def lower_kernel(
    slots, me, s_ref, t_ref, r_ref, values_a, values_b, selected, kept_ref, given_ref, *refs
):
    alpha_ref, beta_ref, pending_ref, x_ref = refs
    alpha = table_lookup(selected[...], values_a[...])
    beta = table_lookup(selected[...], values_b[...])
    alpha_ref[...] = alpha
    beta_ref[...] = beta
    pending_ref[...] = r_ref[...]
    back_substitute(s_ref, t_ref, alpha, beta, pending_ref, x_ref)
    hand_out(me[0] & 1, x_ref, kept_ref, given_ref)


def upper_kernel(slots, me, s_ref, t_ref, r_ref, alpha_ref, beta_ref, *refs):
    piece_refs, (kept_ref, given_ref, lower_ref, pending_ref, x_ref) = refs[:4], refs[4:]
    block = x_ref.shape[0]
    alpha, beta = alpha_ref[...], beta_ref[...]
    put_together(me[0] & 1, (me[0] >> 1) & 1, piece_refs, lower_ref)
    lower = lower_ref[...]
    pending_ref[...] = r_ref[...] - (
        exact_dot(s_ref[:, block:], beta * lower) - exact_dot(t_ref[:, block:], alpha * lower)
    )
    back_substitute(s_ref, t_ref, alpha, beta, pending_ref, x_ref)
    hand_out(me[0] & 1, x_ref, kept_ref, given_ref)


def solve_lower(slots, me, pencil_s, pencil_t, sides, value_alpha, value_beta, selected):
    block, eigs = pencil_s.shape[1] // 2, sides.shape[1]
    count, last = sides.shape[0] // block, slots.shape[0] - 1
    lanes = 128 if value_alpha.shape[0] % 128 == 0 else value_alpha.shape[0]
    table_shape = (value_alpha.shape[0] // lanes, lanes)
    corner = pl.BlockSpec((block, block), lambda i, slots, me: (lax.rem(slots[last], count), 1))
    whole = pl.BlockSpec((block, eigs), lambda i, slots, me: (lax.rem(slots[last], count), 0))
    line = pl.BlockSpec((1, eigs), lambda i, slots, me: (0, 0))
    half = pl.BlockSpec((block // 2, eigs), lambda i, slots, me: (0, 0))
    table = pl.BlockSpec(table_shape, lambda i, slots, me: (0, 0))
    return pl.pallas_call(
        lower_kernel,
        out_shape=(
            *[jax.ShapeDtypeStruct((block // 2, eigs), jnp.float32)] * 2,
            jax.ShapeDtypeStruct((1, eigs), jnp.float32),
            jax.ShapeDtypeStruct((1, eigs), jnp.float32),
        ),
        grid_spec=pltpu.PrefetchScalarGridSpec(
            num_scalar_prefetch=2,
            grid=(1,),
            in_specs=[corner, corner, whole, table, table, line],
            out_specs=(*[half] * 2, line, line),
            scratch_shapes=[pltpu.VMEM((block, eigs), jnp.float32)] * 2,
        ),
        compiler_params=pltpu.CompilerParams(vmem_limit_bytes=FULL_VMEM_BYTES),
        cost_estimate=LIGHT,
        name="solve_lower",
    )(
        slots,
        me,
        pencil_s,
        pencil_t,
        sides,
        value_alpha.reshape(table_shape),
        value_beta.reshape(table_shape),
        selected[None, :],
    )


def solve_upper(slots, me, pencil_s, pencil_t, sides, alpha, beta, pieces):
    block, eigs = pencil_s.shape[1] // 2, sides.shape[1]
    count, index = sides.shape[0] // block, slots.shape[0] - 2
    band = pl.BlockSpec((block, 2 * block), lambda i, slots, me: (lax.rem(slots[index], count), 0))
    whole = pl.BlockSpec((block, eigs), lambda i, slots, me: (lax.rem(slots[index], count), 0))
    line = pl.BlockSpec((1, eigs), lambda i, slots, me: (0, 0))
    fixed = [pl.BlockSpec(piece.shape, lambda i, slots, me: (0, 0)) for piece in pieces]
    return pl.pallas_call(
        upper_kernel,
        out_shape=(
            *[jax.ShapeDtypeStruct((block // 2, eigs), jnp.float32)] * 2,
            jax.ShapeDtypeStruct((block, eigs), jnp.float32),
        ),
        grid_spec=pltpu.PrefetchScalarGridSpec(
            num_scalar_prefetch=2,
            grid=(1,),
            in_specs=[band, band, whole, line, line, *fixed],
            out_specs=(
                *[pl.BlockSpec((block // 2, eigs), lambda i, slots, me: (0, 0))] * 2,
                pl.BlockSpec((block, eigs), lambda i, slots, me: (0, 0)),
            ),
            scratch_shapes=[pltpu.VMEM((block, eigs), jnp.float32)] * 2,
        ),
        compiler_params=pltpu.CompilerParams(vmem_limit_bytes=FULL_VMEM_BYTES),
        cost_estimate=LIGHT,
        name="solve_upper",
    )(slots, me, pencil_s, pencil_t, sides, alpha, beta, *pieces)


def near_dot(left, right_terms):
    high, low = split_two(left)
    return jnp.dot(
        jnp.concatenate([high, low, high], axis=1), right_terms, preferred_element_type=jnp.float32
    )


def three_terms(right):
    high, low = split_two(right)
    return jnp.concatenate([high, high, low], axis=0)


def finish_kernel(slots, me, parts, r_ref, s_ref, t_ref, alpha_ref, beta_ref, lower_ref, *refs):
    piece_refs, (out_ref, terms_ref, upper_ref) = refs[:4], refs[4:]
    put_together(me[0] & 1, (me[0] >> 1) & 1, piece_refs, upper_ref)
    block = upper_ref.shape[0]
    width = block // parts.shape[0]
    for part in range(parts.shape[0]):
        rows = pl.ds(pl.multiple_of(parts[part] * width, width), width)
        for half, source in enumerate((upper_ref, lower_ref)):
            target = (2 * part + half) * width
            high, low = split_two(source[rows, :])
            for term, value in enumerate((high, high, low)):
                first = 2 * block * term + target
                terms_ref[first : first + width, :] = value
    count = out_ref.shape[0] // block
    base = me[0] * count
    alpha, beta = alpha_ref[...], beta_ref[...]
    upper, lower = upper_ref[...], lower_ref[...]
    x = jnp.concatenate([upper, lower], axis=0)
    update = near_dot(s_ref[...], three_terms(beta * x)) - near_dot(t_ref[...], three_terms(alpha * x))
    for slot in range(count):
        span = slice(slot * block, (slot + 1) * block)
        fresh = r_ref[span, :] - update[span, :]
        fresh = jnp.where(slots[slots.shape[0] - 2] == base + slot, upper, fresh)
        out_ref[span, :] = jnp.where(slots[slots.shape[0] - 1] == base + slot, lower, fresh)


def finish_sides(slots, me, parts, sides, pencil_s, pencil_t, alpha, beta, lower, pieces):
    block, eigs = lower.shape
    smem, vmem = pl.BlockSpec(memory_space=pltpu.SMEM), pl.BlockSpec(memory_space=pltpu.VMEM)
    return pl.pallas_call(
        finish_kernel,
        out_shape=(
            jax.ShapeDtypeStruct(sides.shape, jnp.float32),
            jax.ShapeDtypeStruct((6 * block, eigs), jnp.bfloat16),
        ),
        in_specs=[smem] * 3 + [vmem] * (6 + len(pieces)),
        out_specs=(vmem, vmem),
        scratch_shapes=[pltpu.VMEM((block, eigs), jnp.float32)],
        compiler_params=pltpu.CompilerParams(vmem_limit_bytes=VMEM_BYTES),
        cost_estimate=LIGHT,
        name="finish_sides",
    )(slots, me, parts, sides, pencil_s, pencil_t, alpha, beta, lower, *pieces)


def add_kernel(paired, base_ref, terms_ref, *refs):
    part_refs, out_ref = refs[: len(refs) - 1], refs[-1]
    tile = out_ref.shape[0]
    pieces = []
    for ref in part_refs:
        if paired:
            pieces.append(ref[pl.ds(0, tile, 2), :])
            pieces.append(ref[pl.ds(1, tile, 2), :])
        else:
            pieces.append(ref[...])
    basis = jnp.concatenate(pieces, axis=1)
    out_ref[...] = base_ref[...] + near_dot(basis, terms_ref[...])


def add_product(vectors, terms, parts, paired):
    rows, eigs = vectors.shape
    tile = math.gcd(TILE, rows)
    per, width = parts[0].shape[0] // rows, parts[0].shape[1]

    def stream(height, lanes):
        return pl.BlockSpec((height, lanes), lambda i: (i, 0))

    return pl.pallas_call(
        functools.partial(add_kernel, paired),
        out_shape=jax.ShapeDtypeStruct((rows, eigs), jnp.float32),
        grid=(rows // tile,),
        in_specs=[stream(tile, eigs), pl.BlockSpec(memory_space=pltpu.VMEM)]
        + [stream(per * tile, width) for _ in parts],
        out_specs=pl.BlockSpec((tile, eigs), lambda i: (i, 0)),
        compiler_params=pltpu.CompilerParams(vmem_limit_bytes=ADD_VMEM_BYTES),
        cost_estimate=LIGHT,
        name="add_product",
    )(vectors, terms, *parts)


def spread(kept, given, me, owner, axis, size):
    core, side = me & 1, (me >> 1) & 1
    if size & (size - 1) or size < 4:
        parts = [jnp.where(core == 0, kept, given), jnp.where(core == 0, given, kept)]
        block = jnp.concatenate(parts, axis=0)
        block = lax.psum(jnp.where(me == owner, block, jnp.zeros_like(block)), axis)
        quarter = block.shape[0] // 4
        places = [(core, side), (core, 1 - side), (1 - core, side), (1 - core, 1 - side)]
        return [
            lax.dynamic_slice_in_dim(block, (2 * first + second) * quarter, quarter, 0)
            for first, second in places
        ]

    def exchange(value, bit):
        return lax.ppermute(value, axis, [(i, i ^ bit) for i in range(size)])

    apart = me ^ owner
    kept = jnp.where(apart == 0, kept, exchange(given, 1))
    middle = kept.shape[0] // 2
    first, second = kept[:middle], kept[middle:]
    kept, given = jnp.where(side == 0, first, second), jnp.where(side == 0, second, first)
    kept = jnp.where(apart < 2, kept, exchange(given, 2))
    bit = 4
    while bit < size:
        kept = jnp.where(apart < bit, kept, exchange(kept, bit))
        bit *= 2
    return [kept] + [exchange(kept, bits) for bits in (2, 1, 3)]


def on_device(
    row_size,
    col_size,
    right_sides,
    pencil_s,
    pencil_t,
    value_alpha,
    value_beta,
    selected,
    block_slot,
    right_basis,
    vectors,
):
    block = pencil_s.shape[1] // 2
    slot_count = right_sides.shape[0] // block
    block_count = block_slot.shape[0]
    rows, _, width = right_basis.shape
    me_row = lax.axis_index("row")
    me_col = lax.axis_index("col")
    slot_upper = block_slot[block_count - 2]
    slot_lower = block_slot[block_count - 1]

    paired = width % 128 == 0
    own = right_basis.reshape((2 * rows, width) if paired else (rows, 2 * width))
    received = [
        lax.ppermute(own, "col", [(i, (i + step) % col_size) for i in range(col_size)])
        for step in range(1, col_size)
    ]
    me = me_row[None]
    parts = jnp.stack([lax.rem(me_col + (col_size - step), col_size) for step in range(col_size)])
    owner_lower, owner_upper = lax.div(slot_lower, slot_count), lax.div(slot_upper, slot_count)
    kept, given, alpha, beta = solve_lower(
        block_slot, me, pencil_s, pencil_t, right_sides, value_alpha, value_beta, selected
    )
    lower = spread(kept, given, me_row, owner_lower, "row", row_size)
    kept, given, lower = solve_upper(
        block_slot, me, pencil_s, pencil_t, right_sides, alpha, beta, lower
    )
    upper = spread(kept, given, me_row, owner_upper, "row", row_size)
    updated_sides, terms = finish_sides(
        block_slot, me, parts, right_sides, pencil_s, pencil_t, alpha, beta, lower, upper
    )
    updated_vectors = add_product(vectors, terms, [own, *received], paired)
    return (updated_sides, updated_vectors)


def solution(mesh):
    body = functools.partial(on_device, mesh.shape["row"], mesh.shape["col"])
    return jax.shard_map(
        body,
        mesh=mesh,
        in_specs=(
            P("row", "col"),
            P("row", None),
            P("row", None),
            P(),
            P(),
            P("col"),
            P(),
            P("row", None, "col"),
            P("row", "col"),
        ),
        out_specs=(P("row", "col"), P("row", "col")),
        check_vma=False,
    )
```

```python
import functools
import math

import jax
import jax.numpy as jnp
from jax import lax
from jax.experimental import pallas as pl
from jax.experimental.pallas import tpu as pltpu
from jax.sharding import PartitionSpec as P

SUB = 32
GROUP = 8
VMEM_BYTES = 57 * 1024 * 1024
ADD_VMEM_BYTES = 36 * 1024 * 1024
FULL_VMEM_BYTES = 59 * 1024 * 1024
TILE = 512
LIGHT = pl.CostEstimate(flops=1000, bytes_accessed=1000, transcendentals=0)


def exact_dot(left, right):
    return jnp.dot(left, right, precision=lax.Precision.HIGHEST, preferred_element_type=jnp.float32)


def split_two(value):
    high = value.astype(jnp.bfloat16)
    low = (value - high.astype(jnp.float32)).astype(jnp.bfloat16)
    return high, low


def split_three(value):
    high = value.astype(jnp.bfloat16)
    rest = value - high.astype(jnp.float32)
    middle = rest.astype(jnp.bfloat16)
    low = (rest - middle.astype(jnp.float32)).astype(jnp.bfloat16)
    return high, middle, low


def stacked_dot(left, right):
    high, middle, low = split_three(left)
    top, mid, end = split_three(right)
    return jnp.dot(
        jnp.concatenate([high, middle, high, middle, high, low], axis=1),
        jnp.concatenate([top, top, mid, mid, end, top], axis=0),
        preferred_element_type=jnp.float32,
    )


def table_lookup(selected, table):
    table_rows, lanes = table.shape
    lane = lax.broadcasted_iota(jnp.int32, (lanes, selected.shape[1]), 0)
    in_lane = jnp.where(lane == selected % lanes, 1.0, 0.0)
    candidates = exact_dot(table, in_lane)
    row = lax.broadcasted_iota(jnp.int32, candidates.shape, 0)
    return jnp.sum(jnp.where(row == selected // lanes, candidates, 0.0), axis=0, keepdims=True)


def back_substitute(s_ref, t_ref, alpha, beta, pending_ref, x_ref):
    size = x_ref.shape[0]
    rows = lax.broadcasted_iota(jnp.int32, (SUB, SUB), 0)
    cols = lax.broadcasted_iota(jnp.int32, (SUB, SUB), 1)
    groups = SUB // GROUP
    for first in range(size - SUB, -1, -SUB):
        s_small = s_ref[first : first + SUB, first : first + SUB]
        t_small = t_ref[first : first + SUB, first : first + SUB]
        s_diag = jnp.sum(jnp.where(rows == cols, s_small, 0.0), axis=1, keepdims=True)
        t_diag = jnp.sum(jnp.where(rows == cols, t_small, 0.0), axis=1, keepdims=True)
        inverse = 1.0 / (beta * s_diag - alpha * t_diag)
        s_strict = jnp.where(rows < cols, s_small, 0.0)
        t_strict = jnp.where(rows < cols, t_small, 0.0)
        pending = [
            pending_ref[first + g * GROUP : first + (g + 1) * GROUP, :] for g in range(groups)
        ]
        for column in range(SUB - 1, -1, -1):
            own, row = divmod(column, GROUP)
            right = pending[own][row : row + 1, :]
            reciprocal = inverse[column : column + 1, :]
            x_ref[first + column : first + column + 1, :] = right * reciprocal
            scaled_beta = beta * reciprocal
            scaled_alpha = alpha * reciprocal
            for g in range(own + 1):
                span = slice(g * GROUP, (g + 1) * GROUP)
                factor = (
                    s_strict[span, column : column + 1] * scaled_beta
                    - t_strict[span, column : column + 1] * scaled_alpha
                )
                pending[g] = pending[g] - factor * right
        if first:
            block = x_ref[first : first + SUB, :]
            columns = slice(first, first + SUB)
            pending_ref[:first, :] = pending_ref[:first, :] - stacked_dot(
                jnp.concatenate([s_ref[:first, columns], t_ref[:first, columns]], axis=1),
                jnp.concatenate([beta * block, -alpha * block], axis=0),
            )


def put_together(core, side, piece_refs, whole_ref):
    quarter = whole_ref.shape[0] // 4
    places = [(core, side), (core, 1 - side), (1 - core, side), (1 - core, 1 - side)]
    for ref, (half, part) in zip(piece_refs, places):
        start = (2 * half + part) * quarter
        whole_ref[pl.ds(pl.multiple_of(start, quarter), quarter), :] = ref[...]


def hand_out(core, x_ref, kept_ref, given_ref):
    half = kept_ref.shape[0]
    kept_ref[...] = x_ref[pl.ds(pl.multiple_of(core * half, half), half), :]
    given_ref[...] = x_ref[pl.ds(pl.multiple_of((1 - core) * half, half), half), :]


def lower_kernel(
    slots, me, s_ref, t_ref, r_ref, values_a, values_b, selected, kept_ref, given_ref, *refs
):
    alpha_ref, beta_ref, pending_ref, x_ref = refs
    alpha = table_lookup(selected[...], values_a[...])
    beta = table_lookup(selected[...], values_b[...])
    alpha_ref[...] = alpha
    beta_ref[...] = beta
    pending_ref[...] = r_ref[...]
    back_substitute(s_ref, t_ref, alpha, beta, pending_ref, x_ref)
    hand_out(me[0] & 1, x_ref, kept_ref, given_ref)


def upper_kernel(slots, me, s_ref, t_ref, r_ref, alpha_ref, beta_ref, *refs):
    piece_refs, (kept_ref, given_ref, lower_ref, pending_ref, x_ref) = refs[:4], refs[4:]
    block = x_ref.shape[0]
    alpha, beta = alpha_ref[...], beta_ref[...]
    put_together(me[0] & 1, (me[0] >> 1) & 1, piece_refs, lower_ref)
    lower = lower_ref[...]
    pending_ref[...] = r_ref[...] - (
        exact_dot(s_ref[:, block:], beta * lower) - exact_dot(t_ref[:, block:], alpha * lower)
    )
    back_substitute(s_ref, t_ref, alpha, beta, pending_ref, x_ref)
    hand_out(me[0] & 1, x_ref, kept_ref, given_ref)


def solve_lower(slots, me, pencil_s, pencil_t, sides, value_alpha, value_beta, selected):
    block, eigs = pencil_s.shape[1] // 2, sides.shape[1]
    count, last = sides.shape[0] // block, slots.shape[0] - 1
    lanes = 128 if value_alpha.shape[0] % 128 == 0 else value_alpha.shape[0]
    table_shape = (value_alpha.shape[0] // lanes, lanes)
    corner = pl.BlockSpec((block, block), lambda i, slots, me: (lax.rem(slots[last], count), 1))
    whole = pl.BlockSpec((block, eigs), lambda i, slots, me: (lax.rem(slots[last], count), 0))
    line = pl.BlockSpec((1, eigs), lambda i, slots, me: (0, 0))
    half = pl.BlockSpec((block // 2, eigs), lambda i, slots, me: (0, 0))
    table = pl.BlockSpec(table_shape, lambda i, slots, me: (0, 0))
    return pl.pallas_call(
        lower_kernel,
        out_shape=(
            *[jax.ShapeDtypeStruct((block // 2, eigs), jnp.float32)] * 2,
            jax.ShapeDtypeStruct((1, eigs), jnp.float32),
            jax.ShapeDtypeStruct((1, eigs), jnp.float32),
        ),
        grid_spec=pltpu.PrefetchScalarGridSpec(
            num_scalar_prefetch=2,
            grid=(1,),
            in_specs=[corner, corner, whole, table, table, line],
            out_specs=(*[half] * 2, line, line),
            scratch_shapes=[pltpu.VMEM((block, eigs), jnp.float32)] * 2,
        ),
        compiler_params=pltpu.CompilerParams(vmem_limit_bytes=FULL_VMEM_BYTES),
        cost_estimate=LIGHT,
        name="solve_lower",
    )(
        slots,
        me,
        pencil_s,
        pencil_t,
        sides,
        value_alpha.reshape(table_shape),
        value_beta.reshape(table_shape),
        selected[None, :],
    )


def solve_upper(slots, me, pencil_s, pencil_t, sides, alpha, beta, pieces):
    block, eigs = pencil_s.shape[1] // 2, sides.shape[1]
    count, index = sides.shape[0] // block, slots.shape[0] - 2
    band = pl.BlockSpec((block, 2 * block), lambda i, slots, me: (lax.rem(slots[index], count), 0))
    whole = pl.BlockSpec((block, eigs), lambda i, slots, me: (lax.rem(slots[index], count), 0))
    line = pl.BlockSpec((1, eigs), lambda i, slots, me: (0, 0))
    fixed = [pl.BlockSpec(piece.shape, lambda i, slots, me: (0, 0)) for piece in pieces]
    return pl.pallas_call(
        upper_kernel,
        out_shape=(
            *[jax.ShapeDtypeStruct((block // 2, eigs), jnp.float32)] * 2,
            jax.ShapeDtypeStruct((block, eigs), jnp.float32),
        ),
        grid_spec=pltpu.PrefetchScalarGridSpec(
            num_scalar_prefetch=2,
            grid=(1,),
            in_specs=[band, band, whole, line, line, *fixed],
            out_specs=(
                *[pl.BlockSpec((block // 2, eigs), lambda i, slots, me: (0, 0))] * 2,
                pl.BlockSpec((block, eigs), lambda i, slots, me: (0, 0)),
            ),
            scratch_shapes=[pltpu.VMEM((block, eigs), jnp.float32)] * 2,
        ),
        compiler_params=pltpu.CompilerParams(vmem_limit_bytes=FULL_VMEM_BYTES),
        cost_estimate=LIGHT,
        name="solve_upper",
    )(slots, me, pencil_s, pencil_t, sides, alpha, beta, *pieces)


def near_dot(left, right_terms):
    high, low = split_two(left)
    return jnp.dot(
        jnp.concatenate([high, low, high], axis=1), right_terms, preferred_element_type=jnp.float32
    )


def three_terms(right):
    high, low = split_two(right)
    return jnp.concatenate([high, high, low], axis=0)


def finish_kernel(slots, me, parts, r_ref, s_ref, t_ref, alpha_ref, beta_ref, lower_ref, *refs):
    piece_refs, (out_ref, own_terms, other_terms, upper_ref) = refs[:4], refs[4:]
    put_together(me[0] & 1, (me[0] >> 1) & 1, piece_refs, upper_ref)
    block = upper_ref.shape[0]
    width = block // parts.shape[0]
    for part in range(parts.shape[0]):
        rows = pl.ds(pl.multiple_of(parts[part] * width, width), width)
        terms_ref = other_terms if part else own_terms
        for half, source in enumerate((upper_ref, lower_ref)):
            target = (2 * max(part - 1, 0) + half) * width
            high, low = split_two(source[rows, :])
            for term, value in enumerate((high, high, low)):
                first = terms_ref.shape[0] // 3 * term + target
                terms_ref[first : first + width, :] = value
    count = out_ref.shape[0] // block
    base = me[0] * count
    alpha, beta = alpha_ref[...], beta_ref[...]
    upper, lower = upper_ref[...], lower_ref[...]
    x = jnp.concatenate([upper, lower], axis=0)
    update = near_dot(s_ref[...], three_terms(beta * x)) - near_dot(t_ref[...], three_terms(alpha * x))
    for slot in range(count):
        span = slice(slot * block, (slot + 1) * block)
        fresh = r_ref[span, :] - update[span, :]
        fresh = jnp.where(slots[slots.shape[0] - 2] == base + slot, upper, fresh)
        out_ref[span, :] = jnp.where(slots[slots.shape[0] - 1] == base + slot, lower, fresh)


def finish_sides(slots, me, parts, sides, pencil_s, pencil_t, alpha, beta, lower, pieces):
    block, eigs = lower.shape
    width = block // parts.shape[0]
    smem, vmem = pl.BlockSpec(memory_space=pltpu.SMEM), pl.BlockSpec(memory_space=pltpu.VMEM)
    return pl.pallas_call(
        finish_kernel,
        out_shape=(
            jax.ShapeDtypeStruct(sides.shape, jnp.float32),
            jax.ShapeDtypeStruct((6 * width, eigs), jnp.bfloat16),
            jax.ShapeDtypeStruct((6 * (block - width), eigs), jnp.bfloat16),
        ),
        in_specs=[smem] * 3 + [vmem] * (6 + len(pieces)),
        out_specs=(vmem, vmem, vmem),
        scratch_shapes=[pltpu.VMEM((block, eigs), jnp.float32)],
        compiler_params=pltpu.CompilerParams(vmem_limit_bytes=VMEM_BYTES),
        cost_estimate=LIGHT,
        name="finish_sides",
    )(slots, me, parts, sides, pencil_s, pencil_t, alpha, beta, lower, *pieces)


def add_kernel(paired, held, base_ref, terms_ref, *refs):
    part_refs, out_ref = refs[:-1], refs[-1]
    tile = part_refs[0].shape[0] // (2 if paired else 1)
    if paired:
        pieces = [ref[pl.ds(half, tile, 2), :] for ref in part_refs for half in range(2)]
    else:
        pieces = [ref[...] for ref in part_refs]
    product = near_dot(jnp.concatenate(pieces, axis=1), terms_ref[...])
    whole = pl.ds(pl.multiple_of(pl.program_id(0) * tile, tile), tile)
    if held == "out":
        out_ref[whole, :] = base_ref[...] + product
    else:
        out_ref[...] = base_ref[whole, :] + product


def add_product(base, terms, parts, paired, held):
    rows, eigs = base.shape
    tile = math.gcd(TILE, rows)
    per, width = parts[0].shape[0] // rows, parts[0].shape[1]
    tiles, vmem = pl.BlockSpec((tile, eigs), lambda i: (i, 0)), pl.BlockSpec(memory_space=pltpu.VMEM)
    return pl.pallas_call(
        functools.partial(add_kernel, paired, held),
        out_shape=jax.ShapeDtypeStruct((rows, eigs), jnp.float32),
        grid=(rows // tile,),
        in_specs=[vmem if held == "base" else tiles, vmem]
        + [pl.BlockSpec((per * tile, width), lambda i: (i, 0)) for _ in parts],
        out_specs=vmem if held == "out" else tiles,
        compiler_params=pltpu.CompilerParams(vmem_limit_bytes=ADD_VMEM_BYTES),
        cost_estimate=LIGHT,
        name="add_own" if held == "out" else "add_received",
    )(base, terms, *parts)


def spread(kept, given, me, owner, axis, size):
    core, side = me & 1, (me >> 1) & 1
    if size & (size - 1) or size < 4:
        parts = [jnp.where(core == 0, kept, given), jnp.where(core == 0, given, kept)]
        block = jnp.concatenate(parts, axis=0)
        block = lax.psum(jnp.where(me == owner, block, jnp.zeros_like(block)), axis)
        quarter = block.shape[0] // 4
        places = [(core, side), (core, 1 - side), (1 - core, side), (1 - core, 1 - side)]
        return [
            lax.dynamic_slice_in_dim(block, (2 * first + second) * quarter, quarter, 0)
            for first, second in places
        ]

    def exchange(value, bit):
        return lax.ppermute(value, axis, [(i, i ^ bit) for i in range(size)])

    apart = me ^ owner
    kept = jnp.where(apart == 0, kept, exchange(given, 1))
    middle = kept.shape[0] // 2
    first, second = kept[:middle], kept[middle:]
    kept, given = jnp.where(side == 0, first, second), jnp.where(side == 0, second, first)
    kept = jnp.where(apart < 2, kept, exchange(given, 2))
    bit = 4
    while bit < size:
        kept = jnp.where(apart < bit, kept, exchange(kept, bit))
        bit *= 2
    return [kept] + [exchange(kept, bits) for bits in (2, 1, 3)]


def on_device(
    row_size,
    col_size,
    right_sides,
    pencil_s,
    pencil_t,
    value_alpha,
    value_beta,
    selected,
    block_slot,
    right_basis,
    vectors,
):
    block = pencil_s.shape[1] // 2
    slot_count = right_sides.shape[0] // block
    block_count = block_slot.shape[0]
    rows, _, width = right_basis.shape
    me_row = lax.axis_index("row")
    me_col = lax.axis_index("col")
    slot_upper = block_slot[block_count - 2]
    slot_lower = block_slot[block_count - 1]

    paired = width % 128 == 0
    own = right_basis.reshape((2 * rows, width) if paired else (rows, 2 * width))
    received = [
        lax.ppermute(own, "col", [(i, (i + step) % col_size) for i in range(col_size)])
        for step in range(1, col_size)
    ]
    me = me_row[None]
    parts = jnp.stack([lax.rem(me_col + (col_size - step), col_size) for step in range(col_size)])
    owner_lower, owner_upper = lax.div(slot_lower, slot_count), lax.div(slot_upper, slot_count)
    kept, given, alpha, beta = solve_lower(
        block_slot, me, pencil_s, pencil_t, right_sides, value_alpha, value_beta, selected
    )
    lower = spread(kept, given, me_row, owner_lower, "row", row_size)
    kept, given, lower = solve_upper(
        block_slot, me, pencil_s, pencil_t, right_sides, alpha, beta, lower
    )
    upper = spread(kept, given, me_row, owner_upper, "row", row_size)
    updated_sides, own_terms, other_terms = finish_sides(
        block_slot, me, parts, right_sides, pencil_s, pencil_t, alpha, beta, lower, upper
    )
    updated_vectors = add_product(vectors, own_terms, [own], paired, "out")
    updated_vectors = add_product(updated_vectors, other_terms, received, paired, "base")
    return (updated_sides, updated_vectors)


def solution(mesh):
    body = functools.partial(on_device, mesh.shape["row"], mesh.shape["col"])
    return jax.shard_map(
        body,
        mesh=mesh,
        in_specs=(
            P("row", "col"),
            P("row", None),
            P("row", None),
            P(),
            P(),
            P("col"),
            P(),
            P("row", None, "col"),
            P("row", "col"),
        ),
        out_specs=(P("row", "col"), P("row", "col")),
        check_vma=False,
    )
```

```python
import functools
import math

import jax
import jax.numpy as jnp
from jax import lax
from jax.experimental import pallas as pl
from jax.experimental.pallas import tpu as pltpu
from jax.sharding import PartitionSpec as P

SUB = 32
GROUP = 8
VMEM_BYTES = 109 * 512 * 1024
ADD_VMEM_BYTES = 36 * 1024 * 1024
FULL_VMEM_BYTES = 59 * 1024 * 1024
TILE = 512
LIGHT = pl.CostEstimate(flops=1000, bytes_accessed=1000, transcendentals=0)


def exact_dot(left, right):
    return jnp.dot(left, right, precision=lax.Precision.HIGHEST, preferred_element_type=jnp.float32)


def split_two(value):
    high = value.astype(jnp.bfloat16)
    low = (value - high.astype(jnp.float32)).astype(jnp.bfloat16)
    return high, low


def split_three(value):
    high = value.astype(jnp.bfloat16)
    rest = value - high.astype(jnp.float32)
    middle = rest.astype(jnp.bfloat16)
    low = (rest - middle.astype(jnp.float32)).astype(jnp.bfloat16)
    return high, middle, low


def stacked_dot(left, right):
    high, middle, low = split_three(left)
    top, mid, end = split_three(right)
    return jnp.dot(
        jnp.concatenate([high, middle, high, middle, high, low], axis=1),
        jnp.concatenate([top, top, mid, mid, end, top], axis=0),
        preferred_element_type=jnp.float32,
    )


def table_lookup(selected, table):
    table_rows, lanes = table.shape
    lane = lax.broadcasted_iota(jnp.int32, (lanes, selected.shape[1]), 0)
    in_lane = jnp.where(lane == selected % lanes, 1.0, 0.0)
    candidates = exact_dot(table, in_lane)
    row = lax.broadcasted_iota(jnp.int32, candidates.shape, 0)
    return jnp.sum(jnp.where(row == selected // lanes, candidates, 0.0), axis=0, keepdims=True)


def back_substitute(s_ref, t_ref, alpha, beta, pending_ref, x_ref):
    size = x_ref.shape[0]
    rows = lax.broadcasted_iota(jnp.int32, (SUB, SUB), 0)
    cols = lax.broadcasted_iota(jnp.int32, (SUB, SUB), 1)
    groups = SUB // GROUP
    for first in range(size - SUB, -1, -SUB):
        s_small = s_ref[first : first + SUB, first : first + SUB]
        t_small = t_ref[first : first + SUB, first : first + SUB]
        s_diag = jnp.sum(jnp.where(rows == cols, s_small, 0.0), axis=1, keepdims=True)
        t_diag = jnp.sum(jnp.where(rows == cols, t_small, 0.0), axis=1, keepdims=True)
        inverse = 1.0 / (beta * s_diag - alpha * t_diag)
        s_strict = jnp.where(rows < cols, s_small, 0.0)
        t_strict = jnp.where(rows < cols, t_small, 0.0)
        pending = [
            pending_ref[first + g * GROUP : first + (g + 1) * GROUP, :] for g in range(groups)
        ]
        for column in range(SUB - 1, -1, -1):
            own, row = divmod(column, GROUP)
            right = pending[own][row : row + 1, :]
            reciprocal = inverse[column : column + 1, :]
            x_ref[first + column : first + column + 1, :] = right * reciprocal
            scaled_beta = beta * reciprocal
            scaled_alpha = alpha * reciprocal
            for g in range(own + 1):
                span = slice(g * GROUP, (g + 1) * GROUP)
                factor = (
                    s_strict[span, column : column + 1] * scaled_beta
                    - t_strict[span, column : column + 1] * scaled_alpha
                )
                pending[g] = pending[g] - factor * right
        if first:
            block = x_ref[first : first + SUB, :]
            columns = slice(first, first + SUB)
            pending_ref[:first, :] = pending_ref[:first, :] - stacked_dot(
                jnp.concatenate([s_ref[:first, columns], t_ref[:first, columns]], axis=1),
                jnp.concatenate([beta * block, -alpha * block], axis=0),
            )


def put_together(core, side, piece_refs, whole_ref):
    quarter = whole_ref.shape[0] // 4
    places = [(core, side), (core, 1 - side), (1 - core, side), (1 - core, 1 - side)]
    for ref, (half, part) in zip(piece_refs, places):
        start = (2 * half + part) * quarter
        whole_ref[pl.ds(pl.multiple_of(start, quarter), quarter), :] = ref[...]


def hand_out(core, x_ref, kept_ref, given_ref):
    half = kept_ref.shape[0]
    kept_ref[...] = x_ref[pl.ds(pl.multiple_of(core * half, half), half), :]
    given_ref[...] = x_ref[pl.ds(pl.multiple_of((1 - core) * half, half), half), :]


def lower_kernel(
    slots, me, s_ref, t_ref, r_ref, values_a, values_b, selected, kept_ref, given_ref, *refs
):
    alpha_ref, beta_ref, pending_ref, x_ref = refs
    alpha = table_lookup(selected[...], values_a[...])
    beta = table_lookup(selected[...], values_b[...])
    alpha_ref[...] = alpha
    beta_ref[...] = beta
    pending_ref[...] = r_ref[...]
    back_substitute(s_ref, t_ref, alpha, beta, pending_ref, x_ref)
    hand_out(me[0] & 1, x_ref, kept_ref, given_ref)


def upper_kernel(slots, me, s_ref, t_ref, r_ref, alpha_ref, beta_ref, *refs):
    piece_refs, (kept_ref, given_ref, lower_ref, pending_ref, x_ref) = refs[:4], refs[4:]
    block = x_ref.shape[0]
    alpha, beta = alpha_ref[...], beta_ref[...]
    put_together(me[0] & 1, (me[0] >> 1) & 1, piece_refs, lower_ref)
    lower = lower_ref[...]
    pending_ref[...] = r_ref[...] - (
        exact_dot(s_ref[:, block:], beta * lower) - exact_dot(t_ref[:, block:], alpha * lower)
    )
    back_substitute(s_ref, t_ref, alpha, beta, pending_ref, x_ref)
    hand_out(me[0] & 1, x_ref, kept_ref, given_ref)


def solve_lower(slots, me, pencil_s, pencil_t, sides, value_alpha, value_beta, selected):
    block, eigs = pencil_s.shape[1] // 2, sides.shape[1]
    count, last = sides.shape[0] // block, slots.shape[0] - 1
    lanes = 128 if value_alpha.shape[0] % 128 == 0 else value_alpha.shape[0]
    table_shape = (value_alpha.shape[0] // lanes, lanes)
    corner = pl.BlockSpec((block, block), lambda i, slots, me: (lax.rem(slots[last], count), 1))
    whole = pl.BlockSpec((block, eigs), lambda i, slots, me: (lax.rem(slots[last], count), 0))
    line = pl.BlockSpec((1, eigs), lambda i, slots, me: (0, 0))
    half = pl.BlockSpec((block // 2, eigs), lambda i, slots, me: (0, 0))
    table = pl.BlockSpec(table_shape, lambda i, slots, me: (0, 0))
    return pl.pallas_call(
        lower_kernel,
        out_shape=(
            *[jax.ShapeDtypeStruct((block // 2, eigs), jnp.float32)] * 2,
            jax.ShapeDtypeStruct((1, eigs), jnp.float32),
            jax.ShapeDtypeStruct((1, eigs), jnp.float32),
        ),
        grid_spec=pltpu.PrefetchScalarGridSpec(
            num_scalar_prefetch=2,
            grid=(1,),
            in_specs=[corner, corner, whole, table, table, line],
            out_specs=(*[half] * 2, line, line),
            scratch_shapes=[pltpu.VMEM((block, eigs), jnp.float32)] * 2,
        ),
        compiler_params=pltpu.CompilerParams(vmem_limit_bytes=FULL_VMEM_BYTES),
        cost_estimate=LIGHT,
        name="solve_lower",
    )(
        slots,
        me,
        pencil_s,
        pencil_t,
        sides,
        value_alpha.reshape(table_shape),
        value_beta.reshape(table_shape),
        selected[None, :],
    )


def solve_upper(slots, me, pencil_s, pencil_t, sides, alpha, beta, pieces):
    block, eigs = pencil_s.shape[1] // 2, sides.shape[1]
    count, index = sides.shape[0] // block, slots.shape[0] - 2
    band = pl.BlockSpec((block, 2 * block), lambda i, slots, me: (lax.rem(slots[index], count), 0))
    whole = pl.BlockSpec((block, eigs), lambda i, slots, me: (lax.rem(slots[index], count), 0))
    line = pl.BlockSpec((1, eigs), lambda i, slots, me: (0, 0))
    fixed = [pl.BlockSpec(piece.shape, lambda i, slots, me: (0, 0)) for piece in pieces]
    return pl.pallas_call(
        upper_kernel,
        out_shape=(
            *[jax.ShapeDtypeStruct((block // 2, eigs), jnp.float32)] * 2,
            jax.ShapeDtypeStruct((block, eigs), jnp.float32),
        ),
        grid_spec=pltpu.PrefetchScalarGridSpec(
            num_scalar_prefetch=2,
            grid=(1,),
            in_specs=[band, band, whole, line, line, *fixed],
            out_specs=(
                *[pl.BlockSpec((block // 2, eigs), lambda i, slots, me: (0, 0))] * 2,
                pl.BlockSpec((block, eigs), lambda i, slots, me: (0, 0)),
            ),
            scratch_shapes=[pltpu.VMEM((block, eigs), jnp.float32)] * 2,
        ),
        compiler_params=pltpu.CompilerParams(vmem_limit_bytes=FULL_VMEM_BYTES),
        cost_estimate=LIGHT,
        name="solve_upper",
    )(slots, me, pencil_s, pencil_t, sides, alpha, beta, *pieces)


def near_dot(left, right_terms):
    high, low = split_two(left)
    return jnp.dot(
        jnp.concatenate([high, low, high], axis=1), right_terms, preferred_element_type=jnp.float32
    )


def three_terms(right):
    high, low = split_two(right)
    return jnp.concatenate([high, high, low], axis=0)


def finish_kernel(slots, me, parts, r_ref, s_ref, t_ref, alpha_ref, beta_ref, lower_ref, *refs):
    piece_refs, (out_ref, own_terms, other_terms, upper_ref) = refs[:4], refs[4:]
    put_together(me[0] & 1, (me[0] >> 1) & 1, piece_refs, upper_ref)
    block = upper_ref.shape[0]
    width = block // parts.shape[0]
    for part in range(parts.shape[0]):
        rows = pl.ds(pl.multiple_of(parts[part] * width, width), width)
        terms_ref = other_terms if part else own_terms
        for half, source in enumerate((upper_ref, lower_ref)):
            target = (2 * max(part - 1, 0) + half) * width
            high, low = split_two(source[rows, :])
            for term, value in enumerate((high, high, low)):
                first = terms_ref.shape[0] // 3 * term + target
                terms_ref[first : first + width, :] = value
    count = out_ref.shape[0] // block
    base = me[0] * count
    alpha, beta = alpha_ref[...], beta_ref[...]
    upper, lower = upper_ref[...], lower_ref[...]
    x = jnp.concatenate([upper, lower], axis=0)
    update = near_dot(s_ref[...], three_terms(beta * x)) - near_dot(t_ref[...], three_terms(alpha * x))
    for slot in range(count):
        span = slice(slot * block, (slot + 1) * block)
        fresh = r_ref[span, :] - update[span, :]
        fresh = jnp.where(slots[slots.shape[0] - 2] == base + slot, upper, fresh)
        out_ref[span, :] = jnp.where(slots[slots.shape[0] - 1] == base + slot, lower, fresh)


def finish_sides(slots, me, parts, sides, pencil_s, pencil_t, alpha, beta, lower, pieces):
    block, eigs = lower.shape
    width = block // parts.shape[0]
    smem, vmem = pl.BlockSpec(memory_space=pltpu.SMEM), pl.BlockSpec(memory_space=pltpu.VMEM)
    return pl.pallas_call(
        finish_kernel,
        out_shape=(
            jax.ShapeDtypeStruct(sides.shape, jnp.float32),
            jax.ShapeDtypeStruct((6 * width, eigs), jnp.bfloat16),
            jax.ShapeDtypeStruct((6 * (block - width), eigs), jnp.bfloat16),
        ),
        in_specs=[smem] * 3 + [vmem] * (6 + len(pieces)),
        out_specs=(vmem, vmem, vmem),
        scratch_shapes=[pltpu.VMEM((block, eigs), jnp.float32)],
        compiler_params=pltpu.CompilerParams(vmem_limit_bytes=VMEM_BYTES),
        cost_estimate=LIGHT,
        name="finish_sides",
    )(slots, me, parts, sides, pencil_s, pencil_t, alpha, beta, lower, *pieces)


def add_kernel(paired, held, base_ref, terms_ref, *refs):
    part_refs, out_ref = refs[:-1], refs[-1]
    tile = part_refs[0].shape[0] // (2 if paired else 1)
    if paired:
        pieces = [ref[pl.ds(half, tile, 2), :] for ref in part_refs for half in range(2)]
    else:
        pieces = [ref[...] for ref in part_refs]
    product = near_dot(jnp.concatenate(pieces, axis=1), terms_ref[...])
    whole = pl.ds(pl.multiple_of(pl.program_id(0) * tile, tile), tile)
    if held == "out":
        out_ref[whole, :] = base_ref[...] + product
    else:
        out_ref[...] = base_ref[whole, :] + product


def add_product(base, terms, parts, paired, held):
    rows, eigs = base.shape
    tile = math.gcd(TILE, rows)
    per, width = parts[0].shape[0] // rows, parts[0].shape[1]
    tiles, vmem = pl.BlockSpec((tile, eigs), lambda i: (i, 0)), pl.BlockSpec(memory_space=pltpu.VMEM)
    return pl.pallas_call(
        functools.partial(add_kernel, paired, held),
        out_shape=jax.ShapeDtypeStruct((rows, eigs), jnp.float32),
        grid=(rows // tile,),
        in_specs=[vmem if held == "base" else tiles, vmem]
        + [pl.BlockSpec((per * tile, width), lambda i: (i, 0)) for _ in parts],
        out_specs=vmem if held == "out" else tiles,
        compiler_params=pltpu.CompilerParams(vmem_limit_bytes=ADD_VMEM_BYTES),
        cost_estimate=LIGHT,
        name="add_own" if held == "out" else "add_received",
    )(base, terms, *parts)


def spread(kept, given, me, owner, axis, size):
    core, side = me & 1, (me >> 1) & 1
    if size & (size - 1) or size < 4:
        parts = [jnp.where(core == 0, kept, given), jnp.where(core == 0, given, kept)]
        block = jnp.concatenate(parts, axis=0)
        block = lax.psum(jnp.where(me == owner, block, jnp.zeros_like(block)), axis)
        quarter = block.shape[0] // 4
        places = [(core, side), (core, 1 - side), (1 - core, side), (1 - core, 1 - side)]
        return [
            lax.dynamic_slice_in_dim(block, (2 * first + second) * quarter, quarter, 0)
            for first, second in places
        ]

    def exchange(value, bit):
        return lax.ppermute(value, axis, [(i, i ^ bit) for i in range(size)])

    apart = me ^ owner
    kept = jnp.where(apart == 0, kept, exchange(given, 1))
    middle = kept.shape[0] // 2
    first, second = kept[:middle], kept[middle:]
    kept, given = jnp.where(side == 0, first, second), jnp.where(side == 0, second, first)
    kept = jnp.where(apart < 2, kept, exchange(given, 2))
    bit = 4
    while bit < size:
        kept = jnp.where(apart < bit, kept, exchange(kept, bit))
        bit *= 2
    return [kept] + [exchange(kept, bits) for bits in (2, 1, 3)]


def on_device(
    row_size,
    col_size,
    right_sides,
    pencil_s,
    pencil_t,
    value_alpha,
    value_beta,
    selected,
    block_slot,
    right_basis,
    vectors,
):
    block = pencil_s.shape[1] // 2
    slot_count = right_sides.shape[0] // block
    block_count = block_slot.shape[0]
    rows, _, width = right_basis.shape
    me_row = lax.axis_index("row")
    me_col = lax.axis_index("col")
    slot_upper = block_slot[block_count - 2]
    slot_lower = block_slot[block_count - 1]

    paired = width % 128 == 0
    own = right_basis.reshape((2 * rows, width) if paired else (rows, 2 * width))
    received = [
        lax.ppermute(own, "col", [(i, (i + step) % col_size) for i in range(col_size)])
        for step in range(1, col_size)
    ]
    me = me_row[None]
    parts = jnp.stack([lax.rem(me_col + (col_size - step), col_size) for step in range(col_size)])
    owner_lower, owner_upper = lax.div(slot_lower, slot_count), lax.div(slot_upper, slot_count)
    kept, given, alpha, beta = solve_lower(
        block_slot, me, pencil_s, pencil_t, right_sides, value_alpha, value_beta, selected
    )
    lower = spread(kept, given, me_row, owner_lower, "row", row_size)
    kept, given, lower = solve_upper(
        block_slot, me, pencil_s, pencil_t, right_sides, alpha, beta, lower
    )
    upper = spread(kept, given, me_row, owner_upper, "row", row_size)
    updated_sides, own_terms, other_terms = finish_sides(
        block_slot, me, parts, right_sides, pencil_s, pencil_t, alpha, beta, lower, upper
    )
    updated_vectors = add_product(vectors, own_terms, [own], paired, "out")
    updated_vectors = add_product(updated_vectors, other_terms, received, paired, "base")
    return (updated_sides, updated_vectors)


def solution(mesh):
    body = functools.partial(on_device, mesh.shape["row"], mesh.shape["col"])
    return jax.shard_map(
        body,
        mesh=mesh,
        in_specs=(
            P("row", "col"),
            P("row", None),
            P("row", None),
            P(),
            P(),
            P("col"),
            P(),
            P("row", None, "col"),
            P("row", "col"),
        ),
        out_specs=(P("row", "col"), P("row", "col")),
        check_vma=False,
    )
```

```python
import functools
import math

import jax
import jax.numpy as jnp
from jax import lax
from jax.experimental import pallas as pl
from jax.experimental.pallas import tpu as pltpu
from jax.sharding import PartitionSpec as P

SUB = 32
GROUP = 8
VMEM_BYTES = 48 * 1024 * 1024
ADD_VMEM_BYTES = 48 * 1024 * 1024
FULL_VMEM_BYTES = 59 * 1024 * 1024
TILE = 512
LIGHT = pl.CostEstimate(flops=1000, bytes_accessed=1000, transcendentals=0)


def exact_dot(left, right):
    return jnp.dot(left, right, precision=lax.Precision.HIGHEST, preferred_element_type=jnp.float32)


def split_two(value):
    high = value.astype(jnp.bfloat16)
    low = (value - high.astype(jnp.float32)).astype(jnp.bfloat16)
    return high, low


def split_three(value):
    high = value.astype(jnp.bfloat16)
    rest = value - high.astype(jnp.float32)
    middle = rest.astype(jnp.bfloat16)
    low = (rest - middle.astype(jnp.float32)).astype(jnp.bfloat16)
    return high, middle, low


def stacked_dot(left, right):
    high, middle, low = split_three(left)
    top, mid, end = split_three(right)
    return jnp.dot(
        jnp.concatenate([high, middle, high, middle, high, low], axis=1),
        jnp.concatenate([top, top, mid, mid, end, top], axis=0),
        preferred_element_type=jnp.float32,
    )


def table_lookup(selected, table):
    table_rows, lanes = table.shape
    lane = lax.broadcasted_iota(jnp.int32, (lanes, selected.shape[1]), 0)
    in_lane = jnp.where(lane == selected % lanes, 1.0, 0.0)
    candidates = exact_dot(table, in_lane)
    row = lax.broadcasted_iota(jnp.int32, candidates.shape, 0)
    return jnp.sum(jnp.where(row == selected // lanes, candidates, 0.0), axis=0, keepdims=True)


def back_substitute(s_ref, t_ref, alpha, beta, pending_ref, x_ref):
    size = x_ref.shape[0]
    rows = lax.broadcasted_iota(jnp.int32, (SUB, SUB), 0)
    cols = lax.broadcasted_iota(jnp.int32, (SUB, SUB), 1)
    groups = SUB // GROUP
    for first in range(size - SUB, -1, -SUB):
        s_small = s_ref[first : first + SUB, first : first + SUB]
        t_small = t_ref[first : first + SUB, first : first + SUB]
        s_diag = jnp.sum(jnp.where(rows == cols, s_small, 0.0), axis=1, keepdims=True)
        t_diag = jnp.sum(jnp.where(rows == cols, t_small, 0.0), axis=1, keepdims=True)
        inverse = 1.0 / (beta * s_diag - alpha * t_diag)
        s_strict = jnp.where(rows < cols, s_small, 0.0)
        t_strict = jnp.where(rows < cols, t_small, 0.0)
        pending = [
            pending_ref[first + g * GROUP : first + (g + 1) * GROUP, :] for g in range(groups)
        ]
        for column in range(SUB - 1, -1, -1):
            own, row = divmod(column, GROUP)
            right = pending[own][row : row + 1, :]
            reciprocal = inverse[column : column + 1, :]
            x_ref[first + column : first + column + 1, :] = right * reciprocal
            scaled_beta = beta * reciprocal
            scaled_alpha = alpha * reciprocal
            for g in range(own + 1):
                span = slice(g * GROUP, (g + 1) * GROUP)
                factor = (
                    s_strict[span, column : column + 1] * scaled_beta
                    - t_strict[span, column : column + 1] * scaled_alpha
                )
                pending[g] = pending[g] - factor * right
        if first:
            block = x_ref[first : first + SUB, :]
            columns = slice(first, first + SUB)
            pending_ref[:first, :] = pending_ref[:first, :] - stacked_dot(
                jnp.concatenate([s_ref[:first, columns], t_ref[:first, columns]], axis=1),
                jnp.concatenate([beta * block, -alpha * block], axis=0),
            )


def put_together(core, side, piece_refs, whole_ref):
    quarter = whole_ref.shape[0] // 4
    places = [(core, side), (core, 1 - side), (1 - core, side), (1 - core, 1 - side)]
    for ref, (half, part) in zip(piece_refs, places):
        start = (2 * half + part) * quarter
        whole_ref[pl.ds(pl.multiple_of(start, quarter), quarter), :] = ref[...]


def hand_out(core, x_ref, kept_ref, given_ref):
    half = kept_ref.shape[0]
    kept_ref[...] = x_ref[pl.ds(pl.multiple_of(core * half, half), half), :]
    given_ref[...] = x_ref[pl.ds(pl.multiple_of((1 - core) * half, half), half), :]


def lower_kernel(
    slots, me, s_ref, t_ref, r_ref, values_a, values_b, selected, kept_ref, given_ref, *refs
):
    alpha_ref, beta_ref, pending_ref, x_ref = refs
    alpha = table_lookup(selected[...], values_a[...])
    beta = table_lookup(selected[...], values_b[...])
    alpha_ref[...] = alpha
    beta_ref[...] = beta
    pending_ref[...] = r_ref[...]
    back_substitute(s_ref, t_ref, alpha, beta, pending_ref, x_ref)
    hand_out(me[0] & 1, x_ref, kept_ref, given_ref)


def upper_kernel(slots, me, s_ref, t_ref, r_ref, alpha_ref, beta_ref, *refs):
    piece_refs, (kept_ref, given_ref, lower_ref, pending_ref, x_ref) = refs[:4], refs[4:]
    block = x_ref.shape[0]
    alpha, beta = alpha_ref[...], beta_ref[...]
    put_together(me[0] & 1, (me[0] >> 1) & 1, piece_refs, lower_ref)
    lower = lower_ref[...]
    pending_ref[...] = r_ref[...] - (
        exact_dot(s_ref[:, block:], beta * lower) - exact_dot(t_ref[:, block:], alpha * lower)
    )
    back_substitute(s_ref, t_ref, alpha, beta, pending_ref, x_ref)
    hand_out(me[0] & 1, x_ref, kept_ref, given_ref)


def solve_lower(slots, me, pencil_s, pencil_t, sides, value_alpha, value_beta, selected):
    block, eigs = pencil_s.shape[1] // 2, sides.shape[1]
    count, last = sides.shape[0] // block, slots.shape[0] - 1
    lanes = 128 if value_alpha.shape[0] % 128 == 0 else value_alpha.shape[0]
    table_shape = (value_alpha.shape[0] // lanes, lanes)
    corner = pl.BlockSpec((block, block), lambda i, slots, me: (lax.rem(slots[last], count), 1))
    whole = pl.BlockSpec((block, eigs), lambda i, slots, me: (lax.rem(slots[last], count), 0))
    line = pl.BlockSpec((1, eigs), lambda i, slots, me: (0, 0))
    half = pl.BlockSpec((block // 2, eigs), lambda i, slots, me: (0, 0))
    table = pl.BlockSpec(table_shape, lambda i, slots, me: (0, 0))
    return pl.pallas_call(
        lower_kernel,
        out_shape=(
            *[jax.ShapeDtypeStruct((block // 2, eigs), jnp.float32)] * 2,
            jax.ShapeDtypeStruct((1, eigs), jnp.float32),
            jax.ShapeDtypeStruct((1, eigs), jnp.float32),
        ),
        grid_spec=pltpu.PrefetchScalarGridSpec(
            num_scalar_prefetch=2,
            grid=(1,),
            in_specs=[corner, corner, whole, table, table, line],
            out_specs=(*[half] * 2, line, line),
            scratch_shapes=[pltpu.VMEM((block, eigs), jnp.float32)] * 2,
        ),
        compiler_params=pltpu.CompilerParams(vmem_limit_bytes=FULL_VMEM_BYTES),
        cost_estimate=LIGHT,
        name="solve_lower",
    )(
        slots,
        me,
        pencil_s,
        pencil_t,
        sides,
        value_alpha.reshape(table_shape),
        value_beta.reshape(table_shape),
        selected[None, :],
    )


def solve_upper(slots, me, pencil_s, pencil_t, sides, alpha, beta, pieces):
    block, eigs = pencil_s.shape[1] // 2, sides.shape[1]
    count, index = sides.shape[0] // block, slots.shape[0] - 2
    band = pl.BlockSpec((block, 2 * block), lambda i, slots, me: (lax.rem(slots[index], count), 0))
    whole = pl.BlockSpec((block, eigs), lambda i, slots, me: (lax.rem(slots[index], count), 0))
    line = pl.BlockSpec((1, eigs), lambda i, slots, me: (0, 0))
    fixed = [pl.BlockSpec(piece.shape, lambda i, slots, me: (0, 0)) for piece in pieces]
    return pl.pallas_call(
        upper_kernel,
        out_shape=(
            *[jax.ShapeDtypeStruct((block // 2, eigs), jnp.float32)] * 2,
            jax.ShapeDtypeStruct((block, eigs), jnp.float32),
        ),
        grid_spec=pltpu.PrefetchScalarGridSpec(
            num_scalar_prefetch=2,
            grid=(1,),
            in_specs=[band, band, whole, line, line, *fixed],
            out_specs=(
                *[pl.BlockSpec((block // 2, eigs), lambda i, slots, me: (0, 0))] * 2,
                pl.BlockSpec((block, eigs), lambda i, slots, me: (0, 0)),
            ),
            scratch_shapes=[pltpu.VMEM((block, eigs), jnp.float32)] * 2,
        ),
        compiler_params=pltpu.CompilerParams(vmem_limit_bytes=FULL_VMEM_BYTES),
        cost_estimate=LIGHT,
        name="solve_upper",
    )(slots, me, pencil_s, pencil_t, sides, alpha, beta, *pieces)


def near_dot(left, right_terms):
    high, low = split_two(left)
    return jnp.dot(
        jnp.concatenate([high, low, high], axis=1), right_terms, preferred_element_type=jnp.float32
    )


def three_terms(right):
    high, low = split_two(right)
    return jnp.concatenate([high, high, low], axis=0)


def finish_kernel(slots, me, parts, r_ref, s_ref, t_ref, alpha_ref, beta_ref, lower_ref, *refs):
    piece_refs, (out_ref, terms_ref, upper_ref) = refs[:4], refs[4:]
    put_together(me[0] & 1, (me[0] >> 1) & 1, piece_refs, upper_ref)
    block = upper_ref.shape[0]
    width = block // parts.shape[0]
    for part in range(parts.shape[0]):
        rows = pl.ds(pl.multiple_of(parts[part] * width, width), width)
        for half, source in enumerate((upper_ref, lower_ref)):
            target = (2 * part + half) * width
            high, low = split_two(source[rows, :])
            for term, value in enumerate((high, high, low)):
                first = 2 * block * term + target
                terms_ref[first : first + width, :] = value
    count = out_ref.shape[0] // block
    base = me[0] * count
    alpha, beta = alpha_ref[...], beta_ref[...]
    upper, lower = upper_ref[...], lower_ref[...]
    x = jnp.concatenate([upper, lower], axis=0)
    update = near_dot(s_ref[...], three_terms(beta * x)) - near_dot(t_ref[...], three_terms(alpha * x))
    for slot in range(count):
        span = slice(slot * block, (slot + 1) * block)
        fresh = r_ref[span, :] - update[span, :]
        fresh = jnp.where(slots[slots.shape[0] - 2] == base + slot, upper, fresh)
        out_ref[span, :] = jnp.where(slots[slots.shape[0] - 1] == base + slot, lower, fresh)


def finish_sides(slots, me, parts, sides, pencil_s, pencil_t, alpha, beta, lower, pieces):
    block, eigs = lower.shape
    smem, vmem = pl.BlockSpec(memory_space=pltpu.SMEM), pl.BlockSpec(memory_space=pltpu.VMEM)
    return pl.pallas_call(
        finish_kernel,
        out_shape=(
            jax.ShapeDtypeStruct(sides.shape, jnp.float32),
            jax.ShapeDtypeStruct((6 * block, eigs), jnp.bfloat16),
        ),
        in_specs=[smem] * 3 + [vmem] * (6 + len(pieces)),
        out_specs=(vmem, vmem),
        scratch_shapes=[pltpu.VMEM((block, eigs), jnp.float32)],
        compiler_params=pltpu.CompilerParams(vmem_limit_bytes=VMEM_BYTES),
        cost_estimate=LIGHT,
        name="finish_sides",
    )(slots, me, parts, sides, pencil_s, pencil_t, alpha, beta, lower, *pieces)


def add_kernel(paired, base_ref, terms_ref, *refs):
    part_refs, out_ref = refs[: len(refs) - 1], refs[-1]
    tile = out_ref.shape[0]
    pieces = []
    for ref in part_refs:
        if paired:
            pieces.append(ref[pl.ds(0, tile, 2), :])
            pieces.append(ref[pl.ds(1, tile, 2), :])
        else:
            pieces.append(ref[...])
    basis = jnp.concatenate(pieces, axis=1)
    out_ref[...] = base_ref[...] + near_dot(basis, terms_ref[...])


def add_product(vectors, terms, parts, paired):
    rows, eigs = vectors.shape
    tile = math.gcd(TILE, rows)
    per, width = parts[0].shape[0] // rows, parts[0].shape[1]

    def stream(height, lanes):
        return pl.BlockSpec((height, lanes), lambda i: (i, 0))

    return pl.pallas_call(
        functools.partial(add_kernel, paired),
        out_shape=jax.ShapeDtypeStruct((rows, eigs), jnp.float32),
        grid=(rows // tile,),
        in_specs=[stream(tile, eigs), pl.BlockSpec(memory_space=pltpu.VMEM)]
        + [stream(per * tile, width) for _ in parts],
        out_specs=pl.BlockSpec((tile, eigs), lambda i: (i, 0)),
        compiler_params=pltpu.CompilerParams(vmem_limit_bytes=ADD_VMEM_BYTES),
        cost_estimate=LIGHT,
        name="add_product",
    )(vectors, terms, *parts)


def spread(kept, given, me, owner, axis, size):
    core, side = me & 1, (me >> 1) & 1
    if size & (size - 1) or size < 4:
        parts = [jnp.where(core == 0, kept, given), jnp.where(core == 0, given, kept)]
        block = jnp.concatenate(parts, axis=0)
        block = lax.psum(jnp.where(me == owner, block, jnp.zeros_like(block)), axis)
        quarter = block.shape[0] // 4
        places = [(core, side), (core, 1 - side), (1 - core, side), (1 - core, 1 - side)]
        return [
            lax.dynamic_slice_in_dim(block, (2 * first + second) * quarter, quarter, 0)
            for first, second in places
        ]

    def exchange(value, bit):
        return lax.ppermute(value, axis, [(i, i ^ bit) for i in range(size)])

    apart = me ^ owner
    kept = jnp.where(apart == 0, kept, exchange(given, 1))
    middle = kept.shape[0] // 2
    first, second = kept[:middle], kept[middle:]
    kept, given = jnp.where(side == 0, first, second), jnp.where(side == 0, second, first)
    kept = jnp.where(apart < 2, kept, exchange(given, 2))
    bit = 4
    while bit < size:
        kept = jnp.where(apart < bit, kept, exchange(kept, bit))
        bit *= 2
    return [kept] + [exchange(kept, bits) for bits in (2, 1, 3)]


def on_device(
    row_size,
    col_size,
    right_sides,
    pencil_s,
    pencil_t,
    value_alpha,
    value_beta,
    selected,
    block_slot,
    right_basis,
    vectors,
):
    block = pencil_s.shape[1] // 2
    slot_count = right_sides.shape[0] // block
    block_count = block_slot.shape[0]
    rows, _, width = right_basis.shape
    me_row = lax.axis_index("row")
    me_col = lax.axis_index("col")
    slot_upper = block_slot[block_count - 2]
    slot_lower = block_slot[block_count - 1]

    paired = width % 128 == 0
    own = right_basis.reshape((2 * rows, width) if paired else (rows, 2 * width))
    received = [
        lax.ppermute(own, "col", [(i, (i + step) % col_size) for i in range(col_size)])
        for step in range(1, col_size)
    ]
    me = me_row[None]
    parts = jnp.stack([lax.rem(me_col + (col_size - step), col_size) for step in range(col_size)])
    owner_lower, owner_upper = lax.div(slot_lower, slot_count), lax.div(slot_upper, slot_count)
    kept, given, alpha, beta = solve_lower(
        block_slot, me, pencil_s, pencil_t, right_sides, value_alpha, value_beta, selected
    )
    lower = spread(kept, given, me_row, owner_lower, "row", row_size)
    kept, given, lower = solve_upper(
        block_slot, me, pencil_s, pencil_t, right_sides, alpha, beta, lower
    )
    upper = spread(kept, given, me_row, owner_upper, "row", row_size)
    updated_sides, terms = finish_sides(
        block_slot, me, parts, right_sides, pencil_s, pencil_t, alpha, beta, lower, upper
    )
    updated_vectors = add_product(vectors, terms, [own, *received], paired)
    return (updated_sides, updated_vectors)


def solution(mesh):
    body = functools.partial(on_device, mesh.shape["row"], mesh.shape["col"])
    return jax.shard_map(
        body,
        mesh=mesh,
        in_specs=(
            P("row", "col"),
            P("row", None),
            P("row", None),
            P(),
            P(),
            P("col"),
            P(),
            P("row", None, "col"),
            P("row", "col"),
        ),
        out_specs=(P("row", "col"), P("row", "col")),
        check_vma=False,
    )
```

```python
import functools
import math

import jax
import jax.numpy as jnp
from jax import lax
from jax.experimental import pallas as pl
from jax.experimental.pallas import tpu as pltpu
from jax.sharding import PartitionSpec as P

SUB = 32
GROUP = 8
VMEM_BYTES = 48 * 1024 * 1024
ADD_VMEM_BYTES = 48 * 1024 * 1024
FULL_VMEM_BYTES = 59 * 1024 * 1024
TILE = 1024
LIGHT = pl.CostEstimate(flops=1000, bytes_accessed=1000, transcendentals=0)


def exact_dot(left, right):
    return jnp.dot(left, right, precision=lax.Precision.HIGHEST, preferred_element_type=jnp.float32)


def split_two(value):
    high = value.astype(jnp.bfloat16)
    low = (value - high.astype(jnp.float32)).astype(jnp.bfloat16)
    return high, low


def split_three(value):
    high = value.astype(jnp.bfloat16)
    rest = value - high.astype(jnp.float32)
    middle = rest.astype(jnp.bfloat16)
    low = (rest - middle.astype(jnp.float32)).astype(jnp.bfloat16)
    return high, middle, low


def stacked_dot(left, right):
    high, middle, low = split_three(left)
    top, mid, end = split_three(right)
    return jnp.dot(
        jnp.concatenate([high, middle, high, middle, high, low], axis=1),
        jnp.concatenate([top, top, mid, mid, end, top], axis=0),
        preferred_element_type=jnp.float32,
    )


def table_lookup(selected, table):
    table_rows, lanes = table.shape
    lane = lax.broadcasted_iota(jnp.int32, (lanes, selected.shape[1]), 0)
    in_lane = jnp.where(lane == selected % lanes, 1.0, 0.0)
    candidates = exact_dot(table, in_lane)
    row = lax.broadcasted_iota(jnp.int32, candidates.shape, 0)
    return jnp.sum(jnp.where(row == selected // lanes, candidates, 0.0), axis=0, keepdims=True)


def back_substitute(s_ref, t_ref, alpha, beta, pending_ref, x_ref):
    size = x_ref.shape[0]
    rows = lax.broadcasted_iota(jnp.int32, (SUB, SUB), 0)
    cols = lax.broadcasted_iota(jnp.int32, (SUB, SUB), 1)
    groups = SUB // GROUP
    for first in range(size - SUB, -1, -SUB):
        s_small = s_ref[first : first + SUB, first : first + SUB]
        t_small = t_ref[first : first + SUB, first : first + SUB]
        s_diag = jnp.sum(jnp.where(rows == cols, s_small, 0.0), axis=1, keepdims=True)
        t_diag = jnp.sum(jnp.where(rows == cols, t_small, 0.0), axis=1, keepdims=True)
        inverse = 1.0 / (beta * s_diag - alpha * t_diag)
        s_strict = jnp.where(rows < cols, s_small, 0.0)
        t_strict = jnp.where(rows < cols, t_small, 0.0)
        pending = [
            pending_ref[first + g * GROUP : first + (g + 1) * GROUP, :] for g in range(groups)
        ]
        for column in range(SUB - 1, -1, -1):
            own, row = divmod(column, GROUP)
            right = pending[own][row : row + 1, :]
            reciprocal = inverse[column : column + 1, :]
            x_ref[first + column : first + column + 1, :] = right * reciprocal
            scaled_beta = beta * reciprocal
            scaled_alpha = alpha * reciprocal
            for g in range(own + 1):
                span = slice(g * GROUP, (g + 1) * GROUP)
                factor = (
                    s_strict[span, column : column + 1] * scaled_beta
                    - t_strict[span, column : column + 1] * scaled_alpha
                )
                pending[g] = pending[g] - factor * right
        if first:
            block = x_ref[first : first + SUB, :]
            columns = slice(first, first + SUB)
            pending_ref[:first, :] = pending_ref[:first, :] - stacked_dot(
                jnp.concatenate([s_ref[:first, columns], t_ref[:first, columns]], axis=1),
                jnp.concatenate([beta * block, -alpha * block], axis=0),
            )


def put_together(core, side, piece_refs, whole_ref):
    quarter = whole_ref.shape[0] // 4
    places = [(core, side), (core, 1 - side), (1 - core, side), (1 - core, 1 - side)]
    for ref, (half, part) in zip(piece_refs, places):
        start = (2 * half + part) * quarter
        whole_ref[pl.ds(pl.multiple_of(start, quarter), quarter), :] = ref[...]


def hand_out(core, x_ref, kept_ref, given_ref):
    half = kept_ref.shape[0]
    kept_ref[...] = x_ref[pl.ds(pl.multiple_of(core * half, half), half), :]
    given_ref[...] = x_ref[pl.ds(pl.multiple_of((1 - core) * half, half), half), :]


def lower_kernel(
    slots, me, s_ref, t_ref, r_ref, values_a, values_b, selected, kept_ref, given_ref, *refs
):
    alpha_ref, beta_ref, pending_ref, x_ref = refs
    alpha = table_lookup(selected[...], values_a[...])
    beta = table_lookup(selected[...], values_b[...])
    alpha_ref[...] = alpha
    beta_ref[...] = beta
    pending_ref[...] = r_ref[...]
    back_substitute(s_ref, t_ref, alpha, beta, pending_ref, x_ref)
    hand_out(me[0] & 1, x_ref, kept_ref, given_ref)


def upper_kernel(slots, me, s_ref, t_ref, r_ref, alpha_ref, beta_ref, *refs):
    piece_refs, (kept_ref, given_ref, lower_ref, pending_ref, x_ref) = refs[:4], refs[4:]
    block = x_ref.shape[0]
    alpha, beta = alpha_ref[...], beta_ref[...]
    put_together(me[0] & 1, (me[0] >> 1) & 1, piece_refs, lower_ref)
    lower = lower_ref[...]
    pending_ref[...] = r_ref[...] - (
        exact_dot(s_ref[:, block:], beta * lower) - exact_dot(t_ref[:, block:], alpha * lower)
    )
    back_substitute(s_ref, t_ref, alpha, beta, pending_ref, x_ref)
    hand_out(me[0] & 1, x_ref, kept_ref, given_ref)


def solve_lower(slots, me, pencil_s, pencil_t, sides, value_alpha, value_beta, selected):
    block, eigs = pencil_s.shape[1] // 2, sides.shape[1]
    count, last = sides.shape[0] // block, slots.shape[0] - 1
    lanes = 128 if value_alpha.shape[0] % 128 == 0 else value_alpha.shape[0]
    table_shape = (value_alpha.shape[0] // lanes, lanes)
    corner = pl.BlockSpec((block, block), lambda i, slots, me: (lax.rem(slots[last], count), 1))
    whole = pl.BlockSpec((block, eigs), lambda i, slots, me: (lax.rem(slots[last], count), 0))
    line = pl.BlockSpec((1, eigs), lambda i, slots, me: (0, 0))
    half = pl.BlockSpec((block // 2, eigs), lambda i, slots, me: (0, 0))
    table = pl.BlockSpec(table_shape, lambda i, slots, me: (0, 0))
    return pl.pallas_call(
        lower_kernel,
        out_shape=(
            *[jax.ShapeDtypeStruct((block // 2, eigs), jnp.float32)] * 2,
            jax.ShapeDtypeStruct((1, eigs), jnp.float32),
            jax.ShapeDtypeStruct((1, eigs), jnp.float32),
        ),
        grid_spec=pltpu.PrefetchScalarGridSpec(
            num_scalar_prefetch=2,
            grid=(1,),
            in_specs=[corner, corner, whole, table, table, line],
            out_specs=(*[half] * 2, line, line),
            scratch_shapes=[pltpu.VMEM((block, eigs), jnp.float32)] * 2,
        ),
        compiler_params=pltpu.CompilerParams(vmem_limit_bytes=FULL_VMEM_BYTES),
        cost_estimate=LIGHT,
        name="solve_lower",
    )(
        slots,
        me,
        pencil_s,
        pencil_t,
        sides,
        value_alpha.reshape(table_shape),
        value_beta.reshape(table_shape),
        selected[None, :],
    )


def solve_upper(slots, me, pencil_s, pencil_t, sides, alpha, beta, pieces):
    block, eigs = pencil_s.shape[1] // 2, sides.shape[1]
    count, index = sides.shape[0] // block, slots.shape[0] - 2
    band = pl.BlockSpec((block, 2 * block), lambda i, slots, me: (lax.rem(slots[index], count), 0))
    whole = pl.BlockSpec((block, eigs), lambda i, slots, me: (lax.rem(slots[index], count), 0))
    line = pl.BlockSpec((1, eigs), lambda i, slots, me: (0, 0))
    fixed = [pl.BlockSpec(piece.shape, lambda i, slots, me: (0, 0)) for piece in pieces]
    return pl.pallas_call(
        upper_kernel,
        out_shape=(
            *[jax.ShapeDtypeStruct((block // 2, eigs), jnp.float32)] * 2,
            jax.ShapeDtypeStruct((block, eigs), jnp.float32),
        ),
        grid_spec=pltpu.PrefetchScalarGridSpec(
            num_scalar_prefetch=2,
            grid=(1,),
            in_specs=[band, band, whole, line, line, *fixed],
            out_specs=(
                *[pl.BlockSpec((block // 2, eigs), lambda i, slots, me: (0, 0))] * 2,
                pl.BlockSpec((block, eigs), lambda i, slots, me: (0, 0)),
            ),
            scratch_shapes=[pltpu.VMEM((block, eigs), jnp.float32)] * 2,
        ),
        compiler_params=pltpu.CompilerParams(vmem_limit_bytes=FULL_VMEM_BYTES),
        cost_estimate=LIGHT,
        name="solve_upper",
    )(slots, me, pencil_s, pencil_t, sides, alpha, beta, *pieces)


def near_dot(left, right_terms):
    high, low = split_two(left)
    return jnp.dot(
        jnp.concatenate([high, low, high], axis=1), right_terms, preferred_element_type=jnp.float32
    )


def three_terms(right):
    high, low = split_two(right)
    return jnp.concatenate([high, high, low], axis=0)


def finish_kernel(slots, me, parts, r_ref, s_ref, t_ref, alpha_ref, beta_ref, lower_ref, *refs):
    piece_refs, (out_ref, terms_ref, upper_ref) = refs[:4], refs[4:]
    put_together(me[0] & 1, (me[0] >> 1) & 1, piece_refs, upper_ref)
    block = upper_ref.shape[0]
    width = block // parts.shape[0]
    for part in range(parts.shape[0]):
        rows = pl.ds(pl.multiple_of(parts[part] * width, width), width)
        for half, source in enumerate((upper_ref, lower_ref)):
            target = (2 * part + half) * width
            high, low = split_two(source[rows, :])
            for term, value in enumerate((high, high, low)):
                first = 2 * block * term + target
                terms_ref[first : first + width, :] = value
    count = out_ref.shape[0] // block
    base = me[0] * count
    alpha, beta = alpha_ref[...], beta_ref[...]
    upper, lower = upper_ref[...], lower_ref[...]
    x = jnp.concatenate([upper, lower], axis=0)
    update = near_dot(s_ref[...], three_terms(beta * x)) - near_dot(t_ref[...], three_terms(alpha * x))
    for slot in range(count):
        span = slice(slot * block, (slot + 1) * block)
        fresh = r_ref[span, :] - update[span, :]
        fresh = jnp.where(slots[slots.shape[0] - 2] == base + slot, upper, fresh)
        out_ref[span, :] = jnp.where(slots[slots.shape[0] - 1] == base + slot, lower, fresh)


def finish_sides(slots, me, parts, sides, pencil_s, pencil_t, alpha, beta, lower, pieces):
    block, eigs = lower.shape
    smem, vmem = pl.BlockSpec(memory_space=pltpu.SMEM), pl.BlockSpec(memory_space=pltpu.VMEM)
    return pl.pallas_call(
        finish_kernel,
        out_shape=(
            jax.ShapeDtypeStruct(sides.shape, jnp.float32),
            jax.ShapeDtypeStruct((6 * block, eigs), jnp.bfloat16),
        ),
        in_specs=[smem] * 3 + [vmem] * (6 + len(pieces)),
        out_specs=(vmem, vmem),
        scratch_shapes=[pltpu.VMEM((block, eigs), jnp.float32)],
        compiler_params=pltpu.CompilerParams(vmem_limit_bytes=VMEM_BYTES),
        cost_estimate=LIGHT,
        name="finish_sides",
    )(slots, me, parts, sides, pencil_s, pencil_t, alpha, beta, lower, *pieces)


def add_kernel(paired, base_ref, terms_ref, *refs):
    part_refs, out_ref = refs[: len(refs) - 1], refs[-1]
    tile = out_ref.shape[0]
    pieces = []
    for ref in part_refs:
        if paired:
            pieces.append(ref[pl.ds(0, tile, 2), :])
            pieces.append(ref[pl.ds(1, tile, 2), :])
        else:
            pieces.append(ref[...])
    basis = jnp.concatenate(pieces, axis=1)
    out_ref[...] = base_ref[...] + near_dot(basis, terms_ref[...])


def add_product(vectors, terms, parts, paired):
    rows, eigs = vectors.shape
    tile = math.gcd(TILE, rows)
    per, width = parts[0].shape[0] // rows, parts[0].shape[1]

    def stream(height, lanes):
        return pl.BlockSpec((height, lanes), lambda i: (i, 0))

    return pl.pallas_call(
        functools.partial(add_kernel, paired),
        out_shape=jax.ShapeDtypeStruct((rows, eigs), jnp.float32),
        grid=(rows // tile,),
        in_specs=[stream(tile, eigs), pl.BlockSpec(memory_space=pltpu.VMEM)]
        + [stream(per * tile, width) for _ in parts],
        out_specs=pl.BlockSpec((tile, eigs), lambda i: (i, 0)),
        compiler_params=pltpu.CompilerParams(vmem_limit_bytes=ADD_VMEM_BYTES),
        cost_estimate=LIGHT,
        name="add_product",
    )(vectors, terms, *parts)


def spread(kept, given, me, owner, axis, size):
    core, side = me & 1, (me >> 1) & 1
    if size & (size - 1) or size < 4:
        parts = [jnp.where(core == 0, kept, given), jnp.where(core == 0, given, kept)]
        block = jnp.concatenate(parts, axis=0)
        block = lax.psum(jnp.where(me == owner, block, jnp.zeros_like(block)), axis)
        quarter = block.shape[0] // 4
        places = [(core, side), (core, 1 - side), (1 - core, side), (1 - core, 1 - side)]
        return [
            lax.dynamic_slice_in_dim(block, (2 * first + second) * quarter, quarter, 0)
            for first, second in places
        ]

    def exchange(value, bit):
        return lax.ppermute(value, axis, [(i, i ^ bit) for i in range(size)])

    apart = me ^ owner
    kept = jnp.where(apart == 0, kept, exchange(given, 1))
    middle = kept.shape[0] // 2
    first, second = kept[:middle], kept[middle:]
    kept, given = jnp.where(side == 0, first, second), jnp.where(side == 0, second, first)
    kept = jnp.where(apart < 2, kept, exchange(given, 2))
    bit = 4
    while bit < size:
        kept = jnp.where(apart < bit, kept, exchange(kept, bit))
        bit *= 2
    return [kept] + [exchange(kept, bits) for bits in (2, 1, 3)]


def on_device(
    row_size,
    col_size,
    right_sides,
    pencil_s,
    pencil_t,
    value_alpha,
    value_beta,
    selected,
    block_slot,
    right_basis,
    vectors,
):
    block = pencil_s.shape[1] // 2
    slot_count = right_sides.shape[0] // block
    block_count = block_slot.shape[0]
    rows, _, width = right_basis.shape
    me_row = lax.axis_index("row")
    me_col = lax.axis_index("col")
    slot_upper = block_slot[block_count - 2]
    slot_lower = block_slot[block_count - 1]

    paired = width % 128 == 0
    own = right_basis.reshape((2 * rows, width) if paired else (rows, 2 * width))
    received = [
        lax.ppermute(own, "col", [(i, (i + step) % col_size) for i in range(col_size)])
        for step in range(1, col_size)
    ]
    me = me_row[None]
    parts = jnp.stack([lax.rem(me_col + (col_size - step), col_size) for step in range(col_size)])
    owner_lower, owner_upper = lax.div(slot_lower, slot_count), lax.div(slot_upper, slot_count)
    kept, given, alpha, beta = solve_lower(
        block_slot, me, pencil_s, pencil_t, right_sides, value_alpha, value_beta, selected
    )
    lower = spread(kept, given, me_row, owner_lower, "row", row_size)
    kept, given, lower = solve_upper(
        block_slot, me, pencil_s, pencil_t, right_sides, alpha, beta, lower
    )
    upper = spread(kept, given, me_row, owner_upper, "row", row_size)
    updated_sides, terms = finish_sides(
        block_slot, me, parts, right_sides, pencil_s, pencil_t, alpha, beta, lower, upper
    )
    updated_vectors = add_product(vectors, terms, [own, *received], paired)
    return (updated_sides, updated_vectors)


def solution(mesh):
    body = functools.partial(on_device, mesh.shape["row"], mesh.shape["col"])
    return jax.shard_map(
        body,
        mesh=mesh,
        in_specs=(
            P("row", "col"),
            P("row", None),
            P("row", None),
            P(),
            P(),
            P("col"),
            P(),
            P("row", None, "col"),
            P("row", "col"),
        ),
        out_specs=(P("row", "col"), P("row", "col")),
        check_vma=False,
    )
```

```python
import functools
import math

import jax
import jax.numpy as jnp
from jax import lax
from jax.experimental import pallas as pl
from jax.experimental.pallas import tpu as pltpu
from jax.sharding import PartitionSpec as P

SUB = 32
GROUP = 8
VMEM_BYTES = 48 * 1024 * 1024
ADD_VMEM_BYTES = 48 * 1024 * 1024
FULL_VMEM_BYTES = 59 * 1024 * 1024
TILE = 1024
LIGHT = pl.CostEstimate(flops=1000, bytes_accessed=1000, transcendentals=0)


def exact_dot(left, right):
    return jnp.dot(left, right, precision=lax.Precision.HIGHEST, preferred_element_type=jnp.float32)


def split_two(value):
    high = value.astype(jnp.bfloat16)
    low = (value - high.astype(jnp.float32)).astype(jnp.bfloat16)
    return high, low


def split_three(value):
    high = value.astype(jnp.bfloat16)
    rest = value - high.astype(jnp.float32)
    middle = rest.astype(jnp.bfloat16)
    low = (rest - middle.astype(jnp.float32)).astype(jnp.bfloat16)
    return high, middle, low


def stacked_dot(left, right):
    high, middle, low = split_three(left)
    top, mid, end = split_three(right)
    return jnp.dot(
        jnp.concatenate([high, middle, high, middle, high, low], axis=1),
        jnp.concatenate([top, top, mid, mid, end, top], axis=0),
        preferred_element_type=jnp.float32,
    )


def table_lookup(selected, table):
    table_rows, lanes = table.shape
    lane = lax.broadcasted_iota(jnp.int32, (lanes, selected.shape[1]), 0)
    in_lane = jnp.where(lane == selected % lanes, 1.0, 0.0)
    candidates = exact_dot(table, in_lane)
    row = lax.broadcasted_iota(jnp.int32, candidates.shape, 0)
    return jnp.sum(jnp.where(row == selected // lanes, candidates, 0.0), axis=0, keepdims=True)


def back_substitute(s_ref, t_ref, alpha, beta, pending_ref, x_ref):
    size = x_ref.shape[0]
    rows = lax.broadcasted_iota(jnp.int32, (SUB, SUB), 0)
    cols = lax.broadcasted_iota(jnp.int32, (SUB, SUB), 1)
    groups = SUB // GROUP
    for first in range(size - SUB, -1, -SUB):
        s_small = s_ref[first : first + SUB, first : first + SUB]
        t_small = t_ref[first : first + SUB, first : first + SUB]
        s_diag = jnp.sum(jnp.where(rows == cols, s_small, 0.0), axis=1, keepdims=True)
        t_diag = jnp.sum(jnp.where(rows == cols, t_small, 0.0), axis=1, keepdims=True)
        inverse = 1.0 / (beta * s_diag - alpha * t_diag)
        s_strict = jnp.where(rows < cols, s_small, 0.0)
        t_strict = jnp.where(rows < cols, t_small, 0.0)
        pending = [
            pending_ref[first + g * GROUP : first + (g + 1) * GROUP, :] for g in range(groups)
        ]
        for column in range(SUB - 1, -1, -1):
            own, row = divmod(column, GROUP)
            right = pending[own][row : row + 1, :]
            reciprocal = inverse[column : column + 1, :]
            x_ref[first + column : first + column + 1, :] = right * reciprocal
            scaled_beta = beta * reciprocal
            scaled_alpha = alpha * reciprocal
            for g in range(own + 1):
                span = slice(g * GROUP, (g + 1) * GROUP)
                factor = (
                    s_strict[span, column : column + 1] * scaled_beta
                    - t_strict[span, column : column + 1] * scaled_alpha
                )
                pending[g] = pending[g] - factor * right
        if first:
            block = x_ref[first : first + SUB, :]
            columns = slice(first, first + SUB)
            pending_ref[:first, :] = pending_ref[:first, :] - stacked_dot(
                jnp.concatenate([s_ref[:first, columns], t_ref[:first, columns]], axis=1),
                jnp.concatenate([beta * block, -alpha * block], axis=0),
            )


def put_together(core, side, piece_refs, whole_ref):
    quarter = whole_ref.shape[0] // 4
    places = [(core, side), (core, 1 - side), (1 - core, side), (1 - core, 1 - side)]
    for ref, (half, part) in zip(piece_refs, places):
        start = (2 * half + part) * quarter
        whole_ref[pl.ds(pl.multiple_of(start, quarter), quarter), :] = ref[...]


def hand_out(core, x_ref, kept_ref, given_ref):
    half = kept_ref.shape[0]
    kept_ref[...] = x_ref[pl.ds(pl.multiple_of(core * half, half), half), :]
    given_ref[...] = x_ref[pl.ds(pl.multiple_of((1 - core) * half, half), half), :]


def lower_kernel(
    slots, me, s_ref, t_ref, r_ref, values_a, values_b, selected, kept_ref, given_ref, *refs
):
    alpha_ref, beta_ref, pending_ref, x_ref = refs
    alpha = table_lookup(selected[...], values_a[...])
    beta = table_lookup(selected[...], values_b[...])
    alpha_ref[...] = alpha
    beta_ref[...] = beta
    pending_ref[...] = r_ref[...]
    back_substitute(s_ref, t_ref, alpha, beta, pending_ref, x_ref)
    hand_out(me[0] & 1, x_ref, kept_ref, given_ref)


def upper_kernel(slots, me, s_ref, t_ref, r_ref, alpha_ref, beta_ref, *refs):
    piece_refs, (kept_ref, given_ref, lower_ref, pending_ref, x_ref) = refs[:4], refs[4:]
    block = x_ref.shape[0]
    alpha, beta = alpha_ref[...], beta_ref[...]
    put_together(me[0] & 1, (me[0] >> 1) & 1, piece_refs, lower_ref)
    lower = lower_ref[...]
    pending_ref[...] = r_ref[...] - (
        exact_dot(s_ref[:, block:], beta * lower) - exact_dot(t_ref[:, block:], alpha * lower)
    )
    back_substitute(s_ref, t_ref, alpha, beta, pending_ref, x_ref)
    hand_out(me[0] & 1, x_ref, kept_ref, given_ref)


def solve_lower(slots, me, pencil_s, pencil_t, sides, value_alpha, value_beta, selected):
    block, eigs = pencil_s.shape[1] // 2, sides.shape[1]
    count, last = sides.shape[0] // block, slots.shape[0] - 1
    lanes = 128 if value_alpha.shape[0] % 128 == 0 else value_alpha.shape[0]
    table_shape = (value_alpha.shape[0] // lanes, lanes)
    corner = pl.BlockSpec((block, block), lambda i, slots, me: (lax.rem(slots[last], count), 1))
    whole = pl.BlockSpec((block, eigs), lambda i, slots, me: (lax.rem(slots[last], count), 0))
    line = pl.BlockSpec((1, eigs), lambda i, slots, me: (0, 0))
    half = pl.BlockSpec((block // 2, eigs), lambda i, slots, me: (0, 0))
    table = pl.BlockSpec(table_shape, lambda i, slots, me: (0, 0))
    return pl.pallas_call(
        lower_kernel,
        out_shape=(
            *[jax.ShapeDtypeStruct((block // 2, eigs), jnp.float32)] * 2,
            jax.ShapeDtypeStruct((1, eigs), jnp.float32),
            jax.ShapeDtypeStruct((1, eigs), jnp.float32),
        ),
        grid_spec=pltpu.PrefetchScalarGridSpec(
            num_scalar_prefetch=2,
            grid=(1,),
            in_specs=[corner, corner, whole, table, table, line],
            out_specs=(*[half] * 2, line, line),
            scratch_shapes=[pltpu.VMEM((block, eigs), jnp.float32)] * 2,
        ),
        compiler_params=pltpu.CompilerParams(vmem_limit_bytes=FULL_VMEM_BYTES),
        cost_estimate=LIGHT,
        name="solve_lower",
    )(
        slots,
        me,
        pencil_s,
        pencil_t,
        sides,
        value_alpha.reshape(table_shape),
        value_beta.reshape(table_shape),
        selected[None, :],
    )


def solve_upper(slots, me, pencil_s, pencil_t, sides, alpha, beta, pieces):
    block, eigs = pencil_s.shape[1] // 2, sides.shape[1]
    count, index = sides.shape[0] // block, slots.shape[0] - 2
    band = pl.BlockSpec((block, 2 * block), lambda i, slots, me: (lax.rem(slots[index], count), 0))
    whole = pl.BlockSpec((block, eigs), lambda i, slots, me: (lax.rem(slots[index], count), 0))
    line = pl.BlockSpec((1, eigs), lambda i, slots, me: (0, 0))
    fixed = [pl.BlockSpec(piece.shape, lambda i, slots, me: (0, 0)) for piece in pieces]
    return pl.pallas_call(
        upper_kernel,
        out_shape=(
            *[jax.ShapeDtypeStruct((block // 2, eigs), jnp.float32)] * 2,
            jax.ShapeDtypeStruct((block, eigs), jnp.float32),
        ),
        grid_spec=pltpu.PrefetchScalarGridSpec(
            num_scalar_prefetch=2,
            grid=(1,),
            in_specs=[band, band, whole, line, line, *fixed],
            out_specs=(
                *[pl.BlockSpec((block // 2, eigs), lambda i, slots, me: (0, 0))] * 2,
                pl.BlockSpec((block, eigs), lambda i, slots, me: (0, 0)),
            ),
            scratch_shapes=[pltpu.VMEM((block, eigs), jnp.float32)] * 2,
        ),
        compiler_params=pltpu.CompilerParams(vmem_limit_bytes=FULL_VMEM_BYTES),
        cost_estimate=LIGHT,
        name="solve_upper",
    )(slots, me, pencil_s, pencil_t, sides, alpha, beta, *pieces)


def near_dot(left, right_terms):
    high, low = split_two(left)
    return jnp.dot(
        jnp.concatenate([high, low, high], axis=1), right_terms, preferred_element_type=jnp.float32
    )


def three_terms(right):
    high, low = split_two(right)
    return jnp.concatenate([high, high, low], axis=0)


def finish_kernel(slots, me, parts, r_ref, s_ref, t_ref, alpha_ref, beta_ref, lower_ref, *refs):
    piece_refs, (out_ref, terms_ref, upper_ref) = refs[:4], refs[4:]
    put_together(me[0] & 1, (me[0] >> 1) & 1, piece_refs, upper_ref)
    block = upper_ref.shape[0]
    width = block // parts.shape[0]
    for part in range(parts.shape[0]):
        rows = pl.ds(pl.multiple_of(parts[part] * width, width), width)
        for half, source in enumerate((upper_ref, lower_ref)):
            target = (2 * part + half) * width
            high, low = split_two(source[rows, :])
            for term, value in enumerate((high, high, low)):
                first = 2 * block * term + target
                terms_ref[first : first + width, :] = value
    count = out_ref.shape[0] // block
    base = me[0] * count
    alpha, beta = alpha_ref[...], beta_ref[...]
    upper, lower = upper_ref[...], lower_ref[...]
    x = jnp.concatenate([upper, lower], axis=0)
    update = near_dot(s_ref[...], three_terms(beta * x)) - near_dot(t_ref[...], three_terms(alpha * x))
    for slot in range(count):
        span = slice(slot * block, (slot + 1) * block)
        fresh = r_ref[span, :] - update[span, :]
        fresh = jnp.where(slots[slots.shape[0] - 2] == base + slot, upper, fresh)
        out_ref[span, :] = jnp.where(slots[slots.shape[0] - 1] == base + slot, lower, fresh)


def finish_sides(slots, me, parts, sides, pencil_s, pencil_t, alpha, beta, lower, pieces):
    block, eigs = lower.shape
    smem, vmem = pl.BlockSpec(memory_space=pltpu.SMEM), pl.BlockSpec(memory_space=pltpu.VMEM)
    return pl.pallas_call(
        finish_kernel,
        out_shape=(
            jax.ShapeDtypeStruct(sides.shape, jnp.float32),
            jax.ShapeDtypeStruct((6 * block, eigs), jnp.bfloat16),
        ),
        in_specs=[smem] * 3 + [vmem] * (6 + len(pieces)),
        out_specs=(vmem, vmem),
        scratch_shapes=[pltpu.VMEM((block, eigs), jnp.float32)],
        compiler_params=pltpu.CompilerParams(vmem_limit_bytes=VMEM_BYTES),
        cost_estimate=LIGHT,
        name="finish_sides",
    )(slots, me, parts, sides, pencil_s, pencil_t, alpha, beta, lower, *pieces)


def add_kernel(paired, vectors_ref, terms_ref, *refs):
    part_refs, (out_ref, base_ref, done) = refs[:-3], refs[-3:]
    tile = out_ref.shape[0]
    first = pl.multiple_of(pl.program_id(0) * tile, tile)
    load = pltpu.make_async_copy(vectors_ref.at[pl.ds(first, tile)], base_ref, done)
    load.start()
    if paired:
        pieces = [ref[pl.ds(half, tile, 2), :] for ref in part_refs for half in range(2)]
    else:
        pieces = [ref[...] for ref in part_refs]
    product = near_dot(jnp.concatenate(pieces, axis=1), terms_ref[...])
    load.wait()
    out_ref[...] = base_ref[...] + product


def add_product(vectors, terms, parts, paired):
    rows, eigs = vectors.shape
    tile = math.gcd(TILE, rows)
    per, width = parts[0].shape[0] // rows, parts[0].shape[1]

    def stream(height, lanes):
        return pl.BlockSpec((height, lanes), lambda i: (i, 0))

    return pl.pallas_call(
        functools.partial(add_kernel, paired),
        out_shape=jax.ShapeDtypeStruct((rows, eigs), jnp.float32),
        grid=(rows // tile,),
        in_specs=[pl.BlockSpec(memory_space=pl.ANY), pl.BlockSpec(memory_space=pltpu.VMEM)]
        + [stream(per * tile, width) for _ in parts],
        out_specs=pl.BlockSpec((tile, eigs), lambda i: (i, 0)),
        scratch_shapes=[pltpu.VMEM((tile, eigs), jnp.float32), pltpu.SemaphoreType.DMA],
        compiler_params=pltpu.CompilerParams(vmem_limit_bytes=ADD_VMEM_BYTES),
        cost_estimate=LIGHT,
        name="add_product",
    )(vectors, terms, *parts)


def spread(kept, given, me, owner, axis, size):
    core, side = me & 1, (me >> 1) & 1
    if size & (size - 1) or size < 4:
        parts = [jnp.where(core == 0, kept, given), jnp.where(core == 0, given, kept)]
        block = jnp.concatenate(parts, axis=0)
        block = lax.psum(jnp.where(me == owner, block, jnp.zeros_like(block)), axis)
        quarter = block.shape[0] // 4
        places = [(core, side), (core, 1 - side), (1 - core, side), (1 - core, 1 - side)]
        return [
            lax.dynamic_slice_in_dim(block, (2 * first + second) * quarter, quarter, 0)
            for first, second in places
        ]

    def exchange(value, bit):
        return lax.ppermute(value, axis, [(i, i ^ bit) for i in range(size)])

    apart = me ^ owner
    kept = jnp.where(apart == 0, kept, exchange(given, 1))
    middle = kept.shape[0] // 2
    first, second = kept[:middle], kept[middle:]
    kept, given = jnp.where(side == 0, first, second), jnp.where(side == 0, second, first)
    kept = jnp.where(apart < 2, kept, exchange(given, 2))
    bit = 4
    while bit < size:
        kept = jnp.where(apart < bit, kept, exchange(kept, bit))
        bit *= 2
    return [kept] + [exchange(kept, bits) for bits in (2, 1, 3)]


def on_device(
    row_size,
    col_size,
    right_sides,
    pencil_s,
    pencil_t,
    value_alpha,
    value_beta,
    selected,
    block_slot,
    right_basis,
    vectors,
):
    block = pencil_s.shape[1] // 2
    slot_count = right_sides.shape[0] // block
    block_count = block_slot.shape[0]
    rows, _, width = right_basis.shape
    me_row = lax.axis_index("row")
    me_col = lax.axis_index("col")
    slot_upper = block_slot[block_count - 2]
    slot_lower = block_slot[block_count - 1]

    paired = width % 128 == 0
    own = right_basis.reshape((2 * rows, width) if paired else (rows, 2 * width))
    received = [
        lax.ppermute(own, "col", [(i, (i + step) % col_size) for i in range(col_size)])
        for step in range(1, col_size)
    ]
    me = me_row[None]
    parts = jnp.stack([lax.rem(me_col + (col_size - step), col_size) for step in range(col_size)])
    owner_lower, owner_upper = lax.div(slot_lower, slot_count), lax.div(slot_upper, slot_count)
    kept, given, alpha, beta = solve_lower(
        block_slot, me, pencil_s, pencil_t, right_sides, value_alpha, value_beta, selected
    )
    lower = spread(kept, given, me_row, owner_lower, "row", row_size)
    kept, given, lower = solve_upper(
        block_slot, me, pencil_s, pencil_t, right_sides, alpha, beta, lower
    )
    upper = spread(kept, given, me_row, owner_upper, "row", row_size)
    updated_sides, terms = finish_sides(
        block_slot, me, parts, right_sides, pencil_s, pencil_t, alpha, beta, lower, upper
    )
    updated_vectors = add_product(vectors, terms, [own, *received], paired)
    return (updated_sides, updated_vectors)


def solution(mesh):
    body = functools.partial(on_device, mesh.shape["row"], mesh.shape["col"])
    return jax.shard_map(
        body,
        mesh=mesh,
        in_specs=(
            P("row", "col"),
            P("row", None),
            P("row", None),
            P(),
            P(),
            P("col"),
            P(),
            P("row", None, "col"),
            P("row", "col"),
        ),
        out_specs=(P("row", "col"), P("row", "col")),
        check_vma=False,
    )
```

```python
import functools
import math

import jax
import jax.numpy as jnp
from jax import lax
from jax.experimental import pallas as pl
from jax.experimental.pallas import tpu as pltpu
from jax.sharding import PartitionSpec as P

SUB = 32
GROUP = 8
VMEM_BYTES = 48 * 1024 * 1024
ADD_VMEM_BYTES = 48 * 1024 * 1024
FULL_VMEM_BYTES = 59 * 1024 * 1024
TILE = 1024
LIGHT = pl.CostEstimate(flops=1000, bytes_accessed=1000, transcendentals=0)


def exact_dot(left, right):
    return jnp.dot(left, right, precision=lax.Precision.HIGHEST, preferred_element_type=jnp.float32)


def split_two(value):
    high = value.astype(jnp.bfloat16)
    low = (value - high.astype(jnp.float32)).astype(jnp.bfloat16)
    return high, low


def split_three(value):
    high = value.astype(jnp.bfloat16)
    rest = value - high.astype(jnp.float32)
    middle = rest.astype(jnp.bfloat16)
    low = (rest - middle.astype(jnp.float32)).astype(jnp.bfloat16)
    return high, middle, low


def stacked_dot(left, right):
    high, middle, low = split_three(left)
    top, mid, end = split_three(right)
    return jnp.dot(
        jnp.concatenate([high, middle, high, middle, high, low], axis=1),
        jnp.concatenate([top, top, mid, mid, end, top], axis=0),
        preferred_element_type=jnp.float32,
    )


def table_lookup(selected, table):
    table_rows, lanes = table.shape
    lane = lax.broadcasted_iota(jnp.int32, (lanes, selected.shape[1]), 0)
    in_lane = jnp.where(lane == selected % lanes, 1.0, 0.0)
    candidates = exact_dot(table, in_lane)
    row = lax.broadcasted_iota(jnp.int32, candidates.shape, 0)
    return jnp.sum(jnp.where(row == selected // lanes, candidates, 0.0), axis=0, keepdims=True)


def back_substitute(s_ref, t_ref, alpha, beta, pending_ref, x_ref):
    size = x_ref.shape[0]
    rows = lax.broadcasted_iota(jnp.int32, (SUB, SUB), 0)
    cols = lax.broadcasted_iota(jnp.int32, (SUB, SUB), 1)
    groups = SUB // GROUP
    for first in range(size - SUB, -1, -SUB):
        s_small = s_ref[first : first + SUB, first : first + SUB]
        t_small = t_ref[first : first + SUB, first : first + SUB]
        s_diag = jnp.sum(jnp.where(rows == cols, s_small, 0.0), axis=1, keepdims=True)
        t_diag = jnp.sum(jnp.where(rows == cols, t_small, 0.0), axis=1, keepdims=True)
        inverse = 1.0 / (beta * s_diag - alpha * t_diag)
        s_strict = jnp.where(rows < cols, s_small, 0.0)
        t_strict = jnp.where(rows < cols, t_small, 0.0)
        pending = [
            pending_ref[first + g * GROUP : first + (g + 1) * GROUP, :] for g in range(groups)
        ]
        for column in range(SUB - 1, -1, -1):
            own, row = divmod(column, GROUP)
            right = pending[own][row : row + 1, :]
            reciprocal = inverse[column : column + 1, :]
            x_ref[first + column : first + column + 1, :] = right * reciprocal
            scaled_beta = beta * reciprocal
            scaled_alpha = alpha * reciprocal
            for g in range(own + 1):
                span = slice(g * GROUP, (g + 1) * GROUP)
                factor = (
                    s_strict[span, column : column + 1] * scaled_beta
                    - t_strict[span, column : column + 1] * scaled_alpha
                )
                pending[g] = pending[g] - factor * right
        if first:
            block = x_ref[first : first + SUB, :]
            columns = slice(first, first + SUB)
            pending_ref[:first, :] = pending_ref[:first, :] - stacked_dot(
                jnp.concatenate([s_ref[:first, columns], t_ref[:first, columns]], axis=1),
                jnp.concatenate([beta * block, -alpha * block], axis=0),
            )


def put_together(core, side, piece_refs, whole_ref):
    quarter = whole_ref.shape[0] // 4
    places = [(core, side), (core, 1 - side), (1 - core, side), (1 - core, 1 - side)]
    for ref, (half, part) in zip(piece_refs, places):
        start = (2 * half + part) * quarter
        whole_ref[pl.ds(pl.multiple_of(start, quarter), quarter), :] = ref[...]


def hand_out(core, x_ref, kept_ref, given_ref):
    half = kept_ref.shape[0]
    kept_ref[...] = x_ref[pl.ds(pl.multiple_of(core * half, half), half), :]
    given_ref[...] = x_ref[pl.ds(pl.multiple_of((1 - core) * half, half), half), :]


def lower_kernel(
    slots, me, s_ref, t_ref, r_ref, values_a, values_b, selected, kept_ref, given_ref, *refs
):
    alpha_ref, beta_ref, pending_ref, x_ref = refs
    alpha = table_lookup(selected[...], values_a[...])
    beta = table_lookup(selected[...], values_b[...])
    alpha_ref[...] = alpha
    beta_ref[...] = beta
    pending_ref[...] = r_ref[...]
    back_substitute(s_ref, t_ref, alpha, beta, pending_ref, x_ref)
    hand_out(me[0] & 1, x_ref, kept_ref, given_ref)


def upper_kernel(slots, me, s_ref, t_ref, r_ref, alpha_ref, beta_ref, *refs):
    piece_refs, (kept_ref, given_ref, lower_ref, pending_ref, x_ref) = refs[:4], refs[4:]
    block = x_ref.shape[0]
    alpha, beta = alpha_ref[...], beta_ref[...]
    put_together(me[0] & 1, (me[0] >> 1) & 1, piece_refs, lower_ref)
    lower = lower_ref[...]
    pending_ref[...] = r_ref[...] - (
        exact_dot(s_ref[:, block:], beta * lower) - exact_dot(t_ref[:, block:], alpha * lower)
    )
    back_substitute(s_ref, t_ref, alpha, beta, pending_ref, x_ref)
    hand_out(me[0] & 1, x_ref, kept_ref, given_ref)


def solve_lower(slots, me, pencil_s, pencil_t, sides, value_alpha, value_beta, selected):
    block, eigs = pencil_s.shape[1] // 2, sides.shape[1]
    count, last = sides.shape[0] // block, slots.shape[0] - 1
    lanes = 128 if value_alpha.shape[0] % 128 == 0 else value_alpha.shape[0]
    table_shape = (value_alpha.shape[0] // lanes, lanes)
    corner = pl.BlockSpec((block, block), lambda i, slots, me: (lax.rem(slots[last], count), 1))
    whole = pl.BlockSpec((block, eigs), lambda i, slots, me: (lax.rem(slots[last], count), 0))
    line = pl.BlockSpec((1, eigs), lambda i, slots, me: (0, 0))
    half = pl.BlockSpec((block // 2, eigs), lambda i, slots, me: (0, 0))
    table = pl.BlockSpec(table_shape, lambda i, slots, me: (0, 0))
    return pl.pallas_call(
        lower_kernel,
        out_shape=(
            *[jax.ShapeDtypeStruct((block // 2, eigs), jnp.float32)] * 2,
            jax.ShapeDtypeStruct((1, eigs), jnp.float32),
            jax.ShapeDtypeStruct((1, eigs), jnp.float32),
        ),
        grid_spec=pltpu.PrefetchScalarGridSpec(
            num_scalar_prefetch=2,
            grid=(1,),
            in_specs=[corner, corner, whole, table, table, line],
            out_specs=(*[half] * 2, line, line),
            scratch_shapes=[pltpu.VMEM((block, eigs), jnp.float32)] * 2,
        ),
        compiler_params=pltpu.CompilerParams(vmem_limit_bytes=FULL_VMEM_BYTES),
        cost_estimate=LIGHT,
        name="solve_lower",
    )(
        slots,
        me,
        pencil_s,
        pencil_t,
        sides,
        value_alpha.reshape(table_shape),
        value_beta.reshape(table_shape),
        selected[None, :],
    )


def solve_upper(slots, me, pencil_s, pencil_t, sides, alpha, beta, pieces):
    block, eigs = pencil_s.shape[1] // 2, sides.shape[1]
    count, index = sides.shape[0] // block, slots.shape[0] - 2
    band = pl.BlockSpec((block, 2 * block), lambda i, slots, me: (lax.rem(slots[index], count), 0))
    whole = pl.BlockSpec((block, eigs), lambda i, slots, me: (lax.rem(slots[index], count), 0))
    line = pl.BlockSpec((1, eigs), lambda i, slots, me: (0, 0))
    fixed = [pl.BlockSpec(piece.shape, lambda i, slots, me: (0, 0)) for piece in pieces]
    return pl.pallas_call(
        upper_kernel,
        out_shape=(
            *[jax.ShapeDtypeStruct((block // 2, eigs), jnp.float32)] * 2,
            jax.ShapeDtypeStruct((block, eigs), jnp.float32),
        ),
        grid_spec=pltpu.PrefetchScalarGridSpec(
            num_scalar_prefetch=2,
            grid=(1,),
            in_specs=[band, band, whole, line, line, *fixed],
            out_specs=(
                *[pl.BlockSpec((block // 2, eigs), lambda i, slots, me: (0, 0))] * 2,
                pl.BlockSpec((block, eigs), lambda i, slots, me: (0, 0)),
            ),
            scratch_shapes=[pltpu.VMEM((block, eigs), jnp.float32)] * 2,
        ),
        compiler_params=pltpu.CompilerParams(vmem_limit_bytes=FULL_VMEM_BYTES),
        cost_estimate=LIGHT,
        name="solve_upper",
    )(slots, me, pencil_s, pencil_t, sides, alpha, beta, *pieces)


def near_dot(left, right_terms):
    high, low = split_two(left)
    return jnp.dot(
        jnp.concatenate([high, low, high], axis=1), right_terms, preferred_element_type=jnp.float32
    )


def three_terms(right):
    high, low = split_two(right)
    return jnp.concatenate([high, high, low], axis=0)


def finish_kernel(slots, me, parts, r_ref, s_ref, t_ref, alpha_ref, beta_ref, lower_ref, *refs):
    piece_refs, (out_ref, terms_ref, upper_ref) = refs[:4], refs[4:]
    put_together(me[0] & 1, (me[0] >> 1) & 1, piece_refs, upper_ref)
    block = upper_ref.shape[0]
    width = block // parts.shape[0]
    for part in range(parts.shape[0]):
        rows = pl.ds(pl.multiple_of(parts[part] * width, width), width)
        for half, source in enumerate((upper_ref, lower_ref)):
            target = (2 * part + half) * width
            high, low = split_two(source[rows, :])
            for term, value in enumerate((high, high, low)):
                first = 2 * block * term + target
                terms_ref[first : first + width, :] = value
    count = out_ref.shape[0] // block
    base = me[0] * count
    alpha, beta = alpha_ref[...], beta_ref[...]
    upper, lower = upper_ref[...], lower_ref[...]
    x = jnp.concatenate([upper, lower], axis=0)
    update = near_dot(s_ref[...], three_terms(beta * x)) - near_dot(t_ref[...], three_terms(alpha * x))
    for slot in range(count):
        span = slice(slot * block, (slot + 1) * block)
        fresh = r_ref[span, :] - update[span, :]
        fresh = jnp.where(slots[slots.shape[0] - 2] == base + slot, upper, fresh)
        out_ref[span, :] = jnp.where(slots[slots.shape[0] - 1] == base + slot, lower, fresh)


def finish_sides(slots, me, parts, sides, pencil_s, pencil_t, alpha, beta, lower, pieces):
    block, eigs = lower.shape
    smem, vmem = pl.BlockSpec(memory_space=pltpu.SMEM), pl.BlockSpec(memory_space=pltpu.VMEM)
    return pl.pallas_call(
        finish_kernel,
        out_shape=(
            jax.ShapeDtypeStruct(sides.shape, jnp.float32),
            jax.ShapeDtypeStruct((6 * block, eigs), jnp.bfloat16),
        ),
        in_specs=[smem] * 3 + [vmem] * (6 + len(pieces)),
        out_specs=(vmem, vmem),
        scratch_shapes=[pltpu.VMEM((block, eigs), jnp.float32)],
        compiler_params=pltpu.CompilerParams(vmem_limit_bytes=VMEM_BYTES),
        cost_estimate=LIGHT,
        name="finish_sides",
    )(slots, me, parts, sides, pencil_s, pencil_t, alpha, beta, lower, *pieces)


def add_kernel(paired, vectors_ref, terms_ref, *refs):
    part_refs, (out_ref, base_ref, done) = refs[:-3], refs[-3:]
    tile = out_ref.shape[0]
    first = pl.multiple_of(pl.program_id(0) * tile, tile)

    def load(index):
        rows = pl.ds(pl.multiple_of(index * tile, tile), tile)
        return pltpu.make_async_copy(vectors_ref.at[rows], base_ref.at[rows], done.at[index])

    @pl.when(pl.program_id(0) == 0)
    def _():
        for index in range(base_ref.shape[0] // tile):
            load(index).start()

    if paired:
        pieces = [ref[pl.ds(half, tile, 2), :] for ref in part_refs for half in range(2)]
    else:
        pieces = [ref[...] for ref in part_refs]
    product = near_dot(jnp.concatenate(pieces, axis=1), terms_ref[...])
    load(pl.program_id(0)).wait()
    out_ref[...] = base_ref[pl.ds(first, tile), :] + product


def add_product(vectors, terms, parts, paired):
    rows, eigs = vectors.shape
    tile = math.gcd(TILE, rows)
    per, width = parts[0].shape[0] // rows, parts[0].shape[1]

    def stream(height, lanes):
        return pl.BlockSpec((height, lanes), lambda i: (i, 0))

    return pl.pallas_call(
        functools.partial(add_kernel, paired),
        out_shape=jax.ShapeDtypeStruct((rows, eigs), jnp.float32),
        grid=(rows // tile,),
        in_specs=[pl.BlockSpec(memory_space=pl.ANY), pl.BlockSpec(memory_space=pltpu.VMEM)]
        + [stream(per * tile, width) for _ in parts],
        out_specs=pl.BlockSpec((tile, eigs), lambda i: (i, 0)),
        scratch_shapes=[
            pltpu.VMEM((rows, eigs), jnp.float32),
            pltpu.SemaphoreType.DMA((rows // tile,)),
        ],
        compiler_params=pltpu.CompilerParams(vmem_limit_bytes=ADD_VMEM_BYTES),
        cost_estimate=LIGHT,
        name="add_product",
    )(vectors, terms, *parts)


def spread(kept, given, me, owner, axis, size):
    core, side = me & 1, (me >> 1) & 1
    if size & (size - 1) or size < 4:
        parts = [jnp.where(core == 0, kept, given), jnp.where(core == 0, given, kept)]
        block = jnp.concatenate(parts, axis=0)
        block = lax.psum(jnp.where(me == owner, block, jnp.zeros_like(block)), axis)
        quarter = block.shape[0] // 4
        places = [(core, side), (core, 1 - side), (1 - core, side), (1 - core, 1 - side)]
        return [
            lax.dynamic_slice_in_dim(block, (2 * first + second) * quarter, quarter, 0)
            for first, second in places
        ]

    def exchange(value, bit):
        return lax.ppermute(value, axis, [(i, i ^ bit) for i in range(size)])

    apart = me ^ owner
    kept = jnp.where(apart == 0, kept, exchange(given, 1))
    middle = kept.shape[0] // 2
    first, second = kept[:middle], kept[middle:]
    kept, given = jnp.where(side == 0, first, second), jnp.where(side == 0, second, first)
    kept = jnp.where(apart < 2, kept, exchange(given, 2))
    bit = 4
    while bit < size:
        kept = jnp.where(apart < bit, kept, exchange(kept, bit))
        bit *= 2
    return [kept] + [exchange(kept, bits) for bits in (2, 1, 3)]


def on_device(
    row_size,
    col_size,
    right_sides,
    pencil_s,
    pencil_t,
    value_alpha,
    value_beta,
    selected,
    block_slot,
    right_basis,
    vectors,
):
    block = pencil_s.shape[1] // 2
    slot_count = right_sides.shape[0] // block
    block_count = block_slot.shape[0]
    rows, _, width = right_basis.shape
    me_row = lax.axis_index("row")
    me_col = lax.axis_index("col")
    slot_upper = block_slot[block_count - 2]
    slot_lower = block_slot[block_count - 1]

    paired = width % 128 == 0
    own = right_basis.reshape((2 * rows, width) if paired else (rows, 2 * width))
    received = [
        lax.ppermute(own, "col", [(i, (i + step) % col_size) for i in range(col_size)])
        for step in range(1, col_size)
    ]
    me = me_row[None]
    parts = jnp.stack([lax.rem(me_col + (col_size - step), col_size) for step in range(col_size)])
    owner_lower, owner_upper = lax.div(slot_lower, slot_count), lax.div(slot_upper, slot_count)
    kept, given, alpha, beta = solve_lower(
        block_slot, me, pencil_s, pencil_t, right_sides, value_alpha, value_beta, selected
    )
    lower = spread(kept, given, me_row, owner_lower, "row", row_size)
    kept, given, lower = solve_upper(
        block_slot, me, pencil_s, pencil_t, right_sides, alpha, beta, lower
    )
    upper = spread(kept, given, me_row, owner_upper, "row", row_size)
    updated_sides, terms = finish_sides(
        block_slot, me, parts, right_sides, pencil_s, pencil_t, alpha, beta, lower, upper
    )
    updated_vectors = add_product(vectors, terms, [own, *received], paired)
    return (updated_sides, updated_vectors)


def solution(mesh):
    body = functools.partial(on_device, mesh.shape["row"], mesh.shape["col"])
    return jax.shard_map(
        body,
        mesh=mesh,
        in_specs=(
            P("row", "col"),
            P("row", None),
            P("row", None),
            P(),
            P(),
            P("col"),
            P(),
            P("row", None, "col"),
            P("row", "col"),
        ),
        out_specs=(P("row", "col"), P("row", "col")),
        check_vma=False,
    )
```
